128 devices in a mesh: grp: 4 (over y), dev: 32 (over z, x, core).
Axes of the slice: x: 4, y: 4, z: 4, core: 2. Of those that a mesh axis runs over, the one named last changes fastest.
Arguments:
- strain: bfloat16 [16384, 30720], P('grp', 'dev'), may hold values from -6 to 6
- taps: bfloat16 [64], replicated, may hold values from -0.75 to 0.75
- tiles: int32 [4160, 2], replicated, may hold values from 0 to 2047, as said below
- owner: int32 [4160], replicated, may hold values from 0 to 127, as said below
Outputs:
- correlation: float32 [8192, 8, 8, 384], P(('grp', 'dev'))
The draws below stay inside these ranges and needn't reach their ends.
Inputs may be any that keep to these rules, and one draw needn't show every extreme that they name: The two blocks of a tile lie in different groups of 128 consecutive channels, and for every owner all block entries of its tiles lie in pairwise different such groups; the busiest owners use every group. `owner`: two owners hold 1 tile, two hold 2, and so on up to two that hold 64; which owners these are is drawn at random, and the list is in random order.
All inputs are finite; a program needn't handle non-finite values.
Results may differ from the reference program's by a relative error of at most 0.0083.
Values may be sent and summed in bfloat16 or wider, within the bound.
A program may use at most 128 MiB of HBM per device.

```python
import math
import jax
import jax.numpy as jnp
import numpy as np
from jax import lax

NT = 6144
NF = 1024
F0 = 32
NLAG = 384
NTAP = 64
DECIM = 5
BLK = 8
CH_DEV = 128
CHANNELS = 16384
RAW = 30720
NB = 2048
TCAP = 64
NTILES = 4160
SLOTS = 8192
DEVICES = 128


def tile_plan(key):
    order_key, pair_key, local_key, shuffle_key = jax.random.split(key, 4)
    counts = np.arange(DEVICES) // 2 + 1
    rank_of = np.repeat(np.arange(DEVICES), counts)
    seat_of = np.concatenate([np.arange(number) for number in counts])
    order = jax.random.permutation(order_key, DEVICES)
    device_orders = jax.vmap(lambda sub_key: jax.random.permutation(sub_key, DEVICES))(jax.random.split(pair_key, DEVICES))
    per_dev = CH_DEV // BLK
    src_dev = device_orders[rank_of, 2 * seat_of]
    dst_dev = device_orders[rank_of, 2 * seat_of + 1]
    local_ids = jax.random.randint(local_key, (NTILES, 2), 0, per_dev)
    pairs = jnp.stack([src_dev * per_dev + local_ids[:, 0], dst_dev * per_dev + local_ids[:, 1]], axis=1)
    owners = order[rank_of]
    shuffle = jax.random.permutation(shuffle_key, NTILES)
    return (pairs[shuffle].astype(jnp.int32), owners[shuffle].astype(jnp.int32))


def draw_tiles(key, part):
    pairs, owners = tile_plan(key)
    return pairs


def draw_owner(key, part):
    pairs, owners = tile_plan(key)
    return owners


def level_of(stream_key, dims, pieces, least, high):
    def one(dim, shards_of):
        draws = jax.random.uniform(jax.random.fold_in(jax.random.fold_in(stream_key, 6), dim), (shards_of,), jnp.float32, least / len(pieces), high / len(pieces))
        return jnp.repeat(jnp.exp(draws), dims[dim] // shards_of).reshape((-1,) + (1,) * (len(dims) - dim - 1))

    factor_of = one(*pieces[0])
    for cut in pieces[1:]:
        factor_of = factor_of * one(*cut)
    return factor_of


def scatter_about(own_key, extent, deviation, limit, shards=(), kind=jnp.bfloat16):
    values = jax.random.normal(own_key, extent, jnp.float32) * deviation
    if len(shards) > 0:
        values = level_of(own_key, extent, shards, -0.22, 0.18) * values
    return jnp.clip(values, min=-limit, max=limit).astype(kind)


def setup_inputs(seed: int = 0) -> dict:
    arg_keys = jax.random.split(jax.random.key(seed), 5)
    strain = scatter_about(arg_keys[0], (CHANNELS, RAW), 1.0, 6.0, ((0, 4), (1, 32)))
    taps = scatter_about(arg_keys[1], (NTAP,), 0.125, 0.75)
    tiles = draw_tiles(jax.random.fold_in(arg_keys[4], 71), 0)
    owner = draw_owner(jax.random.fold_in(arg_keys[4], 71), 0)
    return dict(strain=strain, taps=taps, tiles=tiles, owner=owner)


def band_matrix(filter_taps, outputs):
    rows = DECIM * outputs + 64
    row_ids = jnp.arange(rows, dtype=jnp.int32)[:, None]
    col_ids = jnp.arange(outputs, dtype=jnp.int32)[None, :]
    tap_ids = DECIM * col_ids + (NTAP - 1) - row_ids
    match = (tap_ids[:, :, None] == jnp.arange(NTAP, dtype=jnp.int32)[None, None, :]).astype(jnp.float32)
    band = lax.optimization_barrier(jnp.sum(match * filter_taps.astype(jnp.float32)[None, None, :], axis=2))
    return band.astype(jnp.bfloat16)

def decimate(front_rows, filter_taps, count):
    outputs = math.gcd(count, 64)
    blocks = count // outputs
    stride = DECIM * outputs
    total = (blocks + 1) * stride
    padded = jnp.pad(front_rows, ((0, 0), (0, total - front_rows.shape[1])))
    channels = padded.shape[0]
    head = padded[:, :blocks * stride].reshape(channels, blocks, stride)
    tail = padded[:, stride:].reshape(channels, blocks, stride)[:, :, :64]
    windows = jnp.concatenate([head, tail], axis=2)
    band = band_matrix(filter_taps, outputs)
    filtered = jnp.einsum('cbr,rj->cbj', windows, band, preferred_element_type=jnp.float32)
    return filtered.reshape(channels, count)

def forward_table(count):
    sample_ids = jnp.arange(count, dtype=jnp.int32)
    bin_ids = F0 + jnp.arange(NF, dtype=jnp.int32)
    phase = sample_ids[:, None] * bin_ids[None, :] % NT
    angle = 2.0 * math.pi / NT * phase.astype(jnp.float32)
    return jnp.concatenate([jnp.cos(angle), -jnp.sin(angle)], axis=1).astype(jnp.bfloat16)

def transform(decimated):
    block_len = NT // 8
    base_table = forward_table(block_len)
    bin_ids = F0 + jnp.arange(NF, dtype=jnp.int32)
    spectrum = jnp.zeros((decimated.shape[0], 2 * NF), jnp.float32)
    for part_index in range(8):
        begin_at = part_index * block_len
        part = jnp.dot(decimated[:, begin_at:begin_at + block_len], base_table, preferred_element_type=jnp.float32)
        phase = begin_at * bin_ids % NT
        angle = 2.0 * math.pi / NT * phase.astype(jnp.float32)
        cosine = jnp.cos(angle)[None, :]
        sine = jnp.sin(angle)[None, :]
        real_part = part[:, :NF]
        imag_part = part[:, NF:]
        turned = jnp.concatenate([real_part * cosine + imag_part * sine, imag_part * cosine - real_part * sine], axis=1)
        spectrum = spectrum + turned
    return spectrum

def lag_table():
    bin_ids = F0 + jnp.arange(NF, dtype=jnp.int32)
    lag_ids = (jnp.arange(NLAG, dtype=jnp.int32) - NLAG // 2) % NT
    phase = bin_ids[:, None] * lag_ids[None, :] % NT
    angle = 2.0 * math.pi / NT * phase.astype(jnp.float32)
    factor = 1.0 / math.sqrt(NF)
    return jnp.concatenate([jnp.cos(angle) * factor, -jnp.sin(angle) * factor], axis=0).astype(jnp.bfloat16)

def whiten(spectrum):
    real_part = spectrum[:, :NF]
    imag_part = spectrum[:, NF:]
    power = real_part * real_part + imag_part * imag_part
    level = lax.optimization_barrier(jnp.mean(power, axis=1, keepdims=True))
    scale = lax.rsqrt(power + level + 1e-06)
    return jnp.concatenate([real_part * scale, imag_part * scale], axis=1).astype(jnp.bfloat16)

def tile_correlation(src_group, dst_group, lag_rows):
    count = src_group.shape[0]
    src_real = src_group[:, :, None, :NF].astype(jnp.float32)
    src_imag = src_group[:, :, None, NF:].astype(jnp.float32)
    dst_real = dst_group[:, None, :, :NF].astype(jnp.float32)
    dst_imag = dst_group[:, None, :, NF:].astype(jnp.float32)
    cross_real = src_real * dst_real + src_imag * dst_imag
    cross_imag = src_imag * dst_real - src_real * dst_imag
    cross = jnp.concatenate([cross_real, cross_imag], axis=3).astype(jnp.bfloat16)
    cross = cross.reshape(count * BLK * BLK, 2 * NF)
    lagged = jnp.dot(cross, lag_rows, preferred_element_type=jnp.float32)
    return lagged.reshape(count, BLK, BLK, NLAG)

def reference(strain, taps, tiles, owner):

    def spectra_of(channel_rows):
        extended = jnp.pad(channel_rows, ((0, 0), (NTAP - 1, 0)))
        decimated = decimate(extended, taps, NT).astype(jnp.bfloat16)
        return whiten(transform(decimated))
    spectra = lax.map(spectra_of, strain.reshape(DEVICES, CH_DEV, RAW))
    blocks = spectra.reshape(NB, BLK, 2 * NF)
    lag_rows = lag_table()
    group_size = 8
    sources = blocks[tiles[:, 0]].reshape(NTILES // group_size, group_size, BLK, 2 * NF)
    targets = blocks[tiles[:, 1]].reshape(NTILES // group_size, group_size, BLK, 2 * NF)
    lagged = lax.map(lambda pair: tile_correlation(pair[0], pair[1], lag_rows), (sources, targets))
    lagged = lagged.reshape(NTILES, BLK, BLK, NLAG)
    owner_hot = (owner[:, None] == jnp.arange(DEVICES, dtype=jnp.int32)[None, :]).astype(jnp.int32)
    tile_rank = lax.optimization_barrier(jnp.sum((jnp.cumsum(owner_hot, axis=0) - owner_hot) * owner_hot, axis=1)).astype(jnp.int32)
    position = (owner * TCAP + tile_rank).astype(jnp.int32)
    result = jnp.zeros((SLOTS, BLK, BLK, NLAG), jnp.float32)
    return result.at[position].set(lagged)
```

```python
import functools
import math

import jax
import jax.numpy as jnp
import ml_dtypes
import numpy as np
from jax import lax
from jax.experimental import pallas as pl
from jax.experimental.pallas import tpu as pltpu
from jax.sharding import PartitionSpec as P

NT = 6144
NF = 1024
F0 = 32
NLAG = 384
NTAP = 64
DECIM = 5
BLK = 8
MEMBERS = 32
GROUPS = 4
DEVICES = 128
COLS = NT // MEMBERS
EXT = 208
PARTS = 8
CH = 128
SLOTS = 64
PIECE = 128
PIECES = NF // PIECE
CUTS = (0, 4, 6, 8)
COUNTS = (4, 2, 2)
TILES = 4
MESH = pl.DeviceIdType.MESH
F32 = jnp.float32
BF16 = jnp.bfloat16


def trig(phase, factor=1.0):
    angle = np.float32(2.0 * math.pi / NT) * phase.astype(np.float32)
    angle = angle.astype(np.float64)
    return np.cos(angle) * factor, -np.sin(angle) * factor


def base_table():
    rows = (np.arange(4)[:, None] * COLS + np.arange(EXT)[None, :]).reshape(-1)
    phase = rows[:, None] * (F0 + np.arange(NF))[None, :] % NT
    real, imag = trig(phase)
    return np.concatenate([real, imag], axis=1).astype(ml_dtypes.bfloat16)


def turns(part):
    eighth = part * lax.broadcasted_iota(jnp.int32, (1, NF), 1) % 8
    half = math.sqrt(0.5)

    def wave(eighth):
        size = jnp.where(eighth % 4 == 0, 1.0, jnp.where(eighth % 4 == 2, 0.0, half))
        return jnp.where((eighth >= 3) & (eighth <= 5), -size, size)

    return wave(eighth), wave((eighth + 6) % 8)


def lag_table():
    lags = (np.arange(NLAG) - NLAG // 2) % NT
    phase = (F0 + np.arange(NF))[:, None] * lags[None, :] % NT
    real, imag = trig(phase, 1.0 / math.sqrt(NF))
    return np.concatenate([real, imag], axis=0).astype(ml_dtypes.bfloat16)


def nt_dot(a, b):
    return lax.dot_general(a, b, (((1,), (1,)), ((), ())), preferred_element_type=F32)


def stack_rows(pieces, rows, fill):
    width = sum(piece.shape[1] for piece in pieces)
    extra = jnp.full((1, rows * 128 - width), fill, jnp.int32)
    line = jnp.concatenate([*pieces, extra], axis=1)
    return jnp.concatenate(
        [line[:, index * 128 : (index + 1) * 128] for index in range(rows)], axis=0
    )


def make_band(member, taps):
    tap = lax.broadcasted_iota(jnp.int32, (NTAP, 1024), 0)
    lane = lax.broadcasted_iota(jnp.int32, (NTAP, 1024), 1)
    place = (lane == (1024 - tap) % 1024).astype(F32).astype(BF16)
    taps = jnp.broadcast_to(taps.astype(F32), (8, NTAP)).astype(BF16)
    line = jnp.dot(taps, place, preferred_element_type=F32)
    first_rows = pltpu.roll(line, 0, 1, stride=DECIM, stride_axis=0)
    band = jnp.concatenate(
        [pltpu.roll(first_rows, 8 * DECIM * index, 1) for index in range(EXT // 8)], axis=0
    )
    row = lax.broadcasted_iota(jnp.int32, (EXT, 1024), 0)
    limit = jnp.where(member == MEMBERS - 1, COLS, 205)
    return jnp.where(row < limit, band, 0.0)[:, :960].astype(BF16)


def coordinates(device):
    return device // 8 % 4, device // 2 % 4, device // 32, device % 2


def line_and_place(device, axis):
    z, x, y, c = coordinates(device)
    if axis == 0:
        return y * 8 + x * 2 + c, z
    if axis == 1:
        return y * 8 + z * 2 + c, x
    return z * 8 + x * 2 + c, y


def device_of(line, place, axis):
    first, second, c = line // 8, line // 2 % 4, line % 2
    if axis == 0:
        return first * 32 + place * 8 + second * 2 + c
    if axis == 1:
        return first * 32 + second * 8 + place * 2 + c
    return place * 32 + line


def make_plan(me, src, dst, own, plan_ref):
    rows = src.shape[0]
    mine = own == me
    lane_a = lax.broadcasted_iota(jnp.int32, (128, 128), 0)
    lane = lax.broadcasted_iota(jnp.int32, (rows, 128), 1)
    row = lax.broadcasted_iota(jnp.int32, (rows, 128), 0)
    flags = jnp.where(mine, 1, 0)
    within = flags
    for shift in (1, 2, 4, 8, 16, 32, 64):
        within = within + jnp.where(lane >= shift, pltpu.roll(within, shift, 1), 0)
    totals = jnp.broadcast_to(jnp.sum(flags, axis=1, keepdims=True), (rows, 128))
    before = totals
    for shift in (1, 2, 4, 8, 16, 32):
        before = before + jnp.where(row >= shift, pltpu.roll(before, shift, 0), 0)
    slot = jnp.where(mine, within - flags + before - totals, -1)
    src_dev, dst_dev = src // 16, dst // 16

    first = jnp.zeros((SLOTS, 128), jnp.int32)
    second = jnp.zeros((SLOTS, 128), jnp.int32)
    for index in range(rows):
        hit = slot[index : index + 1, :] == lane_a[:SLOTS]
        first = first + jnp.where(hit, src_dev[index : index + 1, :], 0)
        second = second + jnp.where(hit, dst_dev[index : index + 1, :], 0)
    ends = jnp.sum(jnp.concatenate([first, second], axis=0).T, axis=0, keepdims=True)
    lines = []
    for axis in range(3):
        line, place = line_and_place(ends, axis)
        lines.append(line * 4 + place)
    count = jnp.sum(flags, axis=(0, 1), keepdims=True)
    lines.append(jnp.broadcast_to(count, (1, 128)))
    plan_ref[12:16, :] = jnp.concatenate(lines, axis=0)

    z, x, y, _ = coordinates(me)

    def wanted(entry, _):
        axis, place = entry // 4, entry % 4
        source = jnp.where(
            axis == 0, me + (place - z) * 8, jnp.where(axis == 1, me + (place - x) * 2, me + (place - y) * 32)
        )
        local = jnp.where(src_dev == source, src % 16, 0) + jnp.where(dst_dev == source, dst % 16, 0)
        blocks = jnp.zeros((128, 128), jnp.int32)
        for index in range(rows):
            hit = own[index : index + 1, :] == lane_a
            blocks = blocks + jnp.where(hit, local[index : index + 1, :], 0)
        plan_ref[pl.ds(entry, 1), :] = jnp.sum(blocks.T, axis=0, keepdims=True)
        return 0

    lax.fori_loop(0, 12, wanted, 0)


def cross_spectra(into, plan, cross, slot, tile, axes):
    width = len(axes) * PIECE
    for index, axis in enumerate(axes):
        a = into[index, plan[12 + axis, slot]].astype(F32)
        b = into[index, plan[12 + axis, SLOTS + slot]].astype(F32)
        ar, ai, br, bi = a[:BLK], a[BLK:], b[:BLK], b[BLK:]
        left = index * PIECE
        for pair in range(BLK // 2):
            reals, imags = [], []
            for i in (2 * pair, 2 * pair + 1):
                xr, xi = ar[i : i + 1, :], ai[i : i + 1, :]
                reals.append(xr * br + xi * bi)
                imags.append(xi * br - xr * bi)
            at = tile * 64 + pair * 16
            cross[at : at + 16, left : left + PIECE] = jnp.concatenate(reals, axis=0).astype(BF16)
            cross[at : at + 16, width + left : width + left + PIECE] = jnp.concatenate(
                imags, axis=0
            ).astype(BF16)


def axes_of(part):
    return [piece % 3 for piece in range(CUTS[part], CUTS[part + 1])]


def exchange_kernel(
    strain_ref, taps_hbm, tiles_hbm, owner_hbm, base_ref, lag0_ref, lag1_ref,
    late_ref, partial_ref, plan_out_ref,
    raw, taps_ref, tiles_ref, owner_ref, base, lag0, lag1, band, plan_vector, plan, send, recv, acc,
    gathered0, gathered1, gathered2, gathered3, gathered4, gathered5, gathered6, gathered7,
    out0, out1, out2, in0, in1, cross0, cross1, first_sums, partial,
    raw_sem, small_sem, base_sem, lag_sem, plan_sem, plan_out_sem, send_sem, recv_sem,
    line_sem, gather_sem, out_sem, in_sem, own_sem, partial_sem, plane_sem,
):
    grp, dev = lax.axis_index("grp"), lax.axis_index("dev")
    me = grp * MEMBERS + dev
    chip, core = dev // 2, dev % 2
    zc, xc = chip // 4, chip % 4

    def turned(offset):
        return jnp.where(core == 0, offset, (4 - offset) % 4)

    def at(z, x, c):
        return z % 4 * 8 + x % 4 * 2 + c

    def chip_at(offset):
        return (zc + turned(offset // 4)) % 4 * 4 + (xc + turned(offset % 4)) % 4

    def raw_copy(offset):
        to_chip = chip_at(offset)
        return pltpu.make_async_copy(
            strain_ref.at[:, pl.ds(pl.multiple_of(to_chip * 256, 256), 256)],
            raw.at[to_chip], raw_sem.at[to_chip],
        )

    def fetch(step, _):
        raw_copy(step * 7 % 16).start()
        return 0

    small = ((taps_hbm, taps_ref), (tiles_hbm, tiles_ref), (owner_hbm, owner_ref))
    small_copies = [
        pltpu.make_async_copy(source, into, small_sem.at[index])
        for index, (source, into) in enumerate(small)
    ]
    for copy in small_copies:
        copy.start()
    lax.fori_loop(0, 16, fetch, 0)
    base_copy = pltpu.make_async_copy(base_ref, base, base_sem)
    base_copy.start()
    lag_copies = [
        pltpu.make_async_copy(lag0_ref, lag0, lag_sem.at[0]),
        pltpu.make_async_copy(lag1_ref, lag1, lag_sem.at[1]),
    ]
    for copy in lag_copies:
        copy.start()

    barrier = pltpu.get_barrier_semaphore()

    def greet(step, _):
        pl.semaphore_signal(
            barrier, inc=1, device_id=(grp, (dev + step) % MEMBERS), device_id_type=MESH
        )
        return 0

    lax.fori_loop(1, MEMBERS, greet, 0)
    for step in range(1, GROUPS):
        pl.semaphore_signal(
            barrier, inc=1, device_id=((grp + step) % GROUPS, dev), device_id_type=MESH
        )
    small_copies[0].wait()
    band[...] = make_band(dev, taps_ref[...])
    pl.semaphore_wait(barrier, MEMBERS - 1 + GROUPS - 1)

    def samples_to(to):
        return pltpu.make_async_remote_copy(
            src_ref=send.at[to], dst_ref=recv.at[dev], send_sem=send_sem.at[to],
            recv_sem=recv_sem.at[dev], device_id=(grp, to), device_id_type=MESH,
        )

    def decimate(pair, _):
        results = []
        for index in range(2):
            offset = (pair * 2 + index) * 7 % 16
            raw_copy(offset).wait()
            to_chip = chip_at(offset)
            result = jnp.dot(band[...], raw[to_chip], preferred_element_type=F32)
            results.append((to_chip, result.astype(BF16)))
        for to_chip, result in results:
            for half in range(2):
                to = to_chip * 2 + half
                send[to] = result[:, half * CH : (half + 1) * CH]

                @pl.when(to != dev)
                def _():
                    samples_to(to).start()

        return 0

    lax.fori_loop(0, 8, decimate, 0)
    recv[dev] = send[dev]
    for step in range(1, GROUPS):
        pl.semaphore_signal(
            plane_sem, inc=1, device_id=((grp + step) % GROUPS, dev), device_id_type=MESH
        )
    for copy in small_copies[1:]:
        copy.wait()
    tile_rows = [stack_rows([tiles_ref[side : side + 1, :]], 40, 0) for side in range(2)]
    owner_rows = stack_rows([owner_ref[...].reshape(1, -1)], 40, -1)
    make_plan(me, *tile_rows, owner_rows, plan_vector)
    plan_copy = pltpu.make_async_copy(plan_vector, plan, plan_sem)
    plan_copy.start()
    plan_out = pltpu.make_async_copy(plan_vector, plan_out_ref, plan_out_sem)
    plan_out.start()
    base_copy.wait()
    acc[...] = jnp.zeros_like(acc)

    def transform(step, _):
        offset = step * 7 % 16
        from_chip = (zc - offset // 4 + 4) % 4 * 4 + (xc - offset % 4 + 4) % 4
        for half in range(2):
            source = from_chip * 2 + half

            @pl.when(source != dev)
            def _():
                pltpu.make_async_remote_copy(
                    src_ref=send.at[source], dst_ref=recv.at[source],
                    send_sem=send_sem.at[source], recv_sem=recv_sem.at[source],
                    device_id=(grp, source), device_id_type=MESH,
                ).wait_recv()

        samples = recv[pl.ds(from_chip * 2, 2)].reshape(2 * EXT, CH)
        part = from_chip // 2
        cosine, sine = turns(part)
        table = base[pl.ds(pl.multiple_of(from_chip % 2 * (2 * EXT), 2 * EXT), 2 * EXT), :]
        result = lax.dot_general(
            samples, table, (((0,), (0,)), ((), ())), preferred_element_type=F32
        )
        real, imag = result[:, :NF], result[:, NF:]
        acc[:, :NF] += real * cosine + imag * sine
        acc[:, NF:] += imag * cosine - real * sine
        return 0

    lax.fori_loop(0, 16, transform, 0)

    real, imag = acc[:, :NF], acc[:, NF:]
    power = real * real + imag * imag
    level = jnp.mean(power, axis=1, keepdims=True)
    scale = lax.rsqrt(power + level + 1e-06)
    whitened = jnp.concatenate(
        [(real * scale).reshape(16, BLK, NF), (imag * scale).reshape(16, BLK, NF)], axis=1
    ).astype(BF16)
    outs, ins = (out0, out1, out2), (in0, in1, late_ref)
    gathered = (gathered0, gathered1, gathered2, gathered3)
    gathered = gathered + (gathered4, gathered5, gathered6, gathered7)
    pl.semaphore_wait(plane_sem, GROUPS - 1)
    for piece in range(PIECES):
        line, place = line_and_place(me, piece % 3)
        gathered[piece][place] = whitened[:, :, piece * PIECE : (piece + 1) * PIECE]
        for step in (1, 3, 2):
            to = device_of(line, (place + step) % 4, piece % 3)
            pltpu.make_async_remote_copy(
                src_ref=gathered[piece].at[place], dst_ref=gathered[piece].at[place],
                send_sem=line_sem.at[piece], recv_sem=gather_sem.at[piece],
                device_id=(to // MEMBERS, to % MEMBERS), device_id_type=MESH,
            ).start()

    def select(piece, to, out):
        axis = piece % 3
        for place in range(4):
            out[place] = gathered[piece][place, plan[4 * axis + place, to]]

    def emit(piece, part):
        axis, index = piece % 3, piece - CUTS[part]
        line, place = line_and_place(me, axis)
        first, second = line // 8, line // 2 % 4

        def one(step, _):
            offset = step * 11 % 32
            to_line = (first + turned(offset // 8)) % 4 * 8 + (second + turned(offset // 2 % 4)) % 4 * 2
            to = device_of(to_line + (core + offset) % 2, place, axis)
            select(piece, to, outs[part].at[index, step])
            pltpu.make_async_remote_copy(
                src_ref=outs[part].at[index, step], dst_ref=ins[part].at[index, pl.ds(line * 4, 4)],
                send_sem=out_sem.at[part], recv_sem=in_sem.at[part],
                device_id=(to // MEMBERS, to % MEMBERS), device_id_type=MESH,
            ).start()
            return 0

        lax.fori_loop(1, MEMBERS, one, 0)
        select(piece, me, outs[part].at[index, 0])
        return pltpu.make_async_copy(
            outs[part].at[index, 0], ins[part].at[index, pl.ds(line * 4, 4)], own_sem.at[piece]
        )

    plan_copy.wait()
    own_copies = []
    for part in range(3):
        for piece in range(CUTS[part], CUTS[part + 1]):
            others = gathered[piece].at[pl.ds(0, 3)]
            pltpu.make_async_copy(others, others, gather_sem.at[piece]).wait()
            own_copies.append(emit(piece, part))
            own_copies[piece].start()

    def drain(step, _):
        samples_to((dev + step) % MEMBERS).wait_send()
        return 0

    lax.fori_loop(1, MEMBERS, drain, 0)
    def await_part(part):
        for piece in range(CUTS[part], CUTS[part + 1]):
            own_copies[piece].wait()
        others = ins[part].at[:, pl.ds(0, DEVICES - 4)]
        pltpu.make_async_copy(others, others, in_sem.at[part]).wait()

    def lagged_tiles(group, into, cross, lag, part):
        for tile in range(TILES):
            cross_spectra(into, plan, cross, group * TILES + tile, tile, axes_of(part))
        lagged = jnp.dot(cross[...], lag[...], preferred_element_type=F32)
        return lagged.reshape(TILES, BLK, BLK, NLAG)

    def first_tiles(group, _):
        first_sums[pl.ds(group * TILES, TILES)] = lagged_tiles(group, in0, cross0, lag0, 0)
        return 0

    def second_tiles(group, _):
        rows = pl.ds(group * TILES, TILES)
        partial[rows] = (first_sums[rows] + lagged_tiles(group, in1, cross1, lag1, 1)).astype(BF16)
        pltpu.make_async_copy(partial.at[rows], partial_ref.at[rows], partial_sem).start()
        return 0

    for copy in lag_copies:
        copy.wait()
    await_part(0)
    lax.fori_loop(0, SLOTS // TILES, first_tiles, 0)
    await_part(1)
    lax.fori_loop(0, SLOTS // TILES, second_tiles, 0)
    pltpu.make_async_copy(partial, partial_ref, partial_sem).wait()
    plan_out.wait()
    for part in range(3):
        sent = outs[part].at[:, pl.ds(0, MEMBERS - 1)]
        pltpu.make_async_copy(sent, sent, out_sem.at[part]).wait()
    await_part(2)
    for piece in range(PIECES):
        others = gathered[piece].at[pl.ds(0, 3)]
        pltpu.make_async_copy(others, others, line_sem.at[piece]).wait()


def late_kernel(
    plan_ref, late_ref, partial_ref, lag_ref, out_ref,
    late, lag, partial, total, cross, late_sem, lag_sem, in_sem, out_sem,
):
    count = plan_ref[15, 0]
    pieces = 4
    size = DEVICES // 2
    late_copies = [
        pltpu.make_async_copy(
            late_ref.at[index // 2, pl.ds(size * (index % 2), size)],
            late.at[index // 2, pl.ds(size * (index % 2), size)],
            late_sem.at[index],
        )
        for index in range(pieces)
    ]
    lag_copy = pltpu.make_async_copy(lag_ref, lag, lag_sem)

    def rows(group):
        return pl.ds(group * TILES, TILES)

    def load(group):
        return pltpu.make_async_copy(
            partial_ref.at[rows(group)], partial.at[rows(group)], in_sem.at[group]
        )

    for copy in late_copies:
        copy.start()
    lag_copy.start()

    def fetch(group, _):
        load(group).start()
        return 0

    lax.fori_loop(0, SLOTS // TILES, fetch, 0)
    for copy in late_copies:
        copy.wait()
    lag_copy.wait()

    def one(group, _):
        load(group).wait()

        @pl.when(group * TILES < count)
        def _():
            for tile in range(TILES):
                cross_spectra(late, plan_ref, cross, group * TILES + tile, tile, axes_of(2))
            lagged = jnp.dot(cross[...], lag[...], preferred_element_type=F32)
            lagged = lagged + partial[rows(group)].astype(F32).reshape(lagged.shape)
            index = lax.broadcasted_iota(jnp.int32, lagged.shape, 0) // 64 + group * TILES
            total[rows(group)] = jnp.where(index < count, lagged, 0.0).reshape(TILES, BLK, BLK, NLAG)

        @pl.when(group * TILES >= count)
        def _():
            total[rows(group)] = jnp.zeros((TILES, BLK, BLK, NLAG), F32)

        pltpu.make_async_copy(total.at[rows(group)], out_ref.at[rows(group)], out_sem).start()
        return 0

    lax.fori_loop(0, SLOTS // TILES, one, 0)
    pltpu.make_async_copy(total, out_ref, out_sem).wait()


def per_device(strain, taps, tiles, owner):
    hbm = pl.BlockSpec(memory_space=pl.ANY)
    lag = lag_table()
    lags = [
        lag.reshape(2, PIECES, PIECE, NLAG)[:, CUTS[part] : CUTS[part + 1]].reshape(-1, NLAG)
        for part in range(3)
    ]
    groups = SLOTS // TILES
    late, partial, plan = pl.pallas_call(
        exchange_kernel,
        out_shape=(
            jax.ShapeDtypeStruct((COUNTS[2], DEVICES, 2 * BLK, PIECE), BF16),
            jax.ShapeDtypeStruct((SLOTS, BLK, BLK, NLAG), BF16),
            jax.ShapeDtypeStruct((16, 128), jnp.int32),
        ),
        in_specs=[hbm] * 7,
        out_specs=(hbm, hbm, hbm),
        scratch_shapes=[
            pltpu.VMEM((16, 960, 256), BF16),
            pltpu.VMEM((1, NTAP), BF16),
            pltpu.VMEM((2, 4160), jnp.int32),
            pltpu.VMEM((4160,), jnp.int32),
            pltpu.VMEM((4 * EXT, 2 * NF), BF16),
            pltpu.VMEM((2 * COUNTS[0] * PIECE, NLAG), BF16),
            pltpu.VMEM((2 * COUNTS[1] * PIECE, NLAG), BF16),
            pltpu.VMEM((EXT, 960), BF16),
            pltpu.VMEM((16, 128), jnp.int32),
            pltpu.SMEM((16, 128), jnp.int32),
            pltpu.VMEM((MEMBERS, EXT, CH), BF16),
            pltpu.VMEM((MEMBERS, EXT, CH), BF16),
            pltpu.VMEM((CH, 2 * NF), F32),
            *[pltpu.VMEM((4, 16, 2 * BLK, PIECE), BF16) for _ in range(PIECES)],
            *[pltpu.VMEM((count, MEMBERS, 4, 2 * BLK, PIECE), BF16) for count in COUNTS],
            *[pltpu.VMEM((count, DEVICES, 2 * BLK, PIECE), BF16) for count in COUNTS[:2]],
            *[pltpu.VMEM((TILES * 64, 2 * count * PIECE), BF16) for count in COUNTS[:2]],
            pltpu.VMEM((SLOTS, BLK, BLK, NLAG), F32),
            pltpu.VMEM((SLOTS, BLK, BLK, NLAG), BF16),
            pltpu.SemaphoreType.DMA((16,)),
            pltpu.SemaphoreType.DMA((3,)),
            pltpu.SemaphoreType.DMA,
            pltpu.SemaphoreType.DMA((2,)),
            pltpu.SemaphoreType.DMA,
            pltpu.SemaphoreType.DMA,
            pltpu.SemaphoreType.DMA((MEMBERS,)),
            pltpu.SemaphoreType.DMA((MEMBERS,)),
            pltpu.SemaphoreType.DMA((PIECES,)),
            pltpu.SemaphoreType.DMA((PIECES,)),
            pltpu.SemaphoreType.DMA((3,)),
            pltpu.SemaphoreType.DMA((3,)),
            pltpu.SemaphoreType.DMA((PIECES,)),
            pltpu.SemaphoreType.DMA,
            pltpu.SemaphoreType.REGULAR,
        ],
        compiler_params=pltpu.CompilerParams(
            collective_id=0, has_side_effects=True, vmem_limit_bytes=60 * 2**20
        ),
    )(
        strain.T, taps[None, :], tiles.T, owner, jnp.asarray(base_table()),
        jnp.asarray(lags[0]), jnp.asarray(lags[1]),
    )

    return pl.pallas_call(
        late_kernel,
        out_shape=jax.ShapeDtypeStruct((SLOTS, BLK, BLK, NLAG), F32),
        in_specs=[pl.BlockSpec(memory_space=pltpu.SMEM), hbm, hbm, hbm],
        out_specs=hbm,
        scratch_shapes=[
            pltpu.VMEM((COUNTS[2], DEVICES, 2 * BLK, PIECE), BF16),
            pltpu.VMEM((2 * COUNTS[2] * PIECE, NLAG), BF16),
            pltpu.VMEM((SLOTS, BLK, BLK, NLAG), BF16),
            pltpu.VMEM((SLOTS, BLK, BLK, NLAG), F32),
            pltpu.VMEM((TILES * 64, 2 * COUNTS[2] * PIECE), BF16),
            pltpu.SemaphoreType.DMA((4,)),
            pltpu.SemaphoreType.DMA,
            pltpu.SemaphoreType.DMA((groups,)),
            pltpu.SemaphoreType.DMA,
        ],
        compiler_params=pltpu.CompilerParams(vmem_limit_bytes=60 * 2**20),
    )(plan, late, partial, jnp.asarray(lags[2]))


def solution(mesh):
    return jax.shard_map(
        per_device,
        mesh=mesh,
        in_specs=(P("grp", "dev"), P(), P(), P()),
        out_specs=P(("grp", "dev"), None, None, None),
        check_vma=False,
    )
```

```python
import functools
import math

import jax
import jax.numpy as jnp
import ml_dtypes
import numpy as np
from jax import lax
from jax.experimental import pallas as pl
from jax.experimental.pallas import tpu as pltpu
from jax.sharding import PartitionSpec as P

NT = 6144
NF = 1024
F0 = 32
NLAG = 384
NTAP = 64
DECIM = 5
BLK = 8
MEMBERS = 32
GROUPS = 4
DEVICES = 128
COLS = NT // MEMBERS
EXT = 208
PARTS = 8
CH = 128
SLOTS = 64
PIECE = 128
PIECES = NF // PIECE
CUTS = (0, 4, 7, 8)
COUNTS = (4, 3, 1)
TILES = 4
MESH = pl.DeviceIdType.MESH
F32 = jnp.float32
BF16 = jnp.bfloat16


def trig(phase, factor=1.0):
    angle = np.float32(2.0 * math.pi / NT) * phase.astype(np.float32)
    angle = angle.astype(np.float64)
    return np.cos(angle) * factor, -np.sin(angle) * factor


def base_table():
    rows = (np.arange(4)[:, None] * COLS + np.arange(EXT)[None, :]).reshape(-1)
    phase = rows[:, None] * (F0 + np.arange(NF))[None, :] % NT
    real, imag = trig(phase)
    return np.concatenate([real, imag], axis=1).astype(ml_dtypes.bfloat16)


def turns(part):
    eighth = part * lax.broadcasted_iota(jnp.int32, (1, NF), 1) % 8
    half = math.sqrt(0.5)

    def wave(eighth):
        size = jnp.where(eighth % 4 == 0, 1.0, jnp.where(eighth % 4 == 2, 0.0, half))
        return jnp.where((eighth >= 3) & (eighth <= 5), -size, size)

    return wave(eighth), wave((eighth + 6) % 8)


def lag_table():
    lags = (np.arange(NLAG) - NLAG // 2) % NT
    phase = (F0 + np.arange(NF))[:, None] * lags[None, :] % NT
    real, imag = trig(phase, 1.0 / math.sqrt(NF))
    return np.concatenate([real, imag], axis=0).astype(ml_dtypes.bfloat16)


def nt_dot(a, b):
    return lax.dot_general(a, b, (((1,), (1,)), ((), ())), preferred_element_type=F32)


def stack_rows(pieces, rows, fill):
    width = sum(piece.shape[1] for piece in pieces)
    extra = jnp.full((1, rows * 128 - width), fill, jnp.int32)
    line = jnp.concatenate([*pieces, extra], axis=1)
    return jnp.concatenate(
        [line[:, index * 128 : (index + 1) * 128] for index in range(rows)], axis=0
    )


def make_band(member, taps):
    tap = lax.broadcasted_iota(jnp.int32, (NTAP, 1024), 0)
    lane = lax.broadcasted_iota(jnp.int32, (NTAP, 1024), 1)
    place = (lane == (1024 - tap) % 1024).astype(F32).astype(BF16)
    taps = jnp.broadcast_to(taps.astype(F32), (8, NTAP)).astype(BF16)
    line = jnp.dot(taps, place, preferred_element_type=F32)
    first_rows = pltpu.roll(line, 0, 1, stride=DECIM, stride_axis=0)
    band = jnp.concatenate(
        [pltpu.roll(first_rows, 8 * DECIM * index, 1) for index in range(EXT // 8)], axis=0
    )
    row = lax.broadcasted_iota(jnp.int32, (EXT, 1024), 0)
    limit = jnp.where(member == MEMBERS - 1, COLS, 205)
    return jnp.where(row < limit, band, 0.0)[:, :960].astype(BF16)


def coordinates(device):
    return device // 8 % 4, device // 2 % 4, device // 32, device % 2


def line_and_place(device, axis):
    z, x, y, c = coordinates(device)
    if axis == 0:
        return y * 8 + x * 2 + c, z
    if axis == 1:
        return y * 8 + z * 2 + c, x
    return z * 8 + x * 2 + c, y


def device_of(line, place, axis):
    first, second, c = line // 8, line // 2 % 4, line % 2
    if axis == 0:
        return first * 32 + place * 8 + second * 2 + c
    if axis == 1:
        return first * 32 + second * 8 + place * 2 + c
    return place * 32 + line


def make_plan(me, src, dst, own, plan_ref):
    rows = src.shape[0]
    mine = own == me
    lane_a = lax.broadcasted_iota(jnp.int32, (128, 128), 0)
    lane = lax.broadcasted_iota(jnp.int32, (rows, 128), 1)
    row = lax.broadcasted_iota(jnp.int32, (rows, 128), 0)
    flags = jnp.where(mine, 1, 0)
    within = flags
    for shift in (1, 2, 4, 8, 16, 32, 64):
        within = within + jnp.where(lane >= shift, pltpu.roll(within, shift, 1), 0)
    totals = jnp.broadcast_to(jnp.sum(flags, axis=1, keepdims=True), (rows, 128))
    before = totals
    for shift in (1, 2, 4, 8, 16, 32):
        before = before + jnp.where(row >= shift, pltpu.roll(before, shift, 0), 0)
    slot = jnp.where(mine, within - flags + before - totals, -1)
    src_dev, dst_dev = src // 16, dst // 16

    first = jnp.zeros((SLOTS, 128), jnp.int32)
    second = jnp.zeros((SLOTS, 128), jnp.int32)
    for index in range(rows):
        hit = slot[index : index + 1, :] == lane_a[:SLOTS]
        first = first + jnp.where(hit, src_dev[index : index + 1, :], 0)
        second = second + jnp.where(hit, dst_dev[index : index + 1, :], 0)
    ends = jnp.sum(jnp.concatenate([first, second], axis=0).T, axis=0, keepdims=True)
    lines = []
    for axis in range(3):
        line, place = line_and_place(ends, axis)
        lines.append(line * 4 + place)
    count = jnp.sum(flags, axis=(0, 1), keepdims=True)
    lines.append(jnp.broadcast_to(count, (1, 128)))
    plan_ref[12:16, :] = jnp.concatenate(lines, axis=0)

    z, x, y, _ = coordinates(me)

    def wanted(entry, _):
        axis, place = entry // 4, entry % 4
        source = jnp.where(
            axis == 0, me + (place - z) * 8, jnp.where(axis == 1, me + (place - x) * 2, me + (place - y) * 32)
        )
        local = jnp.where(src_dev == source, src % 16, 0) + jnp.where(dst_dev == source, dst % 16, 0)
        blocks = jnp.zeros((128, 128), jnp.int32)
        for index in range(rows):
            hit = own[index : index + 1, :] == lane_a
            blocks = blocks + jnp.where(hit, local[index : index + 1, :], 0)
        plan_ref[pl.ds(entry, 1), :] = jnp.sum(blocks.T, axis=0, keepdims=True)
        return 0

    lax.fori_loop(0, 12, wanted, 0)


def cross_spectra(into, plan, cross, slot, tile, axes):
    width = len(axes) * PIECE
    for index, axis in enumerate(axes):
        a = into[index, plan[12 + axis, slot]].astype(F32)
        b = into[index, plan[12 + axis, SLOTS + slot]].astype(F32)
        ar, ai, br, bi = a[:BLK], a[BLK:], b[:BLK], b[BLK:]
        left = index * PIECE
        for pair in range(BLK // 2):
            reals, imags = [], []
            for i in (2 * pair, 2 * pair + 1):
                xr, xi = ar[i : i + 1, :], ai[i : i + 1, :]
                reals.append(xr * br + xi * bi)
                imags.append(xi * br - xr * bi)
            at = tile * 64 + pair * 16
            cross[at : at + 16, left : left + PIECE] = jnp.concatenate(reals, axis=0).astype(BF16)
            cross[at : at + 16, width + left : width + left + PIECE] = jnp.concatenate(
                imags, axis=0
            ).astype(BF16)


def axes_of(part):
    return [piece % 3 for piece in range(CUTS[part], CUTS[part + 1])]


def exchange_kernel(
    strain_ref, taps_hbm, tiles_hbm, owner_hbm, base_ref, lag0_ref, lag1_ref,
    late_ref, partial_ref, plan_out_ref,
    raw, taps_ref, tiles_ref, owner_ref, base, lag0, lag1, band, plan_vector, plan, send, recv, acc,
    gathered0, gathered1, gathered2, gathered3, gathered4, gathered5, gathered6, gathered7,
    out0, out1, out2, in0, in1, cross0, cross1, first_sums, partial,
    raw_sem, small_sem, base_sem, lag_sem, plan_sem, plan_out_sem, send_sem, recv_sem,
    line_sem, gather_sem, out_sem, in_sem, own_sem, partial_sem, plane_sem,
):
    grp, dev = lax.axis_index("grp"), lax.axis_index("dev")
    me = grp * MEMBERS + dev
    chip, core = dev // 2, dev % 2
    zc, xc = chip // 4, chip % 4

    def turned(offset):
        return jnp.where(core == 0, offset, (4 - offset) % 4)

    def at(z, x, c):
        return z % 4 * 8 + x % 4 * 2 + c

    def chip_at(offset):
        return (zc + turned(offset // 4)) % 4 * 4 + (xc + turned(offset % 4)) % 4

    def raw_copy(offset):
        to_chip = chip_at(offset)
        return pltpu.make_async_copy(
            strain_ref.at[:, pl.ds(pl.multiple_of(to_chip * 256, 256), 256)],
            raw.at[to_chip], raw_sem.at[to_chip],
        )

    def fetch(step, _):
        raw_copy(step * 7 % 16).start()
        return 0

    small = ((taps_hbm, taps_ref), (tiles_hbm, tiles_ref), (owner_hbm, owner_ref))
    small_copies = [
        pltpu.make_async_copy(source, into, small_sem.at[index])
        for index, (source, into) in enumerate(small)
    ]
    for copy in small_copies:
        copy.start()
    lax.fori_loop(0, 16, fetch, 0)
    base_copy = pltpu.make_async_copy(base_ref, base, base_sem)
    base_copy.start()
    lag_copies = [
        pltpu.make_async_copy(lag0_ref, lag0, lag_sem.at[0]),
        pltpu.make_async_copy(lag1_ref, lag1, lag_sem.at[1]),
    ]
    for copy in lag_copies:
        copy.start()

    barrier = pltpu.get_barrier_semaphore()

    def greet(step, _):
        pl.semaphore_signal(
            barrier, inc=1, device_id=(grp, (dev + step) % MEMBERS), device_id_type=MESH
        )
        return 0

    lax.fori_loop(1, MEMBERS, greet, 0)
    for step in range(1, GROUPS):
        pl.semaphore_signal(
            barrier, inc=1, device_id=((grp + step) % GROUPS, dev), device_id_type=MESH
        )
    small_copies[0].wait()
    band[...] = make_band(dev, taps_ref[...])
    pl.semaphore_wait(barrier, MEMBERS - 1 + GROUPS - 1)

    def samples_to(to):
        return pltpu.make_async_remote_copy(
            src_ref=send.at[to], dst_ref=recv.at[dev], send_sem=send_sem.at[to],
            recv_sem=recv_sem.at[dev], device_id=(grp, to), device_id_type=MESH,
        )

    def decimate(pair, _):
        results = []
        for index in range(2):
            offset = (pair * 2 + index) * 7 % 16
            raw_copy(offset).wait()
            to_chip = chip_at(offset)
            result = jnp.dot(band[...], raw[to_chip], preferred_element_type=F32)
            results.append((to_chip, result.astype(BF16)))
        for to_chip, result in results:
            for half in range(2):
                send[to_chip * 2 + half] = result[:, half * CH : (half + 1) * CH]

            @pl.when(to_chip * 2 != dev)
            def _():
                samples_to(to_chip * 2).start()

        return 0

    lax.fori_loop(0, 8, decimate, 0)

    def to_second(step, _):
        to = chip_at(step * 7 % 16) * 2 + 1

        @pl.when(to != dev)
        def _():
            samples_to(to).start()

        return 0

    lax.fori_loop(0, 16, to_second, 0)
    recv[dev] = send[dev]
    for step in range(1, GROUPS):
        pl.semaphore_signal(
            plane_sem, inc=1, device_id=((grp + step) % GROUPS, dev), device_id_type=MESH
        )
    for copy in small_copies[1:]:
        copy.wait()
    tile_rows = [stack_rows([tiles_ref[side : side + 1, :]], 40, 0) for side in range(2)]
    owner_rows = stack_rows([owner_ref[...].reshape(1, -1)], 40, -1)
    make_plan(me, *tile_rows, owner_rows, plan_vector)
    plan_copy = pltpu.make_async_copy(plan_vector, plan, plan_sem)
    plan_copy.start()
    plan_out = pltpu.make_async_copy(plan_vector, plan_out_ref, plan_out_sem)
    plan_out.start()
    base_copy.wait()
    acc[...] = jnp.zeros_like(acc)

    def transform(step, _):
        offset = step * 7 % 16
        from_chip = (zc - offset // 4 + 4) % 4 * 4 + (xc - offset % 4 + 4) % 4
        for half in range(2):
            source = from_chip * 2 + half

            @pl.when(source != dev)
            def _():
                pltpu.make_async_remote_copy(
                    src_ref=send.at[source], dst_ref=recv.at[source],
                    send_sem=send_sem.at[source], recv_sem=recv_sem.at[source],
                    device_id=(grp, source), device_id_type=MESH,
                ).wait_recv()

        samples = recv[pl.ds(from_chip * 2, 2)].reshape(2 * EXT, CH)
        part = from_chip // 2
        cosine, sine = turns(part)
        table = base[pl.ds(pl.multiple_of(from_chip % 2 * (2 * EXT), 2 * EXT), 2 * EXT), :]
        result = lax.dot_general(
            samples, table, (((0,), (0,)), ((), ())), preferred_element_type=F32
        )
        real, imag = result[:, :NF], result[:, NF:]
        acc[:, :NF] += real * cosine + imag * sine
        acc[:, NF:] += imag * cosine - real * sine
        return 0

    lax.fori_loop(0, 16, transform, 0)

    real, imag = acc[:, :NF], acc[:, NF:]
    power = real * real + imag * imag
    level = jnp.mean(power, axis=1, keepdims=True)
    scale = lax.rsqrt(power + level + 1e-06)
    whitened = jnp.concatenate(
        [(real * scale).reshape(16, BLK, NF), (imag * scale).reshape(16, BLK, NF)], axis=1
    ).astype(BF16)
    outs, ins = (out0, out1, out2), (in0, in1, late_ref)
    gathered = (gathered0, gathered1, gathered2, gathered3)
    gathered = gathered + (gathered4, gathered5, gathered6, gathered7)
    pl.semaphore_wait(plane_sem, GROUPS - 1)
    for piece in range(PIECES):
        line, place = line_and_place(me, piece % 3)
        gathered[piece][place] = whitened[:, :, piece * PIECE : (piece + 1) * PIECE]
        for step in (1, 3, 2):
            to = device_of(line, (place + step) % 4, piece % 3)
            pltpu.make_async_remote_copy(
                src_ref=gathered[piece].at[place], dst_ref=gathered[piece].at[place],
                send_sem=line_sem.at[piece], recv_sem=gather_sem.at[piece],
                device_id=(to // MEMBERS, to % MEMBERS), device_id_type=MESH,
            ).start()

    def select(piece, to, out):
        axis = piece % 3
        for place in range(4):
            out[place] = gathered[piece][place, plan[4 * axis + place, to]]

    def emit(piece, part):
        axis, index = piece % 3, piece - CUTS[part]
        line, place = line_and_place(me, axis)
        first, second = line // 8, line // 2 % 4

        def one(step, _):
            offset = step * 11 % 32
            to_line = (first + turned(offset // 8)) % 4 * 8 + (second + turned(offset // 2 % 4)) % 4 * 2
            to = device_of(to_line + (core + offset) % 2, place, axis)
            select(piece, to, outs[part].at[index, step])
            pltpu.make_async_remote_copy(
                src_ref=outs[part].at[index, step], dst_ref=ins[part].at[index, pl.ds(line * 4, 4)],
                send_sem=out_sem.at[part], recv_sem=in_sem.at[part],
                device_id=(to // MEMBERS, to % MEMBERS), device_id_type=MESH,
            ).start()
            return 0

        lax.fori_loop(1, MEMBERS, one, 0)
        select(piece, me, outs[part].at[index, 0])
        return pltpu.make_async_copy(
            outs[part].at[index, 0], ins[part].at[index, pl.ds(line * 4, 4)], own_sem.at[piece]
        )

    plan_copy.wait()
    own_copies = []
    for part in range(3):
        for piece in range(CUTS[part], CUTS[part + 1]):
            others = gathered[piece].at[pl.ds(0, 3)]
            pltpu.make_async_copy(others, others, gather_sem.at[piece]).wait()
            own_copies.append(emit(piece, part))
            own_copies[piece].start()

    def drain(step, _):
        samples_to((dev + step) % MEMBERS).wait_send()
        return 0

    lax.fori_loop(1, MEMBERS, drain, 0)
    def await_part(part):
        for piece in range(CUTS[part], CUTS[part + 1]):
            own_copies[piece].wait()
        others = ins[part].at[:, pl.ds(0, DEVICES - 4)]
        pltpu.make_async_copy(others, others, in_sem.at[part]).wait()

    def lagged_tiles(group, into, cross, lag, part):
        for tile in range(TILES):
            cross_spectra(into, plan, cross, group * TILES + tile, tile, axes_of(part))
        lagged = jnp.dot(cross[...], lag[...], preferred_element_type=F32)
        return lagged.reshape(TILES, BLK, BLK, NLAG)

    def first_tiles(group, _):
        first_sums[pl.ds(group * TILES, TILES)] = lagged_tiles(group, in0, cross0, lag0, 0)
        return 0

    def second_tiles(group, _):
        rows = pl.ds(group * TILES, TILES)
        partial[rows] = (first_sums[rows] + lagged_tiles(group, in1, cross1, lag1, 1)).astype(BF16)
        pltpu.make_async_copy(partial.at[rows], partial_ref.at[rows], partial_sem).start()
        return 0

    for copy in lag_copies:
        copy.wait()
    await_part(0)
    lax.fori_loop(0, SLOTS // TILES, first_tiles, 0)
    await_part(1)
    lax.fori_loop(0, SLOTS // TILES, second_tiles, 0)
    pltpu.make_async_copy(partial, partial_ref, partial_sem).wait()
    plan_out.wait()
    for part in range(3):
        sent = outs[part].at[:, pl.ds(0, MEMBERS - 1)]
        pltpu.make_async_copy(sent, sent, out_sem.at[part]).wait()
    await_part(2)
    for piece in range(PIECES):
        others = gathered[piece].at[pl.ds(0, 3)]
        pltpu.make_async_copy(others, others, line_sem.at[piece]).wait()


def late_kernel(
    plan_ref, late_ref, partial_ref, lag_ref, out_ref,
    late, lag, partial, total, cross, late_sem, lag_sem, in_sem, out_sem,
):
    count = plan_ref[15, 0]
    pieces = 4
    size = DEVICES // pieces
    late_copies = [
        pltpu.make_async_copy(
            late_ref.at[:, pl.ds(size * index, size)], late.at[:, pl.ds(size * index, size)],
            late_sem.at[index],
        )
        for index in range(pieces)
    ]
    lag_copy = pltpu.make_async_copy(lag_ref, lag, lag_sem)

    def rows(group):
        return pl.ds(group * TILES, TILES)

    def load(group):
        return pltpu.make_async_copy(
            partial_ref.at[rows(group)], partial.at[rows(group)], in_sem.at[group]
        )

    for copy in late_copies:
        copy.start()
    lag_copy.start()

    def fetch(group, _):
        load(group).start()
        return 0

    lax.fori_loop(0, SLOTS // TILES, fetch, 0)
    for copy in late_copies:
        copy.wait()
    lag_copy.wait()

    def one(group, _):
        load(group).wait()

        @pl.when(group * TILES < count)
        def _():
            for tile in range(TILES):
                cross_spectra(late, plan_ref, cross, group * TILES + tile, tile, axes_of(2))
            lagged = jnp.dot(cross[...], lag[...], preferred_element_type=F32)
            lagged = lagged + partial[rows(group)].astype(F32).reshape(lagged.shape)
            index = lax.broadcasted_iota(jnp.int32, lagged.shape, 0) // 64 + group * TILES
            total[rows(group)] = jnp.where(index < count, lagged, 0.0).reshape(TILES, BLK, BLK, NLAG)

        @pl.when(group * TILES >= count)
        def _():
            total[rows(group)] = jnp.zeros((TILES, BLK, BLK, NLAG), F32)

        pltpu.make_async_copy(total.at[rows(group)], out_ref.at[rows(group)], out_sem).start()
        return 0

    lax.fori_loop(0, SLOTS // TILES, one, 0)
    pltpu.make_async_copy(total, out_ref, out_sem).wait()


def per_device(strain, taps, tiles, owner):
    hbm = pl.BlockSpec(memory_space=pl.ANY)
    lag = lag_table()
    lags = [
        lag.reshape(2, PIECES, PIECE, NLAG)[:, CUTS[part] : CUTS[part + 1]].reshape(-1, NLAG)
        for part in range(3)
    ]
    groups = SLOTS // TILES
    late, partial, plan = pl.pallas_call(
        exchange_kernel,
        out_shape=(
            jax.ShapeDtypeStruct((COUNTS[2], DEVICES, 2 * BLK, PIECE), BF16),
            jax.ShapeDtypeStruct((SLOTS, BLK, BLK, NLAG), BF16),
            jax.ShapeDtypeStruct((16, 128), jnp.int32),
        ),
        in_specs=[hbm] * 7,
        out_specs=(hbm, hbm, hbm),
        scratch_shapes=[
            pltpu.VMEM((16, 960, 256), BF16),
            pltpu.VMEM((1, NTAP), BF16),
            pltpu.VMEM((2, 4160), jnp.int32),
            pltpu.VMEM((4160,), jnp.int32),
            pltpu.VMEM((4 * EXT, 2 * NF), BF16),
            pltpu.VMEM((2 * COUNTS[0] * PIECE, NLAG), BF16),
            pltpu.VMEM((2 * COUNTS[1] * PIECE, NLAG), BF16),
            pltpu.VMEM((EXT, 960), BF16),
            pltpu.VMEM((16, 128), jnp.int32),
            pltpu.SMEM((16, 128), jnp.int32),
            pltpu.VMEM((MEMBERS, EXT, CH), BF16),
            pltpu.VMEM((MEMBERS, EXT, CH), BF16),
            pltpu.VMEM((CH, 2 * NF), F32),
            *[pltpu.VMEM((4, 16, 2 * BLK, PIECE), BF16) for _ in range(PIECES)],
            *[pltpu.VMEM((count, MEMBERS, 4, 2 * BLK, PIECE), BF16) for count in COUNTS],
            *[pltpu.VMEM((count, DEVICES, 2 * BLK, PIECE), BF16) for count in COUNTS[:2]],
            *[pltpu.VMEM((TILES * 64, 2 * count * PIECE), BF16) for count in COUNTS[:2]],
            pltpu.VMEM((SLOTS, BLK, BLK, NLAG), F32),
            pltpu.VMEM((SLOTS, BLK, BLK, NLAG), BF16),
            pltpu.SemaphoreType.DMA((16,)),
            pltpu.SemaphoreType.DMA((3,)),
            pltpu.SemaphoreType.DMA,
            pltpu.SemaphoreType.DMA((2,)),
            pltpu.SemaphoreType.DMA,
            pltpu.SemaphoreType.DMA,
            pltpu.SemaphoreType.DMA((MEMBERS,)),
            pltpu.SemaphoreType.DMA((MEMBERS,)),
            pltpu.SemaphoreType.DMA((PIECES,)),
            pltpu.SemaphoreType.DMA((PIECES,)),
            pltpu.SemaphoreType.DMA((3,)),
            pltpu.SemaphoreType.DMA((3,)),
            pltpu.SemaphoreType.DMA((PIECES,)),
            pltpu.SemaphoreType.DMA,
            pltpu.SemaphoreType.REGULAR,
        ],
        compiler_params=pltpu.CompilerParams(
            collective_id=0, has_side_effects=True, vmem_limit_bytes=60 * 2**20
        ),
    )(
        strain.T, taps[None, :], tiles.T, owner, jnp.asarray(base_table()),
        jnp.asarray(lags[0]), jnp.asarray(lags[1]),
    )

    return pl.pallas_call(
        late_kernel,
        out_shape=jax.ShapeDtypeStruct((SLOTS, BLK, BLK, NLAG), F32),
        in_specs=[pl.BlockSpec(memory_space=pltpu.SMEM), hbm, hbm, hbm],
        out_specs=hbm,
        scratch_shapes=[
            pltpu.VMEM((COUNTS[2], DEVICES, 2 * BLK, PIECE), BF16),
            pltpu.VMEM((2 * COUNTS[2] * PIECE, NLAG), BF16),
            pltpu.VMEM((SLOTS, BLK, BLK, NLAG), BF16),
            pltpu.VMEM((SLOTS, BLK, BLK, NLAG), F32),
            pltpu.VMEM((TILES * 64, 2 * COUNTS[2] * PIECE), BF16),
            pltpu.SemaphoreType.DMA((4,)),
            pltpu.SemaphoreType.DMA,
            pltpu.SemaphoreType.DMA((groups,)),
            pltpu.SemaphoreType.DMA,
        ],
        compiler_params=pltpu.CompilerParams(vmem_limit_bytes=60 * 2**20),
    )(plan, late, partial, jnp.asarray(lags[2]))


def solution(mesh):
    return jax.shard_map(
        per_device,
        mesh=mesh,
        in_specs=(P("grp", "dev"), P(), P(), P()),
        out_specs=P(("grp", "dev"), None, None, None),
        check_vma=False,
    )
```

```python
import functools
import math

import jax
import jax.numpy as jnp
import ml_dtypes
import numpy as np
from jax import lax
from jax.experimental import pallas as pl
from jax.experimental.pallas import tpu as pltpu
from jax.sharding import PartitionSpec as P

NT = 6144
NF = 1024
F0 = 32
NLAG = 384
NTAP = 64
DECIM = 5
BLK = 8
MEMBERS = 32
GROUPS = 4
DEVICES = 128
COLS = NT // MEMBERS
EXT = 208
USED = 205
RANK = 96
PARTS = 8
CH = 128
SLOTS = 64
PIECE = 128
PIECES = NF // PIECE
CUTS = (0, 4, 7, 8)
COUNTS = (4, 3, 1)
TILES = 4
MESH = pl.DeviceIdType.MESH
F32 = jnp.float32
BF16 = jnp.bfloat16


def trig(phase, factor=1.0):
    angle = np.float32(2.0 * math.pi / NT) * phase.astype(np.float32)
    angle = angle.astype(np.float64)
    return np.cos(angle) * factor, -np.sin(angle) * factor


def base_tables():
    samples = np.arange(USED)
    width = (F0 + NF) / NT
    steps = samples[1:] * (USED - samples[1:]) / 2
    diagonal = ((USED - 1) / 2 - samples) ** 2 * math.cos(2 * math.pi * width)
    _, vectors = np.linalg.eigh(np.diag(diagonal) + np.diag(steps, 1) + np.diag(steps, -1))
    basis = vectors[:, ::-1][:, :RANK].T
    half = basis[:, : USED // 2]
    basis = basis * np.sign(np.take_along_axis(half, np.abs(half).argmax(axis=1)[:, None], axis=1))

    def table(place):
        rows = place * COLS + samples
        angle = 2.0 * math.pi / NT * (rows[:, None] * (F0 + np.arange(NF))[None, :] % NT)
        return np.concatenate([np.cos(angle), -np.sin(angle)], axis=1)

    assert np.abs(basis.T @ (basis @ table(0)) - table(0)).max() < 1e-10
    rows = np.concatenate([basis @ table(place) for place in range(4)], axis=0)
    basis = np.pad(basis, ((0, 0), (0, EXT - USED)))
    high = basis.astype(ml_dtypes.bfloat16)
    low = (basis - high.astype(np.float64)).astype(ml_dtypes.bfloat16)
    return np.concatenate([high, low], axis=0), rows.astype(ml_dtypes.bfloat16)


def turns(part):
    eighth = part * lax.broadcasted_iota(jnp.int32, (1, NF), 1) % 8
    half = math.sqrt(0.5)

    def wave(eighth):
        size = jnp.where(eighth % 4 == 0, 1.0, jnp.where(eighth % 4 == 2, 0.0, half))
        return jnp.where((eighth >= 3) & (eighth <= 5), -size, size)

    return wave(eighth), wave((eighth + 6) % 8)


def lag_table():
    lags = (np.arange(NLAG) - NLAG // 2) % NT
    phase = (F0 + np.arange(NF))[:, None] * lags[None, :] % NT
    real, imag = trig(phase, 1.0 / math.sqrt(NF))
    return np.concatenate([real, imag], axis=0).astype(ml_dtypes.bfloat16)


def nt_dot(a, b):
    return lax.dot_general(a, b, (((1,), (1,)), ((), ())), preferred_element_type=F32)


def stack_rows(pieces, rows, fill):
    width = sum(piece.shape[1] for piece in pieces)
    extra = jnp.full((1, rows * 128 - width), fill, jnp.int32)
    line = jnp.concatenate([*pieces, extra], axis=1)
    return jnp.concatenate(
        [line[:, index * 128 : (index + 1) * 128] for index in range(rows)], axis=0
    )


def make_band(member, taps):
    tap = lax.broadcasted_iota(jnp.int32, (NTAP, 1024), 0)
    lane = lax.broadcasted_iota(jnp.int32, (NTAP, 1024), 1)
    place = (lane == (1024 - tap) % 1024).astype(F32).astype(BF16)
    taps = jnp.broadcast_to(taps.astype(F32), (8, NTAP)).astype(BF16)
    line = jnp.dot(taps, place, preferred_element_type=F32)
    first_rows = pltpu.roll(line, 0, 1, stride=DECIM, stride_axis=0)
    band = jnp.concatenate(
        [pltpu.roll(first_rows, 8 * DECIM * index, 1) for index in range(EXT // 8)], axis=0
    )
    row = lax.broadcasted_iota(jnp.int32, (EXT, 1024), 0)
    limit = jnp.where(member == MEMBERS - 1, COLS, USED)
    return jnp.where(row < limit, band, 0.0)[:, :960].astype(BF16)


def coordinates(device):
    return device // 8 % 4, device // 2 % 4, device // 32, device % 2


def line_and_place(device, axis):
    z, x, y, c = coordinates(device)
    if axis == 0:
        return y * 8 + x * 2 + c, z
    if axis == 1:
        return y * 8 + z * 2 + c, x
    return z * 8 + x * 2 + c, y


def device_of(line, place, axis):
    first, second, c = line // 8, line // 2 % 4, line % 2
    if axis == 0:
        return first * 32 + place * 8 + second * 2 + c
    if axis == 1:
        return first * 32 + second * 8 + place * 2 + c
    return place * 32 + line


def make_plan(me, src, dst, own, plan_ref):
    rows = src.shape[0]
    mine = own == me
    lane_a = lax.broadcasted_iota(jnp.int32, (128, 128), 0)
    lane = lax.broadcasted_iota(jnp.int32, (rows, 128), 1)
    row = lax.broadcasted_iota(jnp.int32, (rows, 128), 0)
    flags = jnp.where(mine, 1, 0)
    within = flags
    for shift in (1, 2, 4, 8, 16, 32, 64):
        within = within + jnp.where(lane >= shift, pltpu.roll(within, shift, 1), 0)
    totals = jnp.broadcast_to(jnp.sum(flags, axis=1, keepdims=True), (rows, 128))
    before = totals
    for shift in (1, 2, 4, 8, 16, 32):
        before = before + jnp.where(row >= shift, pltpu.roll(before, shift, 0), 0)
    slot = jnp.where(mine, within - flags + before - totals, -1)
    src_dev, dst_dev = src // 16, dst // 16

    first = jnp.zeros((SLOTS, 128), jnp.int32)
    second = jnp.zeros((SLOTS, 128), jnp.int32)
    for index in range(rows):
        hit = slot[index : index + 1, :] == lane_a[:SLOTS]
        first = first + jnp.where(hit, src_dev[index : index + 1, :], 0)
        second = second + jnp.where(hit, dst_dev[index : index + 1, :], 0)
    ends = jnp.sum(jnp.concatenate([first, second], axis=0).T, axis=0, keepdims=True)
    lines = []
    for axis in range(3):
        line, place = line_and_place(ends, axis)
        lines.append(line * 4 + place)
    count = jnp.sum(flags, axis=(0, 1), keepdims=True)
    lines.append(jnp.broadcast_to(count, (1, 128)))
    plan_ref[12:16, :] = jnp.concatenate(lines, axis=0)

    z, x, y, _ = coordinates(me)

    def wanted(entry, _):
        axis, place = entry // 4, entry % 4
        source = jnp.where(
            axis == 0, me + (place - z) * 8, jnp.where(axis == 1, me + (place - x) * 2, me + (place - y) * 32)
        )
        local = jnp.where(src_dev == source, src % 16, 0) + jnp.where(dst_dev == source, dst % 16, 0)
        blocks = jnp.zeros((128, 128), jnp.int32)
        for index in range(rows):
            hit = own[index : index + 1, :] == lane_a
            blocks = blocks + jnp.where(hit, local[index : index + 1, :], 0)
        plan_ref[pl.ds(entry, 1), :] = jnp.sum(blocks.T, axis=0, keepdims=True)
        return 0

    lax.fori_loop(0, 12, wanted, 0)


def cross_spectra(into, plan, cross, slot, tile, axes):
    width = len(axes) * PIECE
    for index, axis in enumerate(axes):
        a = into[index, plan[12 + axis, slot]].astype(F32)
        b = into[index, plan[12 + axis, SLOTS + slot]].astype(F32)
        ar, ai, br, bi = a[:BLK], a[BLK:], b[:BLK], b[BLK:]
        left = index * PIECE
        for pair in range(BLK // 2):
            reals, imags = [], []
            for i in (2 * pair, 2 * pair + 1):
                xr, xi = ar[i : i + 1, :], ai[i : i + 1, :]
                reals.append(xr * br + xi * bi)
                imags.append(xi * br - xr * bi)
            at = tile * 64 + pair * 16
            cross[at : at + 16, left : left + PIECE] = jnp.concatenate(reals, axis=0).astype(BF16)
            cross[at : at + 16, width + left : width + left + PIECE] = jnp.concatenate(
                imags, axis=0
            ).astype(BF16)


def axes_of(part):
    return [piece % 3 for piece in range(CUTS[part], CUTS[part + 1])]


def exchange_kernel(
    strain_ref, taps_hbm, tiles_hbm, owner_hbm, basis_hbm, base_ref, lag0_ref, lag1_ref,
    late_ref, partial_ref, plan_out_ref,
    raw, taps_ref, tiles_ref, owner_ref, basis, base, lag0, lag1, band, plan_vector, plan, send, recv, acc,
    gathered0, gathered1, gathered2, gathered3, gathered4, gathered5, gathered6, gathered7,
    out0, out1, out2, in0, in1, cross0, cross1, first_sums, partial,
    raw_sem, small_sem, base_sem, lag_sem, plan_sem, plan_out_sem, send_sem, recv_sem,
    line_sem, gather_sem, out_sem, in_sem, own_sem, partial_sem, plane_sem,
):
    grp, dev = lax.axis_index("grp"), lax.axis_index("dev")
    me = grp * MEMBERS + dev
    chip, core = dev // 2, dev % 2
    zc, xc = chip // 4, chip % 4

    def turned(offset):
        return jnp.where(core == 0, offset, (4 - offset) % 4)

    def at(z, x, c):
        return z % 4 * 8 + x % 4 * 2 + c

    def chip_at(offset):
        return (zc + turned(offset // 4)) % 4 * 4 + (xc + turned(offset % 4)) % 4

    def raw_copy(offset):
        to_chip = chip_at(offset)
        return pltpu.make_async_copy(
            strain_ref.at[:, pl.ds(pl.multiple_of(to_chip * 256, 256), 256)],
            raw.at[to_chip], raw_sem.at[to_chip],
        )

    def fetch(step, _):
        raw_copy(step * 7 % 16).start()
        return 0

    small = ((taps_hbm, taps_ref), (basis_hbm, basis), (tiles_hbm, tiles_ref))
    small = small + ((owner_hbm, owner_ref),)
    small_copies = [
        pltpu.make_async_copy(source, into, small_sem.at[index])
        for index, (source, into) in enumerate(small)
    ]
    for copy in small_copies:
        copy.start()
    lax.fori_loop(0, 16, fetch, 0)
    base_copy = pltpu.make_async_copy(base_ref, base, base_sem)
    base_copy.start()
    lag_copies = [
        pltpu.make_async_copy(lag0_ref, lag0, lag_sem.at[0]),
        pltpu.make_async_copy(lag1_ref, lag1, lag_sem.at[1]),
    ]
    for copy in lag_copies:
        copy.start()

    barrier = pltpu.get_barrier_semaphore()

    def greet(step, _):
        pl.semaphore_signal(
            barrier, inc=1, device_id=(grp, (dev + step) % MEMBERS), device_id_type=MESH
        )
        return 0

    lax.fori_loop(1, MEMBERS, greet, 0)
    for step in range(1, GROUPS):
        pl.semaphore_signal(
            barrier, inc=1, device_id=((grp + step) % GROUPS, dev), device_id_type=MESH
        )
    small_copies[0].wait()
    small_copies[1].wait()
    band[...] = make_band(dev, taps_ref[...])
    pl.semaphore_wait(barrier, MEMBERS - 1 + GROUPS - 1)

    def samples_to(to):
        return pltpu.make_async_remote_copy(
            src_ref=send.at[to], dst_ref=recv.at[dev], send_sem=send_sem.at[to],
            recv_sem=recv_sem.at[dev], device_id=(grp, to), device_id_type=MESH,
        )

    def decimate(pair, _):
        results = []
        for index in range(2):
            offset = (pair * 2 + index) * 7 % 16
            raw_copy(offset).wait()
            to_chip = chip_at(offset)
            result = jnp.dot(band[...], raw[to_chip], preferred_element_type=F32).astype(BF16)
            halves = jnp.dot(basis[...], result, preferred_element_type=F32)
            results.append((to_chip, (halves[:RANK] + halves[RANK:]).astype(BF16)))
        for to_chip, result in results:
            for half in range(2):
                send[to_chip * 2 + half] = result[:, half * CH : (half + 1) * CH]
                to = to_chip * 2 + half

                @pl.when(to != dev)
                def _():
                    samples_to(to).start()

        return 0

    lax.fori_loop(0, 8, decimate, 0)
    recv[dev] = send[dev]
    for step in range(1, GROUPS):
        pl.semaphore_signal(
            plane_sem, inc=1, device_id=((grp + step) % GROUPS, dev), device_id_type=MESH
        )
    for copy in small_copies[2:]:
        copy.wait()
    tile_rows = [stack_rows([tiles_ref[side : side + 1, :]], 40, 0) for side in range(2)]
    owner_rows = stack_rows([owner_ref[...].reshape(1, -1)], 40, -1)
    make_plan(me, *tile_rows, owner_rows, plan_vector)
    plan_copy = pltpu.make_async_copy(plan_vector, plan, plan_sem)
    plan_copy.start()
    plan_out = pltpu.make_async_copy(plan_vector, plan_out_ref, plan_out_sem)
    plan_out.start()
    base_copy.wait()
    acc[...] = jnp.zeros_like(acc)

    def transform(step, _):
        offset = step * 7 % 16
        from_chip = (zc - offset // 4 + 4) % 4 * 4 + (xc - offset % 4 + 4) % 4
        for half in range(2):
            source = from_chip * 2 + half

            @pl.when(source != dev)
            def _():
                pltpu.make_async_remote_copy(
                    src_ref=send.at[source], dst_ref=recv.at[source],
                    send_sem=send_sem.at[source], recv_sem=recv_sem.at[source],
                    device_id=(grp, source), device_id_type=MESH,
                ).wait_recv()

        samples = recv[pl.ds(from_chip * 2, 2)].reshape(2 * RANK, CH)
        part = from_chip // 2
        cosine, sine = turns(part)
        table = base[pl.ds(pl.multiple_of(from_chip % 2 * (2 * RANK), 2 * RANK), 2 * RANK), :]
        result = lax.dot_general(
            samples, table, (((0,), (0,)), ((), ())), preferred_element_type=F32
        )
        real, imag = result[:, :NF], result[:, NF:]
        acc[:, :NF] += real * cosine + imag * sine
        acc[:, NF:] += imag * cosine - real * sine
        return 0

    lax.fori_loop(0, 16, transform, 0)

    real, imag = acc[:, :NF], acc[:, NF:]
    power = real * real + imag * imag
    level = jnp.mean(power, axis=1, keepdims=True)
    scale = lax.rsqrt(power + level + 1e-06)
    whitened = jnp.concatenate(
        [(real * scale).reshape(16, BLK, NF), (imag * scale).reshape(16, BLK, NF)], axis=1
    ).astype(BF16)
    outs, ins = (out0, out1, out2), (in0, in1, late_ref)
    gathered = (gathered0, gathered1, gathered2, gathered3)
    gathered = gathered + (gathered4, gathered5, gathered6, gathered7)
    pl.semaphore_wait(plane_sem, GROUPS - 1)
    for piece in range(PIECES):
        line, place = line_and_place(me, piece % 3)
        gathered[piece][place] = whitened[:, :, piece * PIECE : (piece + 1) * PIECE]
        for step in (1, 3, 2):
            to = device_of(line, (place + step) % 4, piece % 3)
            pltpu.make_async_remote_copy(
                src_ref=gathered[piece].at[place], dst_ref=gathered[piece].at[place],
                send_sem=line_sem.at[piece], recv_sem=gather_sem.at[piece],
                device_id=(to // MEMBERS, to % MEMBERS), device_id_type=MESH,
            ).start()

    def select(piece, to, out):
        axis = piece % 3
        for place in range(4):
            out[place] = gathered[piece][place, plan[4 * axis + place, to]]

    def emit(piece, part):
        axis, index = piece % 3, piece - CUTS[part]
        line, place = line_and_place(me, axis)
        first, second = line // 8, line // 2 % 4

        def one(step, _):
            offset = step * 11 % 32
            to_line = (first + turned(offset // 8)) % 4 * 8 + (second + turned(offset // 2 % 4)) % 4 * 2
            to = device_of(to_line + (core + offset) % 2, place, axis)
            select(piece, to, outs[part].at[index, step])
            pltpu.make_async_remote_copy(
                src_ref=outs[part].at[index, step], dst_ref=ins[part].at[index, pl.ds(line * 4, 4)],
                send_sem=out_sem.at[part], recv_sem=in_sem.at[part],
                device_id=(to // MEMBERS, to % MEMBERS), device_id_type=MESH,
            ).start()
            return 0

        lax.fori_loop(1, MEMBERS, one, 0)
        select(piece, me, outs[part].at[index, 0])
        return pltpu.make_async_copy(
            outs[part].at[index, 0], ins[part].at[index, pl.ds(line * 4, 4)], own_sem.at[piece]
        )

    plan_copy.wait()
    own_copies = []
    for part in range(3):
        for piece in range(CUTS[part], CUTS[part + 1]):
            others = gathered[piece].at[pl.ds(0, 3)]
            pltpu.make_async_copy(others, others, gather_sem.at[piece]).wait()
            own_copies.append(emit(piece, part))
            own_copies[piece].start()

    def drain(step, _):
        samples_to((dev + step) % MEMBERS).wait_send()
        return 0

    lax.fori_loop(1, MEMBERS, drain, 0)
    def await_part(part):
        for piece in range(CUTS[part], CUTS[part + 1]):
            own_copies[piece].wait()
        others = ins[part].at[:, pl.ds(0, DEVICES - 4)]
        pltpu.make_async_copy(others, others, in_sem.at[part]).wait()

    def lagged_tiles(group, into, cross, lag, part):
        for tile in range(TILES):
            cross_spectra(into, plan, cross, group * TILES + tile, tile, axes_of(part))
        lagged = jnp.dot(cross[...], lag[...], preferred_element_type=F32)
        return lagged.reshape(TILES, BLK, BLK, NLAG)

    def first_tiles(group, _):
        first_sums[pl.ds(group * TILES, TILES)] = lagged_tiles(group, in0, cross0, lag0, 0)
        return 0

    def second_tiles(group, _):
        rows = pl.ds(group * TILES, TILES)
        partial[rows] = (first_sums[rows] + lagged_tiles(group, in1, cross1, lag1, 1)).astype(BF16)
        pltpu.make_async_copy(partial.at[rows], partial_ref.at[rows], partial_sem).start()
        return 0

    for copy in lag_copies:
        copy.wait()
    await_part(0)
    lax.fori_loop(0, SLOTS // TILES, first_tiles, 0)
    await_part(1)
    lax.fori_loop(0, SLOTS // TILES, second_tiles, 0)
    pltpu.make_async_copy(partial, partial_ref, partial_sem).wait()
    plan_out.wait()
    for part in range(3):
        sent = outs[part].at[:, pl.ds(0, MEMBERS - 1)]
        pltpu.make_async_copy(sent, sent, out_sem.at[part]).wait()
    await_part(2)
    for piece in range(PIECES):
        others = gathered[piece].at[pl.ds(0, 3)]
        pltpu.make_async_copy(others, others, line_sem.at[piece]).wait()


def late_kernel(
    plan_ref, late_ref, partial_ref, lag_ref, out_ref,
    late, lag, partial, total, cross, late_sem, lag_sem, in_sem, out_sem,
):
    count = plan_ref[15, 0]
    pieces = 4
    size = DEVICES // pieces
    late_copies = [
        pltpu.make_async_copy(
            late_ref.at[:, pl.ds(size * index, size)], late.at[:, pl.ds(size * index, size)],
            late_sem.at[index],
        )
        for index in range(pieces)
    ]
    lag_copy = pltpu.make_async_copy(lag_ref, lag, lag_sem)

    def rows(group):
        return pl.ds(group * TILES, TILES)

    def load(group):
        return pltpu.make_async_copy(
            partial_ref.at[rows(group)], partial.at[rows(group)], in_sem.at[group]
        )

    for copy in late_copies:
        copy.start()
    lag_copy.start()

    def fetch(group, _):
        load(group).start()
        return 0

    lax.fori_loop(0, SLOTS // TILES, fetch, 0)
    for copy in late_copies:
        copy.wait()
    lag_copy.wait()

    def one(group, _):
        load(group).wait()

        @pl.when(group * TILES < count)
        def _():
            for tile in range(TILES):
                cross_spectra(late, plan_ref, cross, group * TILES + tile, tile, axes_of(2))
            lagged = jnp.dot(cross[...], lag[...], preferred_element_type=F32)
            lagged = lagged + partial[rows(group)].astype(F32).reshape(lagged.shape)
            index = lax.broadcasted_iota(jnp.int32, lagged.shape, 0) // 64 + group * TILES
            total[rows(group)] = jnp.where(index < count, lagged, 0.0).reshape(TILES, BLK, BLK, NLAG)

        @pl.when(group * TILES >= count)
        def _():
            total[rows(group)] = jnp.zeros((TILES, BLK, BLK, NLAG), F32)

        pltpu.make_async_copy(total.at[rows(group)], out_ref.at[rows(group)], out_sem).start()
        return 0

    lax.fori_loop(0, SLOTS // TILES, one, 0)
    pltpu.make_async_copy(total, out_ref, out_sem).wait()


def per_device(strain, taps, tiles, owner):
    hbm = pl.BlockSpec(memory_space=pl.ANY)
    lag = lag_table()
    basis, rows = base_tables()
    lags = [
        lag.reshape(2, PIECES, PIECE, NLAG)[:, CUTS[part] : CUTS[part + 1]].reshape(-1, NLAG)
        for part in range(3)
    ]
    groups = SLOTS // TILES
    late, partial, plan = pl.pallas_call(
        exchange_kernel,
        out_shape=(
            jax.ShapeDtypeStruct((COUNTS[2], DEVICES, 2 * BLK, PIECE), BF16),
            jax.ShapeDtypeStruct((SLOTS, BLK, BLK, NLAG), BF16),
            jax.ShapeDtypeStruct((16, 128), jnp.int32),
        ),
        in_specs=[hbm] * 8,
        out_specs=(hbm, hbm, hbm),
        scratch_shapes=[
            pltpu.VMEM((16, 960, 256), BF16),
            pltpu.VMEM((1, NTAP), BF16),
            pltpu.VMEM((2, 4160), jnp.int32),
            pltpu.VMEM((4160,), jnp.int32),
            pltpu.VMEM((2 * RANK, EXT), BF16),
            pltpu.VMEM((4 * RANK, 2 * NF), BF16),
            pltpu.VMEM((2 * COUNTS[0] * PIECE, NLAG), BF16),
            pltpu.VMEM((2 * COUNTS[1] * PIECE, NLAG), BF16),
            pltpu.VMEM((EXT, 960), BF16),
            pltpu.VMEM((16, 128), jnp.int32),
            pltpu.SMEM((16, 128), jnp.int32),
            pltpu.VMEM((MEMBERS, RANK, CH), BF16),
            pltpu.VMEM((MEMBERS, RANK, CH), BF16),
            pltpu.VMEM((CH, 2 * NF), F32),
            *[pltpu.VMEM((4, 16, 2 * BLK, PIECE), BF16) for _ in range(PIECES)],
            *[pltpu.VMEM((count, MEMBERS, 4, 2 * BLK, PIECE), BF16) for count in COUNTS],
            *[pltpu.VMEM((count, DEVICES, 2 * BLK, PIECE), BF16) for count in COUNTS[:2]],
            *[pltpu.VMEM((TILES * 64, 2 * count * PIECE), BF16) for count in COUNTS[:2]],
            pltpu.VMEM((SLOTS, BLK, BLK, NLAG), F32),
            pltpu.VMEM((SLOTS, BLK, BLK, NLAG), BF16),
            pltpu.SemaphoreType.DMA((16,)),
            pltpu.SemaphoreType.DMA((4,)),
            pltpu.SemaphoreType.DMA,
            pltpu.SemaphoreType.DMA((2,)),
            pltpu.SemaphoreType.DMA,
            pltpu.SemaphoreType.DMA,
            pltpu.SemaphoreType.DMA((MEMBERS,)),
            pltpu.SemaphoreType.DMA((MEMBERS,)),
            pltpu.SemaphoreType.DMA((PIECES,)),
            pltpu.SemaphoreType.DMA((PIECES,)),
            pltpu.SemaphoreType.DMA((3,)),
            pltpu.SemaphoreType.DMA((3,)),
            pltpu.SemaphoreType.DMA((PIECES,)),
            pltpu.SemaphoreType.DMA,
            pltpu.SemaphoreType.REGULAR,
        ],
        compiler_params=pltpu.CompilerParams(
            collective_id=0, has_side_effects=True, vmem_limit_bytes=60 * 2**20
        ),
    )(
        strain.T, taps[None, :], tiles.T, owner, jnp.asarray(basis), jnp.asarray(rows),
        jnp.asarray(lags[0]), jnp.asarray(lags[1]),
    )

    return pl.pallas_call(
        late_kernel,
        out_shape=jax.ShapeDtypeStruct((SLOTS, BLK, BLK, NLAG), F32),
        in_specs=[pl.BlockSpec(memory_space=pltpu.SMEM), hbm, hbm, hbm],
        out_specs=hbm,
        scratch_shapes=[
            pltpu.VMEM((COUNTS[2], DEVICES, 2 * BLK, PIECE), BF16),
            pltpu.VMEM((2 * COUNTS[2] * PIECE, NLAG), BF16),
            pltpu.VMEM((SLOTS, BLK, BLK, NLAG), BF16),
            pltpu.VMEM((SLOTS, BLK, BLK, NLAG), F32),
            pltpu.VMEM((TILES * 64, 2 * COUNTS[2] * PIECE), BF16),
            pltpu.SemaphoreType.DMA((4,)),
            pltpu.SemaphoreType.DMA,
            pltpu.SemaphoreType.DMA((groups,)),
            pltpu.SemaphoreType.DMA,
        ],
        compiler_params=pltpu.CompilerParams(vmem_limit_bytes=60 * 2**20),
    )(plan, late, partial, jnp.asarray(lags[2]))


def solution(mesh):
    return jax.shard_map(
        per_device,
        mesh=mesh,
        in_specs=(P("grp", "dev"), P(), P(), P()),
        out_specs=P(("grp", "dev"), None, None, None),
        check_vma=False,
    )
```

```python
import functools
import math

import jax
import jax.numpy as jnp
import ml_dtypes
import numpy as np
from jax import lax
from jax.experimental import pallas as pl
from jax.experimental.pallas import tpu as pltpu
from jax.sharding import PartitionSpec as P

NT = 6144
NF = 1024
F0 = 32
NLAG = 384
NTAP = 64
DECIM = 5
BLK = 8
MEMBERS = 32
GROUPS = 4
DEVICES = 128
COLS = NT // MEMBERS
EXT = 208
USED = 205
RANK = 96
PARTS = 8
CH = 128
SLOTS = 64
PIECE = 128
PIECES = NF // PIECE
CUTS = (0, 4, 6, 7, 8)
COUNTS = (4, 2, 1, 1)
EARLY = len(COUNTS) - 1
TILES = 4
MESH = pl.DeviceIdType.MESH
F32 = jnp.float32
BF16 = jnp.bfloat16


def trig(phase, factor=1.0):
    angle = np.float32(2.0 * math.pi / NT) * phase.astype(np.float32)
    angle = angle.astype(np.float64)
    return np.cos(angle) * factor, -np.sin(angle) * factor


def base_tables():
    samples = np.arange(USED)
    width = (F0 + NF) / NT
    steps = samples[1:] * (USED - samples[1:]) / 2
    diagonal = ((USED - 1) / 2 - samples) ** 2 * math.cos(2 * math.pi * width)
    _, vectors = np.linalg.eigh(np.diag(diagonal) + np.diag(steps, 1) + np.diag(steps, -1))
    basis = vectors[:, ::-1][:, :RANK].T
    half = basis[:, : USED // 2]
    basis = basis * np.sign(np.take_along_axis(half, np.abs(half).argmax(axis=1)[:, None], axis=1))

    def table(place):
        rows = place * COLS + samples
        angle = 2.0 * math.pi / NT * (rows[:, None] * (F0 + np.arange(NF))[None, :] % NT)
        return np.concatenate([np.cos(angle), -np.sin(angle)], axis=1)

    assert np.abs(basis.T @ (basis @ table(0)) - table(0)).max() < 1e-10
    rows = np.concatenate([basis @ table(place) for place in range(MEMBERS)], axis=0)
    basis = np.pad(basis, ((0, 0), (0, EXT - USED)))
    high = basis.astype(ml_dtypes.bfloat16)
    low = (basis - high.astype(np.float64)).astype(ml_dtypes.bfloat16)
    return np.concatenate([high, low], axis=0), rows.astype(ml_dtypes.bfloat16)


def lag_table():
    lags = (np.arange(NLAG) - NLAG // 2) % NT
    phase = (F0 + np.arange(NF))[:, None] * lags[None, :] % NT
    real, imag = trig(phase, 1.0 / math.sqrt(NF))
    return np.concatenate([real, imag], axis=0).astype(ml_dtypes.bfloat16)


def nt_dot(a, b):
    return lax.dot_general(a, b, (((1,), (1,)), ((), ())), preferred_element_type=F32)


def stack_rows(pieces, rows, fill):
    width = sum(piece.shape[1] for piece in pieces)
    extra = jnp.full((1, rows * 128 - width), fill, jnp.int32)
    line = jnp.concatenate([*pieces, extra], axis=1)
    return jnp.concatenate(
        [line[:, index * 128 : (index + 1) * 128] for index in range(rows)], axis=0
    )


def make_band(member, taps):
    tap = lax.broadcasted_iota(jnp.int32, (NTAP, 1024), 0)
    lane = lax.broadcasted_iota(jnp.int32, (NTAP, 1024), 1)
    place = (lane == (1024 - tap) % 1024).astype(F32).astype(BF16)
    taps = jnp.broadcast_to(taps.astype(F32), (8, NTAP)).astype(BF16)
    line = jnp.dot(taps, place, preferred_element_type=F32)
    first_rows = pltpu.roll(line, 0, 1, stride=DECIM, stride_axis=0)
    band = jnp.concatenate(
        [pltpu.roll(first_rows, 8 * DECIM * index, 1) for index in range(EXT // 8)], axis=0
    )
    row = lax.broadcasted_iota(jnp.int32, (EXT, 1024), 0)
    limit = jnp.where(member == MEMBERS - 1, COLS, USED)
    return jnp.where(row < limit, band, 0.0)[:, :960].astype(BF16)


def coordinates(device):
    return device // 8 % 4, device // 2 % 4, device // 32, device % 2


def line_and_place(device, axis):
    z, x, y, c = coordinates(device)
    if axis == 0:
        return y * 8 + x * 2 + c, z
    if axis == 1:
        return y * 8 + z * 2 + c, x
    return z * 8 + x * 2 + c, y


def device_of(line, place, axis):
    first, second, c = line // 8, line // 2 % 4, line % 2
    if axis == 0:
        return first * 32 + place * 8 + second * 2 + c
    if axis == 1:
        return first * 32 + second * 8 + place * 2 + c
    return place * 32 + line


def make_plan(me, src, dst, own, plan_ref):
    rows = src.shape[0]
    mine = own == me
    lane_a = lax.broadcasted_iota(jnp.int32, (128, 128), 0)
    lane = lax.broadcasted_iota(jnp.int32, (rows, 128), 1)
    row = lax.broadcasted_iota(jnp.int32, (rows, 128), 0)
    flags = jnp.where(mine, 1, 0)
    within = flags
    for shift in (1, 2, 4, 8, 16, 32, 64):
        within = within + jnp.where(lane >= shift, pltpu.roll(within, shift, 1), 0)
    totals = jnp.broadcast_to(jnp.sum(flags, axis=1, keepdims=True), (rows, 128))
    before = totals
    for shift in (1, 2, 4, 8, 16, 32):
        before = before + jnp.where(row >= shift, pltpu.roll(before, shift, 0), 0)
    slot = jnp.where(mine, within - flags + before - totals, -1)
    src_dev, dst_dev = src // 16, dst // 16

    first = jnp.zeros((SLOTS, 128), jnp.int32)
    second = jnp.zeros((SLOTS, 128), jnp.int32)
    for index in range(rows):
        hit = slot[index : index + 1, :] == lane_a[:SLOTS]
        first = first + jnp.where(hit, src_dev[index : index + 1, :], 0)
        second = second + jnp.where(hit, dst_dev[index : index + 1, :], 0)
    ends = jnp.sum(jnp.concatenate([first, second], axis=0).T, axis=0, keepdims=True)
    lines = []
    for axis in range(3):
        line, place = line_and_place(ends, axis)
        lines.append(line * 4 + place)
    count = jnp.sum(flags, axis=(0, 1), keepdims=True)
    lines.append(jnp.broadcast_to(count, (1, 128)))
    plan_ref[12:16, :] = jnp.concatenate(lines, axis=0)

    z, x, y, _ = coordinates(me)

    def wanted(entry, _):
        axis, place = entry // 4, entry % 4
        source = jnp.where(
            axis == 0, me + (place - z) * 8, jnp.where(axis == 1, me + (place - x) * 2, me + (place - y) * 32)
        )
        local = jnp.where(src_dev == source, src % 16, 0) + jnp.where(dst_dev == source, dst % 16, 0)
        blocks = jnp.zeros((128, 128), jnp.int32)
        for index in range(rows):
            hit = own[index : index + 1, :] == lane_a
            blocks = blocks + jnp.where(hit, local[index : index + 1, :], 0)
        plan_ref[pl.ds(entry, 1), :] = jnp.sum(blocks.T, axis=0, keepdims=True)
        return 0

    lax.fori_loop(0, 12, wanted, 0)


def cross_spectra(into, plan, cross, slot, tile, axes):
    width = len(axes) * PIECE
    for index, axis in enumerate(axes):
        a = into[index, plan[12 + axis, slot]].astype(F32)
        b = into[index, plan[12 + axis, SLOTS + slot]].astype(F32)
        ar, ai, br, bi = a[:BLK], a[BLK:], b[:BLK], b[BLK:]
        left = index * PIECE
        for pair in range(BLK // 2):
            reals, imags = [], []
            for i in (2 * pair, 2 * pair + 1):
                xr, xi = ar[i : i + 1, :], ai[i : i + 1, :]
                reals.append(xr * br + xi * bi)
                imags.append(xi * br - xr * bi)
            at = tile * 64 + pair * 16
            cross[at : at + 16, left : left + PIECE] = jnp.concatenate(reals, axis=0).astype(BF16)
            cross[at : at + 16, width + left : width + left + PIECE] = jnp.concatenate(
                imags, axis=0
            ).astype(BF16)


def axes_of(part):
    return [piece % 3 for piece in range(CUTS[part], CUTS[part + 1])]


def exchange_kernel(
    strain_ref, taps_hbm, tiles_hbm, owner_hbm, basis_hbm, base_ref, lag0_ref, lag1_ref, lag2_ref,
    late_ref, partial_ref, plan_out_ref,
    raw, taps_ref, tiles_ref, owner_ref, basis, base, lag0, lag1, lag2, band, plan_vector, plan, send, recv, acc,
    gathered0, gathered1, gathered2, gathered3, gathered4, gathered5, gathered6, gathered7,
    out0, out1, out2, out3, in0, in1, in2, cross0, cross1, cross2, first_sums, partial,
    raw_sem, small_sem, base_sem, lag_sem, plan_sem, plan_out_sem, send_sem, recv_sem,
    line_sem, gather_sem, out_sem, in_sem, own_sem, partial_sem, plane_sem,
):
    grp, dev = lax.axis_index("grp"), lax.axis_index("dev")
    me = grp * MEMBERS + dev
    chip, core = dev // 2, dev % 2
    zc, xc = chip // 4, chip % 4

    def turned(offset):
        return jnp.where(core == 0, offset, (4 - offset) % 4)

    def at(z, x, c):
        return z % 4 * 8 + x % 4 * 2 + c

    def chip_at(offset):
        return (zc + turned(offset // 4)) % 4 * 4 + (xc + turned(offset % 4)) % 4

    def raw_copy(offset):
        to_chip = chip_at(offset)
        return pltpu.make_async_copy(
            strain_ref.at[:, pl.ds(pl.multiple_of(to_chip * 256, 256), 256)],
            raw.at[to_chip], raw_sem.at[to_chip],
        )

    def fetch(step, _):
        raw_copy(step * 7 % 16).start()
        return 0

    small = ((taps_hbm, taps_ref), (basis_hbm, basis), (tiles_hbm, tiles_ref))
    small = small + ((owner_hbm, owner_ref),)
    small_copies = [
        pltpu.make_async_copy(source, into, small_sem.at[index])
        for index, (source, into) in enumerate(small)
    ]
    for copy in small_copies:
        copy.start()
    lax.fori_loop(0, 16, fetch, 0)
    base_copy = pltpu.make_async_copy(base_ref, base, base_sem)
    base_copy.start()
    lag_copies = [
        pltpu.make_async_copy(lag0_ref, lag0, lag_sem.at[0]),
        pltpu.make_async_copy(lag1_ref, lag1, lag_sem.at[1]),
        pltpu.make_async_copy(lag2_ref, lag2, lag_sem.at[2]),
    ]
    for copy in lag_copies:
        copy.start()

    barrier = pltpu.get_barrier_semaphore()

    def greet(step, _):
        pl.semaphore_signal(
            barrier, inc=1, device_id=(grp, (dev + step) % MEMBERS), device_id_type=MESH
        )
        return 0

    lax.fori_loop(1, MEMBERS, greet, 0)
    for step in range(1, GROUPS):
        pl.semaphore_signal(
            barrier, inc=1, device_id=((grp + step) % GROUPS, dev), device_id_type=MESH
        )
    small_copies[0].wait()
    small_copies[1].wait()
    band[...] = make_band(dev, taps_ref[...])
    pl.semaphore_wait(barrier, MEMBERS - 1 + GROUPS - 1)

    def samples_to(to):
        return pltpu.make_async_remote_copy(
            src_ref=send.at[to], dst_ref=recv.at[dev], send_sem=send_sem.at[to],
            recv_sem=recv_sem.at[dev], device_id=(grp, to), device_id_type=MESH,
        )

    def decimate(pair, _):
        results = []
        for index in range(2):
            offset = (pair * 2 + index) * 7 % 16
            raw_copy(offset).wait()
            to_chip = chip_at(offset)
            result = jnp.dot(band[...], raw[to_chip], preferred_element_type=F32).astype(BF16)
            halves = jnp.dot(basis[...], result, preferred_element_type=F32)
            results.append((to_chip, (halves[:RANK] + halves[RANK:]).astype(BF16)))
        for to_chip, result in results:
            for half in range(2):
                send[to_chip * 2 + half] = result[:, half * CH : (half + 1) * CH]
                to = to_chip * 2 + half

                @pl.when(to != dev)
                def _():
                    samples_to(to).start()

        return 0

    lax.fori_loop(0, 8, decimate, 0)
    recv[dev] = send[dev]
    for step in range(1, GROUPS):
        pl.semaphore_signal(
            plane_sem, inc=1, device_id=((grp + step) % GROUPS, dev), device_id_type=MESH
        )
    base_copy.wait()
    acc[...] = jnp.zeros_like(acc)

    def transform(step, _):
        plane = (zc + step) % 4
        first = plane * 8
        for index in range(8):
            source = first + index

            @pl.when(source != dev)
            def _():
                pltpu.make_async_remote_copy(
                    src_ref=send.at[source], dst_ref=recv.at[source],
                    send_sem=send_sem.at[source], recv_sem=recv_sem.at[source],
                    device_id=(grp, source), device_id_type=MESH,
                ).wait_recv()

        samples = recv[pl.ds(first, 8)].reshape(8 * RANK, CH)
        acc[...] += lax.dot_general(
            samples, base[plane], (((0,), (0,)), ((), ())), preferred_element_type=F32
        )
        return 0

    lax.fori_loop(0, 4, transform, 0)

    real, imag = acc[:, :NF], acc[:, NF:]
    power = real * real + imag * imag
    level = jnp.mean(power, axis=1, keepdims=True)
    scale = lax.rsqrt(power + level + 1e-06)
    whitened = jnp.concatenate(
        [(real * scale).reshape(16, BLK, NF), (imag * scale).reshape(16, BLK, NF)], axis=1
    ).astype(BF16)
    outs, ins = (out0, out1, out2, out3), (in0, in1, in2, late_ref)
    crosses, lags = (cross0, cross1, cross2), (lag0, lag1, lag2)
    gathered = (gathered0, gathered1, gathered2, gathered3)
    gathered = gathered + (gathered4, gathered5, gathered6, gathered7)
    pl.semaphore_wait(plane_sem, GROUPS - 1)
    for piece in range(PIECES):
        line, place = line_and_place(me, piece % 3)
        gathered[piece][place] = whitened[:, :, piece * PIECE : (piece + 1) * PIECE]
        for step in (1, 3, 2):
            to = device_of(line, (place + step) % 4, piece % 3)
            pltpu.make_async_remote_copy(
                src_ref=gathered[piece].at[place], dst_ref=gathered[piece].at[place],
                send_sem=line_sem.at[piece], recv_sem=gather_sem.at[piece],
                device_id=(to // MEMBERS, to % MEMBERS), device_id_type=MESH,
            ).start()

    def select(piece, to, out):
        axis = piece % 3
        for place in range(4):
            out[place] = gathered[piece][place, plan[4 * axis + place, to]]

    def emit(piece, part):
        axis, index = piece % 3, piece - CUTS[part]
        line, place = line_and_place(me, axis)
        first, second = line // 8, line // 2 % 4

        def one(step, _):
            offset = step * 11 % 32
            to_line = (first + turned(offset // 8)) % 4 * 8 + (second + turned(offset // 2 % 4)) % 4 * 2
            to = device_of(to_line + (core + offset) % 2, place, axis)
            select(piece, to, outs[part].at[index, step])
            pltpu.make_async_remote_copy(
                src_ref=outs[part].at[index, step], dst_ref=ins[part].at[index, pl.ds(line * 4, 4)],
                send_sem=out_sem.at[part], recv_sem=in_sem.at[part],
                device_id=(to // MEMBERS, to % MEMBERS), device_id_type=MESH,
            ).start()
            return 0

        lax.fori_loop(1, MEMBERS, one, 0)
        select(piece, me, outs[part].at[index, 0])
        return pltpu.make_async_copy(
            outs[part].at[index, 0], ins[part].at[index, pl.ds(line * 4, 4)], own_sem.at[piece]
        )

    for copy in small_copies[2:]:
        copy.wait()
    tile_rows = [stack_rows([tiles_ref[side : side + 1, :]], 40, 0) for side in range(2)]
    owner_rows = stack_rows([owner_ref[...].reshape(1, -1)], 40, -1)
    make_plan(me, *tile_rows, owner_rows, plan_vector)
    plan_copy = pltpu.make_async_copy(plan_vector, plan, plan_sem)
    plan_copy.start()
    plan_out = pltpu.make_async_copy(plan_vector, plan_out_ref, plan_out_sem)
    plan_out.start()
    plan_copy.wait()
    own_copies = []
    for part in range(EARLY + 1):
        for piece in range(CUTS[part], CUTS[part + 1]):
            others = gathered[piece].at[pl.ds(0, 3)]
            pltpu.make_async_copy(others, others, gather_sem.at[piece]).wait()
            own_copies.append(emit(piece, part))
            own_copies[piece].start()

    def drain(step, _):
        samples_to((dev + step) % MEMBERS).wait_send()
        return 0

    lax.fori_loop(1, MEMBERS, drain, 0)
    def await_part(part):
        for piece in range(CUTS[part], CUTS[part + 1]):
            own_copies[piece].wait()
        others = ins[part].at[:, pl.ds(0, DEVICES - 4)]
        pltpu.make_async_copy(others, others, in_sem.at[part]).wait()

    def tiles_of(part):
        def one(group, _):
            for tile in range(TILES):
                cross_spectra(ins[part], plan, crosses[part], group * TILES + tile, tile, axes_of(part))
            lagged = jnp.dot(crosses[part][...], lags[part][...], preferred_element_type=F32)
            lagged = lagged.reshape(TILES, BLK, BLK, NLAG)
            rows = pl.ds(group * TILES, TILES)
            if part > 0:
                lagged = lagged + first_sums[rows]
            if part < EARLY - 1:
                first_sums[rows] = lagged
            else:
                partial[rows] = lagged.astype(BF16)
                pltpu.make_async_copy(partial.at[rows], partial_ref.at[rows], partial_sem).start()
            return 0

        lax.fori_loop(0, SLOTS // TILES, one, 0)

    for copy in lag_copies:
        copy.wait()
    for part in range(EARLY):
        await_part(part)
        tiles_of(part)
    pltpu.make_async_copy(partial, partial_ref, partial_sem).wait()
    plan_out.wait()
    for part in range(EARLY + 1):
        sent = outs[part].at[:, pl.ds(0, MEMBERS - 1)]
        pltpu.make_async_copy(sent, sent, out_sem.at[part]).wait()
    await_part(EARLY)
    for piece in range(PIECES):
        others = gathered[piece].at[pl.ds(0, 3)]
        pltpu.make_async_copy(others, others, line_sem.at[piece]).wait()


def late_kernel(
    plan_ref, late_ref, partial_ref, lag_ref, out_ref,
    late, lag, partial, total, cross, late_sem, lag_sem, in_sem, out_sem,
):
    count = plan_ref[15, 0]
    pieces = 4
    size = DEVICES // pieces
    late_copies = [
        pltpu.make_async_copy(
            late_ref.at[:, pl.ds(size * index, size)], late.at[:, pl.ds(size * index, size)],
            late_sem.at[index],
        )
        for index in range(pieces)
    ]
    lag_copy = pltpu.make_async_copy(lag_ref, lag, lag_sem)

    def rows(group):
        return pl.ds(group * TILES, TILES)

    def load(group):
        return pltpu.make_async_copy(
            partial_ref.at[rows(group)], partial.at[rows(group)], in_sem.at[group]
        )

    for copy in late_copies:
        copy.start()
    lag_copy.start()

    def fetch(group, _):
        load(group).start()
        return 0

    lax.fori_loop(0, SLOTS // TILES, fetch, 0)
    for copy in late_copies:
        copy.wait()
    lag_copy.wait()

    def one(group, _):
        load(group).wait()

        @pl.when(group * TILES < count)
        def _():
            for tile in range(TILES):
                cross_spectra(late, plan_ref, cross, group * TILES + tile, tile, axes_of(EARLY))
            lagged = jnp.dot(cross[...], lag[...], preferred_element_type=F32)
            lagged = lagged + partial[rows(group)].astype(F32).reshape(lagged.shape)
            index = lax.broadcasted_iota(jnp.int32, lagged.shape, 0) // 64 + group * TILES
            total[rows(group)] = jnp.where(index < count, lagged, 0.0).reshape(TILES, BLK, BLK, NLAG)

        @pl.when(group * TILES >= count)
        def _():
            total[rows(group)] = jnp.zeros((TILES, BLK, BLK, NLAG), F32)

        pltpu.make_async_copy(total.at[rows(group)], out_ref.at[rows(group)], out_sem).start()
        return 0

    lax.fori_loop(0, SLOTS // TILES, one, 0)
    pltpu.make_async_copy(total, out_ref, out_sem).wait()


def per_device(strain, taps, tiles, owner):
    hbm = pl.BlockSpec(memory_space=pl.ANY)
    lag = lag_table()
    basis, rows = base_tables()
    lags = [
        lag.reshape(2, PIECES, PIECE, NLAG)[:, CUTS[part] : CUTS[part + 1]].reshape(-1, NLAG)
        for part in range(EARLY + 1)
    ]
    groups = SLOTS // TILES
    late, partial, plan = pl.pallas_call(
        exchange_kernel,
        out_shape=(
            jax.ShapeDtypeStruct((COUNTS[EARLY], DEVICES, 2 * BLK, PIECE), BF16),
            jax.ShapeDtypeStruct((SLOTS, BLK, BLK, NLAG), BF16),
            jax.ShapeDtypeStruct((16, 128), jnp.int32),
        ),
        in_specs=[hbm] * (6 + EARLY),
        out_specs=(hbm, hbm, hbm),
        scratch_shapes=[
            pltpu.VMEM((16, 960, 256), BF16),
            pltpu.VMEM((1, NTAP), BF16),
            pltpu.VMEM((2, 4160), jnp.int32),
            pltpu.VMEM((4160,), jnp.int32),
            pltpu.VMEM((2 * RANK, EXT), BF16),
            pltpu.VMEM((4, 8 * RANK, 2 * NF), BF16),
            *[pltpu.VMEM((2 * count * PIECE, NLAG), BF16) for count in COUNTS[:EARLY]],
            pltpu.VMEM((EXT, 960), BF16),
            pltpu.VMEM((16, 128), jnp.int32),
            pltpu.SMEM((16, 128), jnp.int32),
            pltpu.VMEM((MEMBERS, RANK, CH), BF16),
            pltpu.VMEM((MEMBERS, RANK, CH), BF16),
            pltpu.VMEM((CH, 2 * NF), F32),
            *[pltpu.VMEM((4, 16, 2 * BLK, PIECE), BF16) for _ in range(PIECES)],
            *[pltpu.VMEM((count, MEMBERS, 4, 2 * BLK, PIECE), BF16) for count in COUNTS],
            *[pltpu.VMEM((count, DEVICES, 2 * BLK, PIECE), BF16) for count in COUNTS[:EARLY]],
            *[pltpu.VMEM((TILES * 64, 2 * count * PIECE), BF16) for count in COUNTS[:EARLY]],
            pltpu.VMEM((SLOTS, BLK, BLK, NLAG), F32),
            pltpu.VMEM((SLOTS, BLK, BLK, NLAG), BF16),
            pltpu.SemaphoreType.DMA((16,)),
            pltpu.SemaphoreType.DMA((4,)),
            pltpu.SemaphoreType.DMA,
            pltpu.SemaphoreType.DMA((EARLY,)),
            pltpu.SemaphoreType.DMA,
            pltpu.SemaphoreType.DMA,
            pltpu.SemaphoreType.DMA((MEMBERS,)),
            pltpu.SemaphoreType.DMA((MEMBERS,)),
            pltpu.SemaphoreType.DMA((PIECES,)),
            pltpu.SemaphoreType.DMA((PIECES,)),
            pltpu.SemaphoreType.DMA((EARLY + 1,)),
            pltpu.SemaphoreType.DMA((EARLY + 1,)),
            pltpu.SemaphoreType.DMA((PIECES,)),
            pltpu.SemaphoreType.DMA,
            pltpu.SemaphoreType.REGULAR,
        ],
        compiler_params=pltpu.CompilerParams(
            collective_id=0, has_side_effects=True, vmem_limit_bytes=60 * 2**20
        ),
    )(
        strain.T, taps[None, :], tiles.T, owner, jnp.asarray(basis), jnp.asarray(rows.reshape(4, 8 * RANK, 2 * NF)),
        *[jnp.asarray(part) for part in lags[:EARLY]],
    )

    return pl.pallas_call(
        late_kernel,
        out_shape=jax.ShapeDtypeStruct((SLOTS, BLK, BLK, NLAG), F32),
        in_specs=[pl.BlockSpec(memory_space=pltpu.SMEM), hbm, hbm, hbm],
        out_specs=hbm,
        scratch_shapes=[
            pltpu.VMEM((COUNTS[EARLY], DEVICES, 2 * BLK, PIECE), BF16),
            pltpu.VMEM((2 * COUNTS[EARLY] * PIECE, NLAG), BF16),
            pltpu.VMEM((SLOTS, BLK, BLK, NLAG), BF16),
            pltpu.VMEM((SLOTS, BLK, BLK, NLAG), F32),
            pltpu.VMEM((TILES * 64, 2 * COUNTS[EARLY] * PIECE), BF16),
            pltpu.SemaphoreType.DMA((4,)),
            pltpu.SemaphoreType.DMA,
            pltpu.SemaphoreType.DMA((groups,)),
            pltpu.SemaphoreType.DMA,
        ],
        compiler_params=pltpu.CompilerParams(vmem_limit_bytes=60 * 2**20),
    )(plan, late, partial, jnp.asarray(lags[EARLY]))


def solution(mesh):
    return jax.shard_map(
        per_device,
        mesh=mesh,
        in_specs=(P("grp", "dev"), P(), P(), P()),
        out_specs=P(("grp", "dev"), None, None, None),
        check_vma=False,
    )
```

```python
import functools
import math

import jax
import jax.numpy as jnp
import ml_dtypes
import numpy as np
from jax import lax
from jax.experimental import pallas as pl
from jax.experimental.pallas import tpu as pltpu
from jax.sharding import PartitionSpec as P

NT = 6144
NF = 1024
F0 = 32
NLAG = 384
NTAP = 64
DECIM = 5
BLK = 8
MEMBERS = 32
GROUPS = 4
DEVICES = 128
COLS = NT // MEMBERS
EXT = 208
USED = 205
RANK = 96
STRETCHES = ((0, 64), (48, 120), (96, 168), (144, 208))
PARTS = 8
CH = 128
SLOTS = 64
PIECE = 128
PIECES = NF // PIECE
CUTS = (0, 4, 6, 7, 8)
COUNTS = (4, 2, 1, 1)
EARLY = len(COUNTS) - 1
TILES = 4
MESH = pl.DeviceIdType.MESH
F32 = jnp.float32
BF16 = jnp.bfloat16


def trig(phase, factor=1.0):
    angle = np.float32(2.0 * math.pi / NT) * phase.astype(np.float32)
    angle = angle.astype(np.float64)
    return np.cos(angle) * factor, -np.sin(angle) * factor


def base_tables():
    samples = np.arange(USED)
    width = (F0 + NF) / NT
    steps = samples[1:] * (USED - samples[1:]) / 2
    diagonal = ((USED - 1) / 2 - samples) ** 2 * math.cos(2 * math.pi * width)
    _, vectors = np.linalg.eigh(np.diag(diagonal) + np.diag(steps, 1) + np.diag(steps, -1))
    basis = vectors[:, ::-1][:, :RANK].T
    half = basis[:, : USED // 2]
    basis = basis * np.sign(np.take_along_axis(half, np.abs(half).argmax(axis=1)[:, None], axis=1))

    def table(place):
        rows = place * COLS + samples
        angle = 2.0 * math.pi / NT * (rows[:, None] * (F0 + np.arange(NF))[None, :] % NT)
        return np.concatenate([np.cos(angle), -np.sin(angle)], axis=1)

    assert np.abs(basis.T @ (basis @ table(0)) - table(0)).max() < 1e-10
    rows = np.concatenate([basis @ table(place) for place in range(MEMBERS)], axis=0)
    basis = np.pad(basis, ((0, 0), (0, EXT - USED)))
    high = basis.astype(ml_dtypes.bfloat16)
    low = (basis - high.astype(np.float64)).astype(ml_dtypes.bfloat16)
    return np.concatenate([high, low], axis=0), rows.astype(ml_dtypes.bfloat16)


def lag_table():
    lags = (np.arange(NLAG) - NLAG // 2) % NT
    phase = (F0 + np.arange(NF))[:, None] * lags[None, :] % NT
    real, imag = trig(phase, 1.0 / math.sqrt(NF))
    return np.concatenate([real, imag], axis=0).astype(ml_dtypes.bfloat16)


def nt_dot(a, b):
    return lax.dot_general(a, b, (((1,), (1,)), ((), ())), preferred_element_type=F32)


def stack_rows(pieces, rows, fill):
    width = sum(piece.shape[1] for piece in pieces)
    extra = jnp.full((1, rows * 128 - width), fill, jnp.int32)
    line = jnp.concatenate([*pieces, extra], axis=1)
    return jnp.concatenate(
        [line[:, index * 128 : (index + 1) * 128] for index in range(rows)], axis=0
    )


def make_band(member, taps):
    tap = lax.broadcasted_iota(jnp.int32, (NTAP, 1024), 0)
    lane = lax.broadcasted_iota(jnp.int32, (NTAP, 1024), 1)
    place = (lane == (1024 - tap) % 1024).astype(F32).astype(BF16)
    taps = jnp.broadcast_to(taps.astype(F32), (8, NTAP)).astype(BF16)
    line = jnp.dot(taps, place, preferred_element_type=F32)
    first_rows = pltpu.roll(line, 0, 1, stride=DECIM, stride_axis=0)
    band = jnp.concatenate(
        [pltpu.roll(first_rows, 8 * DECIM * index, 1) for index in range(EXT // 8)], axis=0
    )
    row = lax.broadcasted_iota(jnp.int32, (EXT, 1024), 0)
    limit = jnp.where(member == MEMBERS - 1, COLS, USED)
    return jnp.where(row < limit, band, 0.0)[:, :960].astype(BF16)


def filtered(band, raw):
    count = raw.shape[0]
    sums = [
        jnp.dot(
            band[low:high, 256 * index : min(256 * (index + 1), count)],
            raw[256 * index : min(256 * (index + 1), count)],
            preferred_element_type=F32,
        )
        for index, (low, high) in enumerate(STRETCHES)
    ]
    pieces = []
    done = 0
    for index, (low, high) in enumerate(STRETCHES):
        end = STRETCHES[index + 1][0] if index + 1 < len(STRETCHES) else high
        pieces.append(sums[index][done - low : end - low])
        if end < high:
            after = STRETCHES[index + 1][0]
            pieces.append(sums[index][end - low :] + sums[index + 1][: high - after])
        done = high
    return jnp.concatenate(pieces, axis=0)


def coordinates(device):
    return device // 8 % 4, device // 2 % 4, device // 32, device % 2


def line_and_place(device, axis):
    z, x, y, c = coordinates(device)
    if axis == 0:
        return y * 8 + x * 2 + c, z
    if axis == 1:
        return y * 8 + z * 2 + c, x
    return z * 8 + x * 2 + c, y


def device_of(line, place, axis):
    first, second, c = line // 8, line // 2 % 4, line % 2
    if axis == 0:
        return first * 32 + place * 8 + second * 2 + c
    if axis == 1:
        return first * 32 + second * 8 + place * 2 + c
    return place * 32 + line


def make_plan(me, src, dst, own, plan_ref):
    rows = src.shape[0]
    mine = own == me
    lane_a = lax.broadcasted_iota(jnp.int32, (128, 128), 0)
    lane = lax.broadcasted_iota(jnp.int32, (rows, 128), 1)
    row = lax.broadcasted_iota(jnp.int32, (rows, 128), 0)
    flags = jnp.where(mine, 1, 0)
    within = flags
    for shift in (1, 2, 4, 8, 16, 32, 64):
        within = within + jnp.where(lane >= shift, pltpu.roll(within, shift, 1), 0)
    totals = jnp.broadcast_to(jnp.sum(flags, axis=1, keepdims=True), (rows, 128))
    before = totals
    for shift in (1, 2, 4, 8, 16, 32):
        before = before + jnp.where(row >= shift, pltpu.roll(before, shift, 0), 0)
    slot = jnp.where(mine, within - flags + before - totals, -1)
    src_dev, dst_dev = src // 16, dst // 16

    first = jnp.zeros((SLOTS, 128), jnp.int32)
    second = jnp.zeros((SLOTS, 128), jnp.int32)
    for index in range(rows):
        hit = slot[index : index + 1, :] == lane_a[:SLOTS]
        first = first + jnp.where(hit, src_dev[index : index + 1, :], 0)
        second = second + jnp.where(hit, dst_dev[index : index + 1, :], 0)
    ends = jnp.sum(jnp.concatenate([first, second], axis=0).T, axis=0, keepdims=True)
    lines = []
    for axis in range(3):
        line, place = line_and_place(ends, axis)
        lines.append(line * 4 + place)
    count = jnp.sum(flags, axis=(0, 1), keepdims=True)
    lines.append(jnp.broadcast_to(count, (1, 128)))
    plan_ref[12:16, :] = jnp.concatenate(lines, axis=0)

    z, x, y, _ = coordinates(me)

    def wanted(entry, _):
        axis, place = entry // 4, entry % 4
        source = jnp.where(
            axis == 0, me + (place - z) * 8, jnp.where(axis == 1, me + (place - x) * 2, me + (place - y) * 32)
        )
        local = jnp.where(src_dev == source, src % 16, 0) + jnp.where(dst_dev == source, dst % 16, 0)
        blocks = jnp.zeros((128, 128), jnp.int32)
        for index in range(rows):
            hit = own[index : index + 1, :] == lane_a
            blocks = blocks + jnp.where(hit, local[index : index + 1, :], 0)
        plan_ref[pl.ds(entry, 1), :] = jnp.sum(blocks.T, axis=0, keepdims=True)
        return 0

    lax.fori_loop(0, 12, wanted, 0)


def cross_spectra(into, plan, cross, slot, tile, axes):
    width = len(axes) * PIECE
    for index, axis in enumerate(axes):
        a = into[index, plan[12 + axis, slot]].astype(F32)
        b = into[index, plan[12 + axis, SLOTS + slot]].astype(F32)
        ar, ai, br, bi = a[:BLK], a[BLK:], b[:BLK], b[BLK:]
        left = index * PIECE
        for pair in range(BLK // 2):
            reals, imags = [], []
            for i in (2 * pair, 2 * pair + 1):
                xr, xi = ar[i : i + 1, :], ai[i : i + 1, :]
                reals.append(xr * br + xi * bi)
                imags.append(xi * br - xr * bi)
            at = tile * 64 + pair * 16
            cross[at : at + 16, left : left + PIECE] = jnp.concatenate(reals, axis=0).astype(BF16)
            cross[at : at + 16, width + left : width + left + PIECE] = jnp.concatenate(
                imags, axis=0
            ).astype(BF16)


def axes_of(part):
    return [piece % 3 for piece in range(CUTS[part], CUTS[part + 1])]


def exchange_kernel(
    strain_ref, taps_hbm, tiles_hbm, owner_hbm, basis_hbm, base_ref, lag0_ref, lag1_ref, lag2_ref,
    late_ref, partial_ref, plan_out_ref,
    raw, taps_ref, tiles_ref, owner_ref, basis, base, lag0, lag1, lag2, band, plan_vector, plan, send, recv, acc,
    gathered0, gathered1, gathered2, gathered3, gathered4, gathered5, gathered6, gathered7,
    out0, out1, out2, out3, in0, in1, in2, cross0, cross1, cross2, first_sums, partial,
    raw_sem, small_sem, base_sem, lag_sem, plan_sem, plan_out_sem, send_sem, recv_sem,
    line_sem, gather_sem, out_sem, in_sem, own_sem, partial_sem, plane_sem,
):
    grp, dev = lax.axis_index("grp"), lax.axis_index("dev")
    me = grp * MEMBERS + dev
    chip, core = dev // 2, dev % 2
    zc, xc = chip // 4, chip % 4

    def turned(offset):
        return jnp.where(core == 0, offset, (4 - offset) % 4)

    def at(z, x, c):
        return z % 4 * 8 + x % 4 * 2 + c

    def chip_at(offset):
        return (zc + turned(offset // 4)) % 4 * 4 + (xc + turned(offset % 4)) % 4

    def raw_copy(offset):
        to_chip = chip_at(offset)
        return pltpu.make_async_copy(
            strain_ref.at[:, pl.ds(pl.multiple_of(to_chip * 256, 256), 256)],
            raw.at[to_chip], raw_sem.at[to_chip],
        )

    def fetch(step, _):
        raw_copy(step * 7 % 16).start()
        return 0

    small = ((taps_hbm, taps_ref), (basis_hbm, basis), (tiles_hbm, tiles_ref))
    small = small + ((owner_hbm, owner_ref),)
    small_copies = [
        pltpu.make_async_copy(source, into, small_sem.at[index])
        for index, (source, into) in enumerate(small)
    ]
    for copy in small_copies:
        copy.start()
    lax.fori_loop(0, 16, fetch, 0)
    def base_copy(plane):
        return pltpu.make_async_copy(base_ref.at[plane], base.at[plane], base_sem.at[plane])

    lag_copies = [
        pltpu.make_async_copy(lag0_ref, lag0, lag_sem.at[0]),
        pltpu.make_async_copy(lag1_ref, lag1, lag_sem.at[1]),
        pltpu.make_async_copy(lag2_ref, lag2, lag_sem.at[2]),
    ]

    barrier = pltpu.get_barrier_semaphore()

    def greet(step, _):
        pl.semaphore_signal(
            barrier, inc=1, device_id=(grp, (dev + step) % MEMBERS), device_id_type=MESH
        )
        return 0

    lax.fori_loop(1, MEMBERS, greet, 0)
    for step in range(1, GROUPS):
        pl.semaphore_signal(
            barrier, inc=1, device_id=((grp + step) % GROUPS, dev), device_id_type=MESH
        )
    small_copies[0].wait()
    small_copies[1].wait()
    band[...] = make_band(dev, taps_ref[...])
    pl.semaphore_wait(barrier, MEMBERS - 1 + GROUPS - 1)

    def samples_to(to):
        return pltpu.make_async_remote_copy(
            src_ref=send.at[to], dst_ref=recv.at[dev], send_sem=send_sem.at[to],
            recv_sem=recv_sem.at[dev], device_id=(grp, to), device_id_type=MESH,
        )

    def decimate(pair, _):
        results = []
        for index in range(2):
            offset = (pair * 2 + index) * 7 % 16
            raw_copy(offset).wait()
            to_chip = chip_at(offset)
            result = filtered(band, raw.at[to_chip]).astype(BF16)
            halves = jnp.dot(basis[...], result, preferred_element_type=F32)
            results.append((to_chip, (halves[:RANK] + halves[RANK:]).astype(BF16)))
        @pl.when(pair % 2 == 1)
        def _():
            base_copy((zc + pair // 2) % 4).start()

        for to_chip, result in results:
            for half in range(2):
                send[to_chip * 2 + half] = result[:, half * CH : (half + 1) * CH]
                to = to_chip * 2 + half

                @pl.when(to != dev)
                def _():
                    samples_to(to).start()

        return 0

    lax.fori_loop(0, 8, decimate, 0)
    for copy in lag_copies:
        copy.start()
    recv[dev] = send[dev]
    for step in range(1, GROUPS):
        pl.semaphore_signal(
            plane_sem, inc=1, device_id=((grp + step) % GROUPS, dev), device_id_type=MESH
        )
    acc[...] = jnp.zeros_like(acc)

    def transform(step, _):
        plane = (zc + step) % 4
        first = plane * 8
        for index in range(8):
            source = first + index

            @pl.when(source != dev)
            def _():
                pltpu.make_async_remote_copy(
                    src_ref=send.at[source], dst_ref=recv.at[source],
                    send_sem=send_sem.at[source], recv_sem=recv_sem.at[source],
                    device_id=(grp, source), device_id_type=MESH,
                ).wait_recv()

        base_copy(plane).wait()
        samples = recv[pl.ds(first, 8)].reshape(8 * RANK, CH)
        acc[...] += lax.dot_general(
            samples, base[plane], (((0,), (0,)), ((), ())), preferred_element_type=F32
        )
        return 0

    lax.fori_loop(0, 4, transform, 0)

    real, imag = acc[:, :NF], acc[:, NF:]
    power = real * real + imag * imag
    level = jnp.mean(power, axis=1, keepdims=True)
    scale = lax.rsqrt(power + level + 1e-06)
    outs, ins = (out0, out1, out2, out3), (in0, in1, in2, late_ref)
    crosses, lags = (cross0, cross1, cross2), (lag0, lag1, lag2)
    gathered = (gathered0, gathered1, gathered2, gathered3)
    gathered = gathered + (gathered4, gathered5, gathered6, gathered7)
    pl.semaphore_wait(plane_sem, GROUPS - 1)
    for piece in range(PIECES):
        line, place = line_and_place(me, piece % 3)
        bins = slice(piece * PIECE, (piece + 1) * PIECE)
        factor = scale[:, bins]
        parts = (acc[:, bins] * factor, acc[:, NF + piece * PIECE : NF + (piece + 1) * PIECE] * factor)
        gathered[piece][place] = jnp.concatenate(
            [half.reshape(16, BLK, PIECE) for half in parts], axis=1
        ).astype(BF16)
        for step in (1, 3, 2):
            to = device_of(line, (place + step) % 4, piece % 3)
            pltpu.make_async_remote_copy(
                src_ref=gathered[piece].at[place], dst_ref=gathered[piece].at[place],
                send_sem=line_sem.at[piece], recv_sem=gather_sem.at[piece],
                device_id=(to // MEMBERS, to % MEMBERS), device_id_type=MESH,
            ).start()

    def select(piece, to, out):
        axis = piece % 3
        for place in range(4):
            out[place] = gathered[piece][place, plan[4 * axis + place, to]]

    def emit(piece, part):
        axis, index = piece % 3, piece - CUTS[part]
        line, place = line_and_place(me, axis)
        first, second = line // 8, line // 2 % 4

        def one(step, _):
            offset = step * 11 % 32
            to_line = (first + turned(offset // 8)) % 4 * 8 + (second + turned(offset // 2 % 4)) % 4 * 2
            to = device_of(to_line + (core + offset) % 2, place, axis)
            select(piece, to, outs[part].at[index, step])
            pltpu.make_async_remote_copy(
                src_ref=outs[part].at[index, step], dst_ref=ins[part].at[index, pl.ds(line * 4, 4)],
                send_sem=out_sem.at[part], recv_sem=in_sem.at[part],
                device_id=(to // MEMBERS, to % MEMBERS), device_id_type=MESH,
            ).start()
            return 0

        lax.fori_loop(1, MEMBERS, one, 0)
        select(piece, me, outs[part].at[index, 0])
        return pltpu.make_async_copy(
            outs[part].at[index, 0], ins[part].at[index, pl.ds(line * 4, 4)], own_sem.at[piece]
        )

    for copy in small_copies[2:]:
        copy.wait()
    tile_rows = [stack_rows([tiles_ref[side : side + 1, :]], 40, 0) for side in range(2)]
    owner_rows = stack_rows([owner_ref[...].reshape(1, -1)], 40, -1)
    make_plan(me, *tile_rows, owner_rows, plan_vector)
    plan_copy = pltpu.make_async_copy(plan_vector, plan, plan_sem)
    plan_copy.start()
    plan_out = pltpu.make_async_copy(plan_vector, plan_out_ref, plan_out_sem)
    plan_out.start()
    plan_copy.wait()
    own_copies = []
    for part in range(EARLY + 1):
        for piece in range(CUTS[part], CUTS[part + 1]):
            others = gathered[piece].at[pl.ds(0, 3)]
            pltpu.make_async_copy(others, others, gather_sem.at[piece]).wait()
            own_copies.append(emit(piece, part))
            own_copies[piece].start()

    def drain(step, _):
        samples_to((dev + step) % MEMBERS).wait_send()
        return 0

    lax.fori_loop(1, MEMBERS, drain, 0)
    def await_part(part):
        for piece in range(CUTS[part], CUTS[part + 1]):
            own_copies[piece].wait()
        others = ins[part].at[:, pl.ds(0, DEVICES - 4)]
        pltpu.make_async_copy(others, others, in_sem.at[part]).wait()

    def tiles_of(part):
        def one(group, _):
            for tile in range(TILES):
                cross_spectra(ins[part], plan, crosses[part], group * TILES + tile, tile, axes_of(part))
            lagged = jnp.dot(crosses[part][...], lags[part][...], preferred_element_type=F32)
            lagged = lagged.reshape(TILES, BLK, BLK, NLAG)
            rows = pl.ds(group * TILES, TILES)
            if part > 0:
                lagged = lagged + first_sums[rows]
            if part < EARLY - 1:
                first_sums[rows] = lagged
            else:
                partial[rows] = lagged.astype(BF16)
                pltpu.make_async_copy(partial.at[rows], partial_ref.at[rows], partial_sem).start()
            return 0

        lax.fori_loop(0, SLOTS // TILES, one, 0)

    for copy in lag_copies:
        copy.wait()
    for part in range(EARLY):
        await_part(part)
        tiles_of(part)
    pltpu.make_async_copy(partial, partial_ref, partial_sem).wait()
    plan_out.wait()
    for part in range(EARLY + 1):
        sent = outs[part].at[:, pl.ds(0, MEMBERS - 1)]
        pltpu.make_async_copy(sent, sent, out_sem.at[part]).wait()
    await_part(EARLY)
    for piece in range(PIECES):
        others = gathered[piece].at[pl.ds(0, 3)]
        pltpu.make_async_copy(others, others, line_sem.at[piece]).wait()


def late_kernel(
    plan_ref, late_ref, partial_ref, lag_ref, out_ref,
    late, lag, partial, total, cross, late_sem, lag_sem, in_sem, out_sem,
):
    count = plan_ref[15, 0]
    pieces = 4
    size = DEVICES // pieces
    late_copies = [
        pltpu.make_async_copy(
            late_ref.at[:, pl.ds(size * index, size)], late.at[:, pl.ds(size * index, size)],
            late_sem.at[index],
        )
        for index in range(pieces)
    ]
    lag_copy = pltpu.make_async_copy(lag_ref, lag, lag_sem)

    def rows(group):
        return pl.ds(group * TILES, TILES)

    def load(group):
        return pltpu.make_async_copy(
            partial_ref.at[rows(group)], partial.at[rows(group)], in_sem.at[group]
        )

    for copy in late_copies:
        copy.start()
    lag_copy.start()

    def fetch(group, _):
        load(group).start()
        return 0

    lax.fori_loop(0, SLOTS // TILES, fetch, 0)
    for copy in late_copies:
        copy.wait()
    lag_copy.wait()

    def one(group, _):
        load(group).wait()

        @pl.when(group * TILES < count)
        def _():
            for tile in range(TILES):
                cross_spectra(late, plan_ref, cross, group * TILES + tile, tile, axes_of(EARLY))
            lagged = jnp.dot(cross[...], lag[...], preferred_element_type=F32)
            lagged = lagged + partial[rows(group)].astype(F32).reshape(lagged.shape)
            index = lax.broadcasted_iota(jnp.int32, lagged.shape, 0) // 64 + group * TILES
            total[rows(group)] = jnp.where(index < count, lagged, 0.0).reshape(TILES, BLK, BLK, NLAG)

        @pl.when(group * TILES >= count)
        def _():
            total[rows(group)] = jnp.zeros((TILES, BLK, BLK, NLAG), F32)

        pltpu.make_async_copy(total.at[rows(group)], out_ref.at[rows(group)], out_sem).start()
        return 0

    lax.fori_loop(0, SLOTS // TILES, one, 0)
    pltpu.make_async_copy(total, out_ref, out_sem).wait()


def per_device(strain, taps, tiles, owner):
    hbm = pl.BlockSpec(memory_space=pl.ANY)
    lag = lag_table()
    basis, rows = base_tables()
    lags = [
        lag.reshape(2, PIECES, PIECE, NLAG)[:, CUTS[part] : CUTS[part + 1]].reshape(-1, NLAG)
        for part in range(EARLY + 1)
    ]
    groups = SLOTS // TILES
    late, partial, plan = pl.pallas_call(
        exchange_kernel,
        out_shape=(
            jax.ShapeDtypeStruct((COUNTS[EARLY], DEVICES, 2 * BLK, PIECE), BF16),
            jax.ShapeDtypeStruct((SLOTS, BLK, BLK, NLAG), BF16),
            jax.ShapeDtypeStruct((16, 128), jnp.int32),
        ),
        in_specs=[hbm] * (6 + EARLY),
        out_specs=(hbm, hbm, hbm),
        scratch_shapes=[
            pltpu.VMEM((16, 960, 256), BF16),
            pltpu.VMEM((1, NTAP), BF16),
            pltpu.VMEM((2, 4160), jnp.int32),
            pltpu.VMEM((4160,), jnp.int32),
            pltpu.VMEM((2 * RANK, EXT), BF16),
            pltpu.VMEM((4, 8 * RANK, 2 * NF), BF16),
            *[pltpu.VMEM((2 * count * PIECE, NLAG), BF16) for count in COUNTS[:EARLY]],
            pltpu.VMEM((EXT, 960), BF16),
            pltpu.VMEM((16, 128), jnp.int32),
            pltpu.SMEM((16, 128), jnp.int32),
            pltpu.VMEM((MEMBERS, RANK, CH), BF16),
            pltpu.VMEM((MEMBERS, RANK, CH), BF16),
            pltpu.VMEM((CH, 2 * NF), F32),
            *[pltpu.VMEM((4, 16, 2 * BLK, PIECE), BF16) for _ in range(PIECES)],
            *[pltpu.VMEM((count, MEMBERS, 4, 2 * BLK, PIECE), BF16) for count in COUNTS],
            *[pltpu.VMEM((count, DEVICES, 2 * BLK, PIECE), BF16) for count in COUNTS[:EARLY]],
            *[pltpu.VMEM((TILES * 64, 2 * count * PIECE), BF16) for count in COUNTS[:EARLY]],
            pltpu.VMEM((SLOTS, BLK, BLK, NLAG), F32),
            pltpu.VMEM((SLOTS, BLK, BLK, NLAG), BF16),
            pltpu.SemaphoreType.DMA((16,)),
            pltpu.SemaphoreType.DMA((4,)),
            pltpu.SemaphoreType.DMA((4,)),
            pltpu.SemaphoreType.DMA((EARLY,)),
            pltpu.SemaphoreType.DMA,
            pltpu.SemaphoreType.DMA,
            pltpu.SemaphoreType.DMA((MEMBERS,)),
            pltpu.SemaphoreType.DMA((MEMBERS,)),
            pltpu.SemaphoreType.DMA((PIECES,)),
            pltpu.SemaphoreType.DMA((PIECES,)),
            pltpu.SemaphoreType.DMA((EARLY + 1,)),
            pltpu.SemaphoreType.DMA((EARLY + 1,)),
            pltpu.SemaphoreType.DMA((PIECES,)),
            pltpu.SemaphoreType.DMA,
            pltpu.SemaphoreType.REGULAR,
        ],
        compiler_params=pltpu.CompilerParams(
            collective_id=0, has_side_effects=True, vmem_limit_bytes=60 * 2**20
        ),
    )(
        strain.T, taps[None, :], tiles.T, owner, jnp.asarray(basis), jnp.asarray(rows.reshape(4, 8 * RANK, 2 * NF)),
        *[jnp.asarray(part) for part in lags[:EARLY]],
    )

    return pl.pallas_call(
        late_kernel,
        out_shape=jax.ShapeDtypeStruct((SLOTS, BLK, BLK, NLAG), F32),
        in_specs=[pl.BlockSpec(memory_space=pltpu.SMEM), hbm, hbm, hbm],
        out_specs=hbm,
        scratch_shapes=[
            pltpu.VMEM((COUNTS[EARLY], DEVICES, 2 * BLK, PIECE), BF16),
            pltpu.VMEM((2 * COUNTS[EARLY] * PIECE, NLAG), BF16),
            pltpu.VMEM((SLOTS, BLK, BLK, NLAG), BF16),
            pltpu.VMEM((SLOTS, BLK, BLK, NLAG), F32),
            pltpu.VMEM((TILES * 64, 2 * COUNTS[EARLY] * PIECE), BF16),
            pltpu.SemaphoreType.DMA((4,)),
            pltpu.SemaphoreType.DMA,
            pltpu.SemaphoreType.DMA((groups,)),
            pltpu.SemaphoreType.DMA,
        ],
        compiler_params=pltpu.CompilerParams(vmem_limit_bytes=60 * 2**20),
    )(plan, late, partial, jnp.asarray(lags[EARLY]))


def solution(mesh):
    return jax.shard_map(
        per_device,
        mesh=mesh,
        in_specs=(P("grp", "dev"), P(), P(), P()),
        out_specs=P(("grp", "dev"), None, None, None),
        check_vma=False,
    )
```

```python
import functools
import math

import jax
import jax.numpy as jnp
import ml_dtypes
import numpy as np
from jax import lax
from jax.experimental import pallas as pl
from jax.experimental.pallas import tpu as pltpu
from jax.sharding import PartitionSpec as P

NT = 6144
NF = 1024
F0 = 32
NLAG = 384
NTAP = 64
DECIM = 5
BLK = 8
MEMBERS = 32
GROUPS = 4
DEVICES = 128
COLS = NT // MEMBERS
EXT = 208
USED = 205
RANK = 96
STRETCHES = ((0, 64), (48, 120), (96, 168), (144, 208))
PARTS = 8
CH = 128
SLOTS = 64
PIECE = 128
PIECES = NF // PIECE
CUTS = (0, 4, 6, 7, 8)
COUNTS = (4, 2, 1, 1)
EARLY = len(COUNTS) - 1
TILES = 4
MESH = pl.DeviceIdType.MESH
F32 = jnp.float32
BF16 = jnp.bfloat16


def trig(phase, factor=1.0):
    angle = np.float32(2.0 * math.pi / NT) * phase.astype(np.float32)
    angle = angle.astype(np.float64)
    return np.cos(angle) * factor, -np.sin(angle) * factor


def base_tables():
    samples = np.arange(USED)
    width = (F0 + NF) / NT
    steps = samples[1:] * (USED - samples[1:]) / 2
    diagonal = ((USED - 1) / 2 - samples) ** 2 * math.cos(2 * math.pi * width)
    _, vectors = np.linalg.eigh(np.diag(diagonal) + np.diag(steps, 1) + np.diag(steps, -1))
    basis = vectors[:, ::-1][:, :RANK].T
    half = basis[:, : USED // 2]
    basis = basis * np.sign(np.take_along_axis(half, np.abs(half).argmax(axis=1)[:, None], axis=1))

    def table(place):
        rows = place * COLS + samples
        angle = 2.0 * math.pi / NT * (rows[:, None] * (F0 + np.arange(NF))[None, :] % NT)
        return np.concatenate([np.cos(angle), -np.sin(angle)], axis=1)

    assert np.abs(basis.T @ (basis @ table(0)) - table(0)).max() < 1e-10
    rows = np.concatenate([basis @ table(place) for place in range(MEMBERS)], axis=0)
    basis = np.pad(basis, ((0, 0), (0, EXT - USED)))
    high = basis.astype(ml_dtypes.bfloat16)
    low = (basis - high.astype(np.float64)).astype(ml_dtypes.bfloat16)
    return np.concatenate([high, low], axis=0), rows.astype(ml_dtypes.bfloat16)


def lag_table():
    lags = (np.arange(NLAG) - NLAG // 2) % NT
    phase = (F0 + np.arange(NF))[:, None] * lags[None, :] % NT
    real, imag = trig(phase, 1.0 / math.sqrt(NF))
    return np.concatenate([real, imag], axis=0).astype(ml_dtypes.bfloat16)


def nt_dot(a, b):
    return lax.dot_general(a, b, (((1,), (1,)), ((), ())), preferred_element_type=F32)


def stack_rows(pieces, rows, fill):
    width = sum(piece.shape[1] for piece in pieces)
    extra = jnp.full((1, rows * 128 - width), fill, jnp.int32)
    line = jnp.concatenate([*pieces, extra], axis=1)
    return jnp.concatenate(
        [line[:, index * 128 : (index + 1) * 128] for index in range(rows)], axis=0
    )


def make_band(member, taps):
    tap = lax.broadcasted_iota(jnp.int32, (NTAP, 1024), 0)
    lane = lax.broadcasted_iota(jnp.int32, (NTAP, 1024), 1)
    place = (lane == (1024 - tap) % 1024).astype(F32).astype(BF16)
    taps = jnp.broadcast_to(taps.astype(F32), (8, NTAP)).astype(BF16)
    line = jnp.dot(taps, place, preferred_element_type=F32)
    first_rows = pltpu.roll(line, 0, 1, stride=DECIM, stride_axis=0)
    band = jnp.concatenate(
        [pltpu.roll(first_rows, 8 * DECIM * index, 1) for index in range(EXT // 8)], axis=0
    )
    row = lax.broadcasted_iota(jnp.int32, (EXT, 1024), 0)
    limit = jnp.where(member == MEMBERS - 1, COLS, USED)
    return jnp.where(row < limit, band, 0.0)[:, :960].astype(BF16)


def filtered(band, raw):
    count = raw.shape[0]
    sums = [
        jnp.dot(
            band[low:high, 256 * index : min(256 * (index + 1), count)],
            raw[256 * index : min(256 * (index + 1), count)],
            preferred_element_type=F32,
        )
        for index, (low, high) in enumerate(STRETCHES)
    ]
    pieces = []
    done = 0
    for index, (low, high) in enumerate(STRETCHES):
        end = STRETCHES[index + 1][0] if index + 1 < len(STRETCHES) else high
        pieces.append(sums[index][done - low : end - low])
        if end < high:
            after = STRETCHES[index + 1][0]
            pieces.append(sums[index][end - low :] + sums[index + 1][: high - after])
        done = high
    return jnp.concatenate(pieces, axis=0)


def coordinates(device):
    return device // 8 % 4, device // 2 % 4, device // 32, device % 2


def axis_of(turn, core):
    return (turn + 2 * core) % 3


def line_and_place(device, axis):
    z, x, y, c = coordinates(device)
    first, second = jnp.where(axis == 2, z, y), jnp.where(axis == 1, z, x)
    return first * 8 + second * 2 + c, jnp.where(axis == 0, z, jnp.where(axis == 1, x, y))


def device_of(line, place, axis):
    first, second, c = line // 8, line // 2 % 4, line % 2
    z = jnp.where(axis == 0, place, jnp.where(axis == 1, second, first))
    x, y = jnp.where(axis == 1, place, second), jnp.where(axis == 2, place, first)
    return y * 32 + z * 8 + x * 2 + c


def make_plan(me, src, dst, own, plan_ref):
    rows = src.shape[0]
    mine = own == me
    lane_a = lax.broadcasted_iota(jnp.int32, (128, 128), 0)
    lane = lax.broadcasted_iota(jnp.int32, (rows, 128), 1)
    row = lax.broadcasted_iota(jnp.int32, (rows, 128), 0)
    flags = jnp.where(mine, 1, 0)
    within = flags
    for shift in (1, 2, 4, 8, 16, 32, 64):
        within = within + jnp.where(lane >= shift, pltpu.roll(within, shift, 1), 0)
    totals = jnp.broadcast_to(jnp.sum(flags, axis=1, keepdims=True), (rows, 128))
    before = totals
    for shift in (1, 2, 4, 8, 16, 32):
        before = before + jnp.where(row >= shift, pltpu.roll(before, shift, 0), 0)
    slot = jnp.where(mine, within - flags + before - totals, -1)
    src_dev, dst_dev = src // 16, dst // 16

    first = jnp.zeros((SLOTS, 128), jnp.int32)
    second = jnp.zeros((SLOTS, 128), jnp.int32)
    for index in range(rows):
        hit = slot[index : index + 1, :] == lane_a[:SLOTS]
        first = first + jnp.where(hit, src_dev[index : index + 1, :], 0)
        second = second + jnp.where(hit, dst_dev[index : index + 1, :], 0)
    ends = jnp.sum(jnp.concatenate([first, second], axis=0).T, axis=0, keepdims=True)
    lines = []
    for turn in range(3):
        line, place = line_and_place(ends, axis_of(turn, ends % 2))
        lines.append(line * 4 + place)
    count = jnp.sum(flags, axis=(0, 1), keepdims=True)
    lines.append(jnp.broadcast_to(count, (1, 128)))
    plan_ref[12:16, :] = jnp.concatenate(lines, axis=0)

    z, x, y, _ = coordinates(me)

    def wanted(entry, _):
        axis, place = entry // 4, entry % 4
        source = jnp.where(
            axis == 0, me + (place - z) * 8, jnp.where(axis == 1, me + (place - x) * 2, me + (place - y) * 32)
        )
        local = jnp.where(src_dev == source, src % 16, 0) + jnp.where(dst_dev == source, dst % 16, 0)
        blocks = jnp.zeros((128, 128), jnp.int32)
        for index in range(rows):
            hit = own[index : index + 1, :] == lane_a
            blocks = blocks + jnp.where(hit, local[index : index + 1, :], 0)
        plan_ref[pl.ds(entry, 1), :] = jnp.sum(blocks.T, axis=0, keepdims=True)
        return 0

    lax.fori_loop(0, 12, wanted, 0)


def cross_spectra(into, plan, cross, slot, tile, turns):
    width = len(turns) * PIECE
    for index, turn in enumerate(turns):
        a = into[index, plan[12 + turn, slot]].astype(F32)
        b = into[index, plan[12 + turn, SLOTS + slot]].astype(F32)
        ar, ai, br, bi = a[:BLK], a[BLK:], b[:BLK], b[BLK:]
        left = index * PIECE
        for pair in range(BLK // 2):
            reals, imags = [], []
            for i in (2 * pair, 2 * pair + 1):
                xr, xi = ar[i : i + 1, :], ai[i : i + 1, :]
                reals.append(xr * br + xi * bi)
                imags.append(xi * br - xr * bi)
            at = tile * 64 + pair * 16
            cross[at : at + 16, left : left + PIECE] = jnp.concatenate(reals, axis=0).astype(BF16)
            cross[at : at + 16, width + left : width + left + PIECE] = jnp.concatenate(
                imags, axis=0
            ).astype(BF16)


def turns_of(part):
    return [piece % 3 for piece in range(CUTS[part], CUTS[part + 1])]


def exchange_kernel(
    strain_ref, taps_hbm, tiles_hbm, owner_hbm, basis_hbm, base_ref, lag0_ref, lag1_ref, lag2_ref,
    late_ref, partial_ref, plan_out_ref,
    raw, taps_ref, tiles_ref, owner_ref, basis, base, lag0, lag1, lag2, band, plan_vector, plan, send, recv, acc,
    gathered0, gathered1, gathered2, gathered3, gathered4, gathered5, gathered6, gathered7,
    out0, out1, out2, out3, in0, in1, in2, cross0, cross1, cross2, first_sums, partial,
    raw_sem, small_sem, base_sem, lag_sem, plan_sem, plan_out_sem, send_sem, recv_sem,
    line_sem, gather_sem, out_sem, in_sem, own_sem, partial_sem, plane_sem,
):
    grp, dev = lax.axis_index("grp"), lax.axis_index("dev")
    me = grp * MEMBERS + dev
    chip, core = dev // 2, dev % 2
    zc, xc = chip // 4, chip % 4

    def turned(offset):
        return jnp.where(core == 0, offset, (4 - offset) % 4)

    def at(z, x, c):
        return z % 4 * 8 + x % 4 * 2 + c

    def chip_at(offset):
        return (zc + turned(offset // 4)) % 4 * 4 + (xc + turned(offset % 4)) % 4

    def raw_copy(offset):
        to_chip = chip_at(offset)
        return pltpu.make_async_copy(
            strain_ref.at[:, pl.ds(pl.multiple_of(to_chip * 256, 256), 256)],
            raw.at[to_chip], raw_sem.at[to_chip],
        )

    def fetch(step, _):
        raw_copy(step * 7 % 16).start()
        return 0

    small = ((taps_hbm, taps_ref), (basis_hbm, basis), (tiles_hbm, tiles_ref))
    small = small + ((owner_hbm, owner_ref),)
    small_copies = [
        pltpu.make_async_copy(source, into, small_sem.at[index])
        for index, (source, into) in enumerate(small)
    ]
    for copy in small_copies:
        copy.start()
    lax.fori_loop(0, 16, fetch, 0)
    def base_copy(plane):
        return pltpu.make_async_copy(base_ref.at[plane], base.at[plane], base_sem.at[plane])

    lag_copies = [
        pltpu.make_async_copy(lag0_ref, lag0, lag_sem.at[0]),
        pltpu.make_async_copy(lag1_ref, lag1, lag_sem.at[1]),
        pltpu.make_async_copy(lag2_ref, lag2, lag_sem.at[2]),
    ]

    barrier = pltpu.get_barrier_semaphore()

    def greet(step, _):
        pl.semaphore_signal(
            barrier, inc=1, device_id=(grp, (dev + step) % MEMBERS), device_id_type=MESH
        )
        return 0

    lax.fori_loop(1, MEMBERS, greet, 0)
    for step in range(1, GROUPS):
        pl.semaphore_signal(
            barrier, inc=1, device_id=((grp + step) % GROUPS, dev), device_id_type=MESH
        )
    small_copies[0].wait()
    small_copies[1].wait()
    band[...] = make_band(dev, taps_ref[...])
    pl.semaphore_wait(barrier, MEMBERS - 1 + GROUPS - 1)

    def samples_to(to):
        return pltpu.make_async_remote_copy(
            src_ref=send.at[to], dst_ref=recv.at[dev], send_sem=send_sem.at[to],
            recv_sem=recv_sem.at[dev], device_id=(grp, to), device_id_type=MESH,
        )

    def decimate(pair, _):
        results = []
        for index in range(2):
            offset = (pair * 2 + index) * 7 % 16
            raw_copy(offset).wait()
            to_chip = chip_at(offset)
            result = filtered(band, raw.at[to_chip]).astype(BF16)
            halves = jnp.dot(basis[...], result, preferred_element_type=F32)
            results.append((to_chip, (halves[:RANK] + halves[RANK:]).astype(BF16)))
        @pl.when(pair % 2 == 1)
        def _():
            base_copy((zc + pair // 2) % 4).start()

        for to_chip, result in results:
            for half in range(2):
                send[to_chip * 2 + half] = result[:, half * CH : (half + 1) * CH]
                to = to_chip * 2 + half

                @pl.when(to != dev)
                def _():
                    samples_to(to).start()

        return 0

    lax.fori_loop(0, 8, decimate, 0)
    for copy in lag_copies:
        copy.start()
    recv[dev] = send[dev]
    for step in range(1, GROUPS):
        pl.semaphore_signal(
            plane_sem, inc=1, device_id=((grp + step) % GROUPS, dev), device_id_type=MESH
        )
    acc[...] = jnp.zeros_like(acc)

    def transform(step, _):
        plane = (zc + step) % 4
        first = plane * 8
        for index in range(8):
            source = first + index

            @pl.when(source != dev)
            def _():
                pltpu.make_async_remote_copy(
                    src_ref=send.at[source], dst_ref=recv.at[source],
                    send_sem=send_sem.at[source], recv_sem=recv_sem.at[source],
                    device_id=(grp, source), device_id_type=MESH,
                ).wait_recv()

        base_copy(plane).wait()
        samples = recv[pl.ds(first, 8)].reshape(8 * RANK, CH)
        acc[...] += lax.dot_general(
            samples, base[plane], (((0,), (0,)), ((), ())), preferred_element_type=F32
        )
        return 0

    lax.fori_loop(0, 4, transform, 0)

    real, imag = acc[:, :NF], acc[:, NF:]
    power = real * real + imag * imag
    level = jnp.mean(power, axis=1, keepdims=True)
    scale = lax.rsqrt(power + level + 1e-06)
    outs, ins = (out0, out1, out2, out3), (in0, in1, in2, late_ref)
    crosses, lags = (cross0, cross1, cross2), (lag0, lag1, lag2)
    gathered = (gathered0, gathered1, gathered2, gathered3)
    gathered = gathered + (gathered4, gathered5, gathered6, gathered7)
    pl.semaphore_wait(plane_sem, GROUPS - 1)
    for piece in range(PIECES):
        axis = axis_of(piece % 3, core)
        line, place = line_and_place(me, axis)
        bins = slice(piece * PIECE, (piece + 1) * PIECE)
        factor = scale[:, bins]
        parts = (acc[:, bins] * factor, acc[:, NF + piece * PIECE : NF + (piece + 1) * PIECE] * factor)
        gathered[piece][place] = jnp.concatenate(
            [half.reshape(16, BLK, PIECE) for half in parts], axis=1
        ).astype(BF16)
        for step in (1, 3, 2):
            to = device_of(line, (place + step) % 4, axis)
            pltpu.make_async_remote_copy(
                src_ref=gathered[piece].at[place], dst_ref=gathered[piece].at[place],
                send_sem=line_sem.at[piece], recv_sem=gather_sem.at[piece],
                device_id=(to // MEMBERS, to % MEMBERS), device_id_type=MESH,
            ).start()

    def select(piece, to, out):
        axis = axis_of(piece % 3, core)
        for place in range(4):
            out[place] = gathered[piece][place, plan[4 * axis + place, to]]

    def emit(piece, part):
        axis, index = axis_of(piece % 3, core), piece - CUTS[part]
        line, place = line_and_place(me, axis)
        first, second = line // 8, line // 2 % 4

        def one(step, _):
            offset = step * 11 % 32
            to_line = (first + turned(offset // 8)) % 4 * 8 + (second + turned(offset // 2 % 4)) % 4 * 2
            to = device_of(to_line + (core + offset) % 2, place, axis)
            select(piece, to, outs[part].at[index, step])
            pltpu.make_async_remote_copy(
                src_ref=outs[part].at[index, step], dst_ref=ins[part].at[index, pl.ds(line * 4, 4)],
                send_sem=out_sem.at[part], recv_sem=in_sem.at[part],
                device_id=(to // MEMBERS, to % MEMBERS), device_id_type=MESH,
            ).start()
            return 0

        lax.fori_loop(1, MEMBERS, one, 0)
        select(piece, me, outs[part].at[index, 0])
        return pltpu.make_async_copy(
            outs[part].at[index, 0], ins[part].at[index, pl.ds(line * 4, 4)], own_sem.at[piece]
        )

    for copy in small_copies[2:]:
        copy.wait()
    tile_rows = [stack_rows([tiles_ref[side : side + 1, :]], 40, 0) for side in range(2)]
    owner_rows = stack_rows([owner_ref[...].reshape(1, -1)], 40, -1)
    make_plan(me, *tile_rows, owner_rows, plan_vector)
    plan_copy = pltpu.make_async_copy(plan_vector, plan, plan_sem)
    plan_copy.start()
    plan_out = pltpu.make_async_copy(plan_vector, plan_out_ref, plan_out_sem)
    plan_out.start()
    plan_copy.wait()
    own_copies = []
    for part in range(EARLY + 1):
        for piece in range(CUTS[part], CUTS[part + 1]):
            others = gathered[piece].at[pl.ds(0, 3)]
            pltpu.make_async_copy(others, others, gather_sem.at[piece]).wait()
            own_copies.append(emit(piece, part))
            own_copies[piece].start()

    def drain(step, _):
        samples_to((dev + step) % MEMBERS).wait_send()
        return 0

    lax.fori_loop(1, MEMBERS, drain, 0)
    def await_part(part):
        for piece in range(CUTS[part], CUTS[part + 1]):
            own_copies[piece].wait()
        others = ins[part].at[:, pl.ds(0, DEVICES - 4)]
        pltpu.make_async_copy(others, others, in_sem.at[part]).wait()

    def tiles_of(part):
        def one(group, _):
            for tile in range(TILES):
                cross_spectra(ins[part], plan, crosses[part], group * TILES + tile, tile, turns_of(part))
            lagged = jnp.dot(crosses[part][...], lags[part][...], preferred_element_type=F32)
            lagged = lagged.reshape(TILES, BLK, BLK, NLAG)
            rows = pl.ds(group * TILES, TILES)
            if part > 0:
                lagged = lagged + first_sums[rows]
            if part < EARLY - 1:
                first_sums[rows] = lagged
            else:
                partial[rows] = lagged.astype(BF16)
                pltpu.make_async_copy(partial.at[rows], partial_ref.at[rows], partial_sem).start()
            return 0

        lax.fori_loop(0, SLOTS // TILES, one, 0)

    for copy in lag_copies:
        copy.wait()
    for part in range(EARLY):
        await_part(part)
        tiles_of(part)
    pltpu.make_async_copy(partial, partial_ref, partial_sem).wait()
    plan_out.wait()
    for part in range(EARLY + 1):
        sent = outs[part].at[:, pl.ds(0, MEMBERS - 1)]
        pltpu.make_async_copy(sent, sent, out_sem.at[part]).wait()
    await_part(EARLY)
    for piece in range(PIECES):
        others = gathered[piece].at[pl.ds(0, 3)]
        pltpu.make_async_copy(others, others, line_sem.at[piece]).wait()


def late_kernel(
    plan_ref, late_ref, partial_ref, lag_ref, out_ref,
    late, lag, partial, total, cross, late_sem, lag_sem, in_sem, out_sem,
):
    count = plan_ref[15, 0]
    pieces = 4
    size = DEVICES // pieces
    late_copies = [
        pltpu.make_async_copy(
            late_ref.at[:, pl.ds(size * index, size)], late.at[:, pl.ds(size * index, size)],
            late_sem.at[index],
        )
        for index in range(pieces)
    ]
    lag_copy = pltpu.make_async_copy(lag_ref, lag, lag_sem)

    def rows(group):
        return pl.ds(group * TILES, TILES)

    def load(group):
        return pltpu.make_async_copy(
            partial_ref.at[rows(group)], partial.at[rows(group)], in_sem.at[group]
        )

    for copy in late_copies:
        copy.start()
    lag_copy.start()

    def fetch(group, _):
        load(group).start()
        return 0

    lax.fori_loop(0, SLOTS // TILES, fetch, 0)
    for copy in late_copies:
        copy.wait()
    lag_copy.wait()

    def one(group, _):
        load(group).wait()

        @pl.when(group * TILES < count)
        def _():
            for tile in range(TILES):
                cross_spectra(late, plan_ref, cross, group * TILES + tile, tile, turns_of(EARLY))
            lagged = jnp.dot(cross[...], lag[...], preferred_element_type=F32)
            lagged = lagged + partial[rows(group)].astype(F32).reshape(lagged.shape)
            index = lax.broadcasted_iota(jnp.int32, lagged.shape, 0) // 64 + group * TILES
            total[rows(group)] = jnp.where(index < count, lagged, 0.0).reshape(TILES, BLK, BLK, NLAG)

        @pl.when(group * TILES >= count)
        def _():
            total[rows(group)] = jnp.zeros((TILES, BLK, BLK, NLAG), F32)

        pltpu.make_async_copy(total.at[rows(group)], out_ref.at[rows(group)], out_sem).start()
        return 0

    lax.fori_loop(0, SLOTS // TILES, one, 0)
    pltpu.make_async_copy(total, out_ref, out_sem).wait()


def per_device(strain, taps, tiles, owner):
    hbm = pl.BlockSpec(memory_space=pl.ANY)
    lag = lag_table()
    basis, rows = base_tables()
    lags = [
        lag.reshape(2, PIECES, PIECE, NLAG)[:, CUTS[part] : CUTS[part + 1]].reshape(-1, NLAG)
        for part in range(EARLY + 1)
    ]
    groups = SLOTS // TILES
    late, partial, plan = pl.pallas_call(
        exchange_kernel,
        out_shape=(
            jax.ShapeDtypeStruct((COUNTS[EARLY], DEVICES, 2 * BLK, PIECE), BF16),
            jax.ShapeDtypeStruct((SLOTS, BLK, BLK, NLAG), BF16),
            jax.ShapeDtypeStruct((16, 128), jnp.int32),
        ),
        in_specs=[hbm] * (6 + EARLY),
        out_specs=(hbm, hbm, hbm),
        scratch_shapes=[
            pltpu.VMEM((16, 960, 256), BF16),
            pltpu.VMEM((1, NTAP), BF16),
            pltpu.VMEM((2, 4160), jnp.int32),
            pltpu.VMEM((4160,), jnp.int32),
            pltpu.VMEM((2 * RANK, EXT), BF16),
            pltpu.VMEM((4, 8 * RANK, 2 * NF), BF16),
            *[pltpu.VMEM((2 * count * PIECE, NLAG), BF16) for count in COUNTS[:EARLY]],
            pltpu.VMEM((EXT, 960), BF16),
            pltpu.VMEM((16, 128), jnp.int32),
            pltpu.SMEM((16, 128), jnp.int32),
            pltpu.VMEM((MEMBERS, RANK, CH), BF16),
            pltpu.VMEM((MEMBERS, RANK, CH), BF16),
            pltpu.VMEM((CH, 2 * NF), F32),
            *[pltpu.VMEM((4, 16, 2 * BLK, PIECE), BF16) for _ in range(PIECES)],
            *[pltpu.VMEM((count, MEMBERS, 4, 2 * BLK, PIECE), BF16) for count in COUNTS],
            *[pltpu.VMEM((count, DEVICES, 2 * BLK, PIECE), BF16) for count in COUNTS[:EARLY]],
            *[pltpu.VMEM((TILES * 64, 2 * count * PIECE), BF16) for count in COUNTS[:EARLY]],
            pltpu.VMEM((SLOTS, BLK, BLK, NLAG), F32),
            pltpu.VMEM((SLOTS, BLK, BLK, NLAG), BF16),
            pltpu.SemaphoreType.DMA((16,)),
            pltpu.SemaphoreType.DMA((4,)),
            pltpu.SemaphoreType.DMA((4,)),
            pltpu.SemaphoreType.DMA((EARLY,)),
            pltpu.SemaphoreType.DMA,
            pltpu.SemaphoreType.DMA,
            pltpu.SemaphoreType.DMA((MEMBERS,)),
            pltpu.SemaphoreType.DMA((MEMBERS,)),
            pltpu.SemaphoreType.DMA((PIECES,)),
            pltpu.SemaphoreType.DMA((PIECES,)),
            pltpu.SemaphoreType.DMA((EARLY + 1,)),
            pltpu.SemaphoreType.DMA((EARLY + 1,)),
            pltpu.SemaphoreType.DMA((PIECES,)),
            pltpu.SemaphoreType.DMA,
            pltpu.SemaphoreType.REGULAR,
        ],
        compiler_params=pltpu.CompilerParams(
            collective_id=0, has_side_effects=True, vmem_limit_bytes=60 * 2**20
        ),
    )(
        strain.T, taps[None, :], tiles.T, owner, jnp.asarray(basis), jnp.asarray(rows.reshape(4, 8 * RANK, 2 * NF)),
        *[jnp.asarray(part) for part in lags[:EARLY]],
    )

    return pl.pallas_call(
        late_kernel,
        out_shape=jax.ShapeDtypeStruct((SLOTS, BLK, BLK, NLAG), F32),
        in_specs=[pl.BlockSpec(memory_space=pltpu.SMEM), hbm, hbm, hbm],
        out_specs=hbm,
        scratch_shapes=[
            pltpu.VMEM((COUNTS[EARLY], DEVICES, 2 * BLK, PIECE), BF16),
            pltpu.VMEM((2 * COUNTS[EARLY] * PIECE, NLAG), BF16),
            pltpu.VMEM((SLOTS, BLK, BLK, NLAG), BF16),
            pltpu.VMEM((SLOTS, BLK, BLK, NLAG), F32),
            pltpu.VMEM((TILES * 64, 2 * COUNTS[EARLY] * PIECE), BF16),
            pltpu.SemaphoreType.DMA((4,)),
            pltpu.SemaphoreType.DMA,
            pltpu.SemaphoreType.DMA((groups,)),
            pltpu.SemaphoreType.DMA,
        ],
        compiler_params=pltpu.CompilerParams(vmem_limit_bytes=60 * 2**20),
    )(plan, late, partial, jnp.asarray(lags[EARLY]))


def solution(mesh):
    return jax.shard_map(
        per_device,
        mesh=mesh,
        in_specs=(P("grp", "dev"), P(), P(), P()),
        out_specs=P(("grp", "dev"), None, None, None),
        check_vma=False,
    )
```

```python
import functools
import math

import jax
import jax.numpy as jnp
import ml_dtypes
import numpy as np
from jax import lax
from jax.experimental import pallas as pl
from jax.experimental.pallas import tpu as pltpu
from jax.sharding import PartitionSpec as P

NT = 6144
NF = 1024
F0 = 32
NLAG = 384
NTAP = 64
DECIM = 5
BLK = 8
MEMBERS = 32
GROUPS = 4
DEVICES = 128
COLS = NT // MEMBERS
EXT = 208
USED = 205
RANK = 96
STRETCHES = ((0, 64), (48, 120), (96, 168), (144, 208))
PARTS = 8
CH = 128
SLOTS = 64
PIECE = 128
PIECES = NF // PIECE
CUTS = (0, 4, 6, 7, 8)
COUNTS = (4, 2, 1, 1)
EARLY = len(COUNTS) - 1
TILES = 4
MESH = pl.DeviceIdType.MESH
F32 = jnp.float32
BF16 = jnp.bfloat16


def trig(phase, factor=1.0):
    angle = np.float32(2.0 * math.pi / NT) * phase.astype(np.float32)
    angle = angle.astype(np.float64)
    return np.cos(angle) * factor, -np.sin(angle) * factor


def base_tables():
    samples = np.arange(USED)
    width = (F0 + NF) / NT
    steps = samples[1:] * (USED - samples[1:]) / 2
    diagonal = ((USED - 1) / 2 - samples) ** 2 * math.cos(2 * math.pi * width)
    _, vectors = np.linalg.eigh(np.diag(diagonal) + np.diag(steps, 1) + np.diag(steps, -1))
    basis = vectors[:, ::-1][:, :RANK].T
    half = basis[:, : USED // 2]
    basis = basis * np.sign(np.take_along_axis(half, np.abs(half).argmax(axis=1)[:, None], axis=1))

    def table(place):
        rows = place * COLS + samples
        angle = 2.0 * math.pi / NT * (rows[:, None] * (F0 + np.arange(NF))[None, :] % NT)
        return np.concatenate([np.cos(angle), -np.sin(angle)], axis=1)

    assert np.abs(basis.T @ (basis @ table(0)) - table(0)).max() < 1e-10
    rows = np.concatenate([basis @ table(place) for place in range(MEMBERS)], axis=0)
    basis = np.pad(basis, ((0, 0), (0, EXT - USED)))
    high = basis.astype(ml_dtypes.bfloat16)
    low = (basis - high.astype(np.float64)).astype(ml_dtypes.bfloat16)
    return np.concatenate([high, low], axis=0), rows.astype(ml_dtypes.bfloat16)


def lag_table():
    lags = (np.arange(NLAG) - NLAG // 2) % NT
    phase = (F0 + np.arange(NF))[:, None] * lags[None, :] % NT
    real, imag = trig(phase, 1.0 / math.sqrt(NF))
    return np.concatenate([real, imag], axis=0).astype(ml_dtypes.bfloat16)


def nt_dot(a, b):
    return lax.dot_general(a, b, (((1,), (1,)), ((), ())), preferred_element_type=F32)


def stack_rows(pieces, rows, fill):
    width = sum(piece.shape[1] for piece in pieces)
    extra = jnp.full((1, rows * 128 - width), fill, jnp.int32)
    line = jnp.concatenate([*pieces, extra], axis=1)
    return jnp.concatenate(
        [line[:, index * 128 : (index + 1) * 128] for index in range(rows)], axis=0
    )


def make_band(member, taps):
    tap = lax.broadcasted_iota(jnp.int32, (NTAP, 1024), 0)
    lane = lax.broadcasted_iota(jnp.int32, (NTAP, 1024), 1)
    place = (lane == (1024 - tap) % 1024).astype(F32).astype(BF16)
    taps = jnp.broadcast_to(taps.astype(F32), (8, NTAP)).astype(BF16)
    line = jnp.dot(taps, place, preferred_element_type=F32)
    first_rows = pltpu.roll(line, 0, 1, stride=DECIM, stride_axis=0)
    band = jnp.concatenate(
        [pltpu.roll(first_rows, 8 * DECIM * index, 1) for index in range(EXT // 8)], axis=0
    )
    row = lax.broadcasted_iota(jnp.int32, (EXT, 1024), 0)
    limit = jnp.where(member == MEMBERS - 1, COLS, USED)
    return jnp.where(row < limit, band, 0.0)[:, :960].astype(BF16)


def filtered(band, raw):
    count = raw.shape[0]
    sums = [
        jnp.dot(
            band[low:high, 256 * index : min(256 * (index + 1), count)],
            raw[256 * index : min(256 * (index + 1), count)],
            preferred_element_type=F32,
        )
        for index, (low, high) in enumerate(STRETCHES)
    ]
    pieces = []
    done = 0
    for index, (low, high) in enumerate(STRETCHES):
        end = STRETCHES[index + 1][0] if index + 1 < len(STRETCHES) else high
        pieces.append(sums[index][done - low : end - low])
        if end < high:
            after = STRETCHES[index + 1][0]
            pieces.append(sums[index][end - low :] + sums[index + 1][: high - after])
        done = high
    return jnp.concatenate(pieces, axis=0)


def coordinates(device):
    return device // 8 % 4, device // 2 % 4, device // 32, device % 2


def line_and_place(device, axis):
    z, x, y, c = coordinates(device)
    if axis == 0:
        return y * 8 + x * 2 + c, z
    if axis == 1:
        return y * 8 + z * 2 + c, x
    return z * 8 + x * 2 + c, y


def device_of(line, place, axis):
    first, second, c = line // 8, line // 2 % 4, line % 2
    if axis == 0:
        return first * 32 + place * 8 + second * 2 + c
    if axis == 1:
        return first * 32 + second * 8 + place * 2 + c
    return place * 32 + line


def make_plan(me, src, dst, own, plan_ref):
    rows = src.shape[0]
    mine = own == me
    lane_a = lax.broadcasted_iota(jnp.int32, (128, 128), 0)
    lane = lax.broadcasted_iota(jnp.int32, (rows, 128), 1)
    row = lax.broadcasted_iota(jnp.int32, (rows, 128), 0)
    flags = jnp.where(mine, 1, 0)
    within = flags
    for shift in (1, 2, 4, 8, 16, 32, 64):
        within = within + jnp.where(lane >= shift, pltpu.roll(within, shift, 1), 0)
    totals = jnp.broadcast_to(jnp.sum(flags, axis=1, keepdims=True), (rows, 128))
    before = totals
    for shift in (1, 2, 4, 8, 16, 32):
        before = before + jnp.where(row >= shift, pltpu.roll(before, shift, 0), 0)
    slot = jnp.where(mine, within - flags + before - totals, -1)
    src_dev, dst_dev = src // 16, dst // 16

    first = jnp.zeros((SLOTS, 128), jnp.int32)
    second = jnp.zeros((SLOTS, 128), jnp.int32)
    for index in range(rows):
        hit = slot[index : index + 1, :] == lane_a[:SLOTS]
        first = first + jnp.where(hit, src_dev[index : index + 1, :], 0)
        second = second + jnp.where(hit, dst_dev[index : index + 1, :], 0)
    ends = jnp.sum(jnp.concatenate([first, second], axis=0).T, axis=0, keepdims=True)
    lines = []
    for axis in range(3):
        line, place = line_and_place(ends, axis)
        lines.append(line * 4 + place)
    count = jnp.sum(flags, axis=(0, 1), keepdims=True)
    lines.append(jnp.broadcast_to(count, (1, 128)))
    plan_ref[12:16, :] = jnp.concatenate(lines, axis=0)

    z, x, y, _ = coordinates(me)

    def wanted(entry, _):
        axis, place = entry // 4, entry % 4
        source = jnp.where(
            axis == 0, me + (place - z) * 8, jnp.where(axis == 1, me + (place - x) * 2, me + (place - y) * 32)
        )
        local = jnp.where(src_dev == source, src % 16, 0) + jnp.where(dst_dev == source, dst % 16, 0)
        blocks = jnp.zeros((128, 128), jnp.int32)
        for index in range(rows):
            hit = own[index : index + 1, :] == lane_a
            blocks = blocks + jnp.where(hit, local[index : index + 1, :], 0)
        plan_ref[pl.ds(entry, 1), :] = jnp.sum(blocks.T, axis=0, keepdims=True)
        return 0

    lax.fori_loop(0, 12, wanted, 0)


def cross_spectra(into, plan, cross, slot, tile, axes):
    width = len(axes) * PIECE
    for index, axis in enumerate(axes):
        a = into[index, plan[12 + axis, slot]].astype(F32)
        b = into[index, plan[12 + axis, SLOTS + slot]].astype(F32)
        ar, ai, br, bi = a[:BLK], a[BLK:], b[:BLK], b[BLK:]
        left = index * PIECE
        for pair in range(BLK // 2):
            reals, imags = [], []
            for i in (2 * pair, 2 * pair + 1):
                xr, xi = ar[i : i + 1, :], ai[i : i + 1, :]
                reals.append(xr * br + xi * bi)
                imags.append(xi * br - xr * bi)
            at = tile * 64 + pair * 16
            cross[at : at + 16, left : left + PIECE] = jnp.concatenate(reals, axis=0).astype(BF16)
            cross[at : at + 16, width + left : width + left + PIECE] = jnp.concatenate(
                imags, axis=0
            ).astype(BF16)


def axes_of(part):
    return [piece % 3 for piece in range(CUTS[part], CUTS[part + 1])]


def exchange_kernel(
    strain_ref, taps_hbm, tiles_hbm, owner_hbm, basis_hbm, base_ref, lag0_ref, lag1_ref, lag2_ref,
    late_ref, partial_ref, plan_out_ref,
    raw, taps_ref, tiles_ref, owner_ref, basis, base, lag0, lag1, lag2, band, plan_vector, plan, send, recv, acc,
    gathered0, gathered1, gathered2, gathered3, gathered4, gathered5, gathered6, gathered7,
    out0, out1, out2, out3, in0, in1, in2, cross0, cross1, cross2, first_sums, partial,
    raw_sem, small_sem, base_sem, lag_sem, plan_sem, plan_out_sem, send_sem, recv_sem,
    line_sem, gather_sem, out_sem, in_sem, own_sem, partial_sem, plane_sem,
):
    grp, dev = lax.axis_index("grp"), lax.axis_index("dev")
    me = grp * MEMBERS + dev
    chip, core = dev // 2, dev % 2
    zc, xc = chip // 4, chip % 4

    def turned(offset):
        return jnp.where(core == 0, offset, (4 - offset) % 4)

    def at(z, x, c):
        return z % 4 * 8 + x % 4 * 2 + c

    def chip_at(offset):
        return (zc + turned(offset // 4)) % 4 * 4 + (xc + turned(offset % 4)) % 4

    def raw_copy(offset):
        to_chip = chip_at(offset)
        return pltpu.make_async_copy(
            strain_ref.at[:, pl.ds(pl.multiple_of(to_chip * 256, 256), 256)],
            raw.at[to_chip], raw_sem.at[to_chip],
        )

    def fetch(step, _):
        raw_copy(step * 7 % 16).start()
        return 0

    small = ((taps_hbm, taps_ref), (basis_hbm, basis), (tiles_hbm, tiles_ref))
    small = small + ((owner_hbm, owner_ref),)
    small_copies = [
        pltpu.make_async_copy(source, into, small_sem.at[index])
        for index, (source, into) in enumerate(small)
    ]
    for copy in small_copies:
        copy.start()
    lax.fori_loop(0, 16, fetch, 0)
    def base_copy(plane):
        return pltpu.make_async_copy(base_ref.at[plane], base.at[plane], base_sem.at[plane])

    lag_copies = [
        pltpu.make_async_copy(lag0_ref, lag0, lag_sem.at[0]),
        pltpu.make_async_copy(lag1_ref, lag1, lag_sem.at[1]),
        pltpu.make_async_copy(lag2_ref, lag2, lag_sem.at[2]),
    ]

    barrier = pltpu.get_barrier_semaphore()

    def greet(step, _):
        pl.semaphore_signal(
            barrier, inc=1, device_id=(grp, (dev + step) % MEMBERS), device_id_type=MESH
        )
        return 0

    lax.fori_loop(1, MEMBERS, greet, 0)
    for step in range(1, GROUPS):
        pl.semaphore_signal(
            barrier, inc=1, device_id=((grp + step) % GROUPS, dev), device_id_type=MESH
        )
    small_copies[0].wait()
    small_copies[1].wait()
    band[...] = make_band(dev, taps_ref[...])
    pl.semaphore_wait(barrier, MEMBERS - 1 + GROUPS - 1)

    def samples_to(to):
        return pltpu.make_async_remote_copy(
            src_ref=send.at[to], dst_ref=recv.at[dev], send_sem=send_sem.at[to],
            recv_sem=recv_sem.at[dev], device_id=(grp, to), device_id_type=MESH,
        )

    def decimate(pair, _):
        results = []
        for index in range(2):
            offset = (pair * 2 + index) * 7 % 16
            raw_copy(offset).wait()
            to_chip = chip_at(offset)
            result = filtered(band, raw.at[to_chip]).astype(BF16)
            halves = jnp.dot(basis[...], result, preferred_element_type=F32)
            results.append((to_chip, (halves[:RANK] + halves[RANK:]).astype(BF16)))
        @pl.when(pair % 2 == 1)
        def _():
            base_copy((zc + pair // 2) % 4).start()

        for to_chip, result in results:
            for half in range(2):
                send[to_chip * 2 + half] = result[:, half * CH : (half + 1) * CH]
                to = to_chip * 2 + half

                @pl.when(to != dev)
                def _():
                    samples_to(to).start()

        return 0

    lax.fori_loop(0, 8, decimate, 0)
    for copy in lag_copies:
        copy.start()
    recv[dev] = send[dev]
    for step in range(1, GROUPS):
        pl.semaphore_signal(
            plane_sem, inc=1, device_id=((grp + step) % GROUPS, dev), device_id_type=MESH
        )
    acc[...] = jnp.zeros_like(acc)

    def transform(step, _):
        plane = (zc + step) % 4
        first = plane * 8
        for index in range(8):
            source = first + index

            @pl.when(source != dev)
            def _():
                pltpu.make_async_remote_copy(
                    src_ref=send.at[source], dst_ref=recv.at[source],
                    send_sem=send_sem.at[source], recv_sem=recv_sem.at[source],
                    device_id=(grp, source), device_id_type=MESH,
                ).wait_recv()

        base_copy(plane).wait()
        samples = recv[pl.ds(first, 8)].reshape(8 * RANK, CH)
        acc[...] += lax.dot_general(
            samples, base[plane], (((0,), (0,)), ((), ())), preferred_element_type=F32
        )
        return 0

    lax.fori_loop(0, 4, transform, 0)

    real, imag = acc[:, :NF], acc[:, NF:]
    power = real * real + imag * imag
    level = jnp.mean(power, axis=1, keepdims=True)
    scale = lax.rsqrt(power + level + 1e-06)
    outs, ins = (out0, out1, out2, out3), (in0, in1, in2, late_ref)
    crosses, lags = (cross0, cross1, cross2), (lag0, lag1, lag2)
    gathered = (gathered0, gathered1, gathered2, gathered3)
    gathered = gathered + (gathered4, gathered5, gathered6, gathered7)
    pl.semaphore_wait(plane_sem, GROUPS - 1)
    for piece in range(PIECES):
        line, place = line_and_place(me, piece % 3)
        bins = slice(piece * PIECE, (piece + 1) * PIECE)
        factor = scale[:, bins]
        parts = (acc[:, bins] * factor, acc[:, NF + piece * PIECE : NF + (piece + 1) * PIECE] * factor)
        gathered[piece][place] = jnp.concatenate(
            [half.reshape(16, BLK, PIECE) for half in parts], axis=1
        ).astype(BF16)
        for step in (1, 3, 2):
            to = device_of(line, (place + step) % 4, piece % 3)
            pltpu.make_async_remote_copy(
                src_ref=gathered[piece].at[place], dst_ref=gathered[piece].at[place],
                send_sem=line_sem.at[piece], recv_sem=gather_sem.at[piece],
                device_id=(to // MEMBERS, to % MEMBERS), device_id_type=MESH,
            ).start()

    def select(piece, to, out):
        axis = piece % 3
        for place in range(4):
            out[place] = gathered[piece][place, plan[4 * axis + place, to]]

    def shifted(start, offset):
        return lax.rem(start + jnp.where(core == 0, offset, 4 - offset), 4)

    z_at, x_at = ([shifted(start, offset) for offset in range(4)] for start in (zc, xc))
    mate = 1 - core

    def emit(piece, part):
        axis, index = piece % 3, piece - CUTS[part]
        line, _ = line_and_place(me, axis)
        second_at = z_at if axis == 1 else x_at

        def eight(turn, _):
            step = lax.rem(turn + 1, 4)
            first = shifted(zc if axis == 2 else grp, step)
            for offset in (1, 3, 2, 0):
                second = second_at[offset]
                for cross in range(2):
                    to_core = mate if cross else core
                    if axis == 0:
                        to_grp, to_dev = first, zc * 8 + second * 2 + to_core
                    elif axis == 1:
                        to_grp, to_dev = first, second * 8 + xc * 2 + to_core
                    else:
                        to_grp, to_dev = grp, first * 8 + second * 2 + to_core
                    slot = step * 8 + (offset * 2 + cross)

                    def send_one(to_grp=to_grp, to_dev=to_dev, slot=slot):
                        out = outs[part].at[index, slot]
                        select(piece, to_grp * MEMBERS + to_dev, out)
                        pltpu.make_async_remote_copy(
                            src_ref=out, dst_ref=ins[part].at[index, pl.ds(line * 4, 4)],
                            send_sem=out_sem.at[part], recv_sem=in_sem.at[part],
                            device_id=(to_grp, to_dev), device_id_type=MESH,
                        ).start()

                    if offset == 0 and cross == 0:
                        pl.when(step != 0)(send_one)
                    else:
                        send_one()
            return 0

        lax.fori_loop(0, 4, eight, 0)
        select(piece, me, outs[part].at[index, 0])
        return pltpu.make_async_copy(
            outs[part].at[index, 0], ins[part].at[index, pl.ds(line * 4, 4)], own_sem.at[piece]
        )

    for copy in small_copies[2:]:
        copy.wait()
    tile_rows = [stack_rows([tiles_ref[side : side + 1, :]], 40, 0) for side in range(2)]
    owner_rows = stack_rows([owner_ref[...].reshape(1, -1)], 40, -1)
    make_plan(me, *tile_rows, owner_rows, plan_vector)
    plan_copy = pltpu.make_async_copy(plan_vector, plan, plan_sem)
    plan_copy.start()
    plan_out = pltpu.make_async_copy(plan_vector, plan_out_ref, plan_out_sem)
    plan_out.start()
    plan_copy.wait()
    own_copies = []
    for part in range(EARLY + 1):
        for piece in range(CUTS[part], CUTS[part + 1]):
            others = gathered[piece].at[pl.ds(0, 3)]
            pltpu.make_async_copy(others, others, gather_sem.at[piece]).wait()
            own_copies.append(emit(piece, part))
            own_copies[piece].start()

    def drain(step, _):
        samples_to((dev + step) % MEMBERS).wait_send()
        return 0

    lax.fori_loop(1, MEMBERS, drain, 0)
    def await_part(part):
        for piece in range(CUTS[part], CUTS[part + 1]):
            own_copies[piece].wait()
        others = ins[part].at[:, pl.ds(0, DEVICES - 4)]
        pltpu.make_async_copy(others, others, in_sem.at[part]).wait()

    def tiles_of(part):
        def one(group, _):
            for tile in range(TILES):
                cross_spectra(ins[part], plan, crosses[part], group * TILES + tile, tile, axes_of(part))
            lagged = jnp.dot(crosses[part][...], lags[part][...], preferred_element_type=F32)
            lagged = lagged.reshape(TILES, BLK, BLK, NLAG)
            rows = pl.ds(group * TILES, TILES)
            if part > 0:
                lagged = lagged + first_sums[rows]
            if part < EARLY - 1:
                first_sums[rows] = lagged
            else:
                partial[rows] = lagged.astype(BF16)
                pltpu.make_async_copy(partial.at[rows], partial_ref.at[rows], partial_sem).start()
            return 0

        lax.fori_loop(0, SLOTS // TILES, one, 0)

    for copy in lag_copies:
        copy.wait()
    for part in range(EARLY):
        await_part(part)
        tiles_of(part)
    pltpu.make_async_copy(partial, partial_ref, partial_sem).wait()
    plan_out.wait()
    for part in range(EARLY + 1):
        sent = outs[part].at[:, pl.ds(0, MEMBERS - 1)]
        pltpu.make_async_copy(sent, sent, out_sem.at[part]).wait()
    await_part(EARLY)
    for piece in range(PIECES):
        others = gathered[piece].at[pl.ds(0, 3)]
        pltpu.make_async_copy(others, others, line_sem.at[piece]).wait()


def late_kernel(
    plan_ref, late_ref, partial_ref, lag_ref, out_ref,
    late, lag, partial, total, cross, late_sem, lag_sem, in_sem, out_sem,
):
    count = plan_ref[15, 0]
    pieces = 4
    size = DEVICES // pieces
    late_copies = [
        pltpu.make_async_copy(
            late_ref.at[:, pl.ds(size * index, size)], late.at[:, pl.ds(size * index, size)],
            late_sem.at[index],
        )
        for index in range(pieces)
    ]
    lag_copy = pltpu.make_async_copy(lag_ref, lag, lag_sem)

    def rows(group):
        return pl.ds(group * TILES, TILES)

    def load(group):
        return pltpu.make_async_copy(
            partial_ref.at[rows(group)], partial.at[rows(group)], in_sem.at[group]
        )

    for copy in late_copies:
        copy.start()
    lag_copy.start()

    def fetch(group, _):
        load(group).start()
        return 0

    lax.fori_loop(0, SLOTS // TILES, fetch, 0)
    for copy in late_copies:
        copy.wait()
    lag_copy.wait()

    def one(group, _):
        load(group).wait()

        @pl.when(group * TILES < count)
        def _():
            for tile in range(TILES):
                cross_spectra(late, plan_ref, cross, group * TILES + tile, tile, axes_of(EARLY))
            lagged = jnp.dot(cross[...], lag[...], preferred_element_type=F32)
            lagged = lagged + partial[rows(group)].astype(F32).reshape(lagged.shape)
            index = lax.broadcasted_iota(jnp.int32, lagged.shape, 0) // 64 + group * TILES
            total[rows(group)] = jnp.where(index < count, lagged, 0.0).reshape(TILES, BLK, BLK, NLAG)

        @pl.when(group * TILES >= count)
        def _():
            total[rows(group)] = jnp.zeros((TILES, BLK, BLK, NLAG), F32)

        pltpu.make_async_copy(total.at[rows(group)], out_ref.at[rows(group)], out_sem).start()
        return 0

    lax.fori_loop(0, SLOTS // TILES, one, 0)
    pltpu.make_async_copy(total, out_ref, out_sem).wait()


def per_device(strain, taps, tiles, owner):
    hbm = pl.BlockSpec(memory_space=pl.ANY)
    lag = lag_table()
    basis, rows = base_tables()
    lags = [
        lag.reshape(2, PIECES, PIECE, NLAG)[:, CUTS[part] : CUTS[part + 1]].reshape(-1, NLAG)
        for part in range(EARLY + 1)
    ]
    groups = SLOTS // TILES
    late, partial, plan = pl.pallas_call(
        exchange_kernel,
        out_shape=(
            jax.ShapeDtypeStruct((COUNTS[EARLY], DEVICES, 2 * BLK, PIECE), BF16),
            jax.ShapeDtypeStruct((SLOTS, BLK, BLK, NLAG), BF16),
            jax.ShapeDtypeStruct((16, 128), jnp.int32),
        ),
        in_specs=[hbm] * (6 + EARLY),
        out_specs=(hbm, hbm, hbm),
        scratch_shapes=[
            pltpu.VMEM((16, 960, 256), BF16),
            pltpu.VMEM((1, NTAP), BF16),
            pltpu.VMEM((2, 4160), jnp.int32),
            pltpu.VMEM((4160,), jnp.int32),
            pltpu.VMEM((2 * RANK, EXT), BF16),
            pltpu.VMEM((4, 8 * RANK, 2 * NF), BF16),
            *[pltpu.VMEM((2 * count * PIECE, NLAG), BF16) for count in COUNTS[:EARLY]],
            pltpu.VMEM((EXT, 960), BF16),
            pltpu.VMEM((16, 128), jnp.int32),
            pltpu.SMEM((16, 128), jnp.int32),
            pltpu.VMEM((MEMBERS, RANK, CH), BF16),
            pltpu.VMEM((MEMBERS, RANK, CH), BF16),
            pltpu.VMEM((CH, 2 * NF), F32),
            *[pltpu.VMEM((4, 16, 2 * BLK, PIECE), BF16) for _ in range(PIECES)],
            *[pltpu.VMEM((count, MEMBERS, 4, 2 * BLK, PIECE), BF16) for count in COUNTS],
            *[pltpu.VMEM((count, DEVICES, 2 * BLK, PIECE), BF16) for count in COUNTS[:EARLY]],
            *[pltpu.VMEM((TILES * 64, 2 * count * PIECE), BF16) for count in COUNTS[:EARLY]],
            pltpu.VMEM((SLOTS, BLK, BLK, NLAG), F32),
            pltpu.VMEM((SLOTS, BLK, BLK, NLAG), BF16),
            pltpu.SemaphoreType.DMA((16,)),
            pltpu.SemaphoreType.DMA((4,)),
            pltpu.SemaphoreType.DMA((4,)),
            pltpu.SemaphoreType.DMA((EARLY,)),
            pltpu.SemaphoreType.DMA,
            pltpu.SemaphoreType.DMA,
            pltpu.SemaphoreType.DMA((MEMBERS,)),
            pltpu.SemaphoreType.DMA((MEMBERS,)),
            pltpu.SemaphoreType.DMA((PIECES,)),
            pltpu.SemaphoreType.DMA((PIECES,)),
            pltpu.SemaphoreType.DMA((EARLY + 1,)),
            pltpu.SemaphoreType.DMA((EARLY + 1,)),
            pltpu.SemaphoreType.DMA((PIECES,)),
            pltpu.SemaphoreType.DMA,
            pltpu.SemaphoreType.REGULAR,
        ],
        compiler_params=pltpu.CompilerParams(
            collective_id=0, has_side_effects=True, vmem_limit_bytes=60 * 2**20
        ),
    )(
        strain.T, taps[None, :], tiles.T, owner, jnp.asarray(basis), jnp.asarray(rows.reshape(4, 8 * RANK, 2 * NF)),
        *[jnp.asarray(part) for part in lags[:EARLY]],
    )

    return pl.pallas_call(
        late_kernel,
        out_shape=jax.ShapeDtypeStruct((SLOTS, BLK, BLK, NLAG), F32),
        in_specs=[pl.BlockSpec(memory_space=pltpu.SMEM), hbm, hbm, hbm],
        out_specs=hbm,
        scratch_shapes=[
            pltpu.VMEM((COUNTS[EARLY], DEVICES, 2 * BLK, PIECE), BF16),
            pltpu.VMEM((2 * COUNTS[EARLY] * PIECE, NLAG), BF16),
            pltpu.VMEM((SLOTS, BLK, BLK, NLAG), BF16),
            pltpu.VMEM((SLOTS, BLK, BLK, NLAG), F32),
            pltpu.VMEM((TILES * 64, 2 * COUNTS[EARLY] * PIECE), BF16),
            pltpu.SemaphoreType.DMA((4,)),
            pltpu.SemaphoreType.DMA,
            pltpu.SemaphoreType.DMA((groups,)),
            pltpu.SemaphoreType.DMA,
        ],
        compiler_params=pltpu.CompilerParams(vmem_limit_bytes=60 * 2**20),
    )(plan, late, partial, jnp.asarray(lags[EARLY]))


def solution(mesh):
    return jax.shard_map(
        per_device,
        mesh=mesh,
        in_specs=(P("grp", "dev"), P(), P(), P()),
        out_specs=P(("grp", "dev"), None, None, None),
        check_vma=False,
    )
```

```python
import functools
import math

import jax
import jax.numpy as jnp
import ml_dtypes
import numpy as np
from jax import lax
from jax.experimental import pallas as pl
from jax.experimental.pallas import tpu as pltpu
from jax.sharding import PartitionSpec as P

NT = 6144
NF = 1024
F0 = 32
NLAG = 384
NTAP = 64
DECIM = 5
BLK = 8
MEMBERS = 32
GROUPS = 4
DEVICES = 128
COLS = NT // MEMBERS
EXT = 208
USED = 205
RANK = 96
STRETCHES = ((0, 64), (48, 120), (96, 168), (144, 208))
PARTS = 8
CH = 128
SLOTS = 64
PIECE = 128
PIECES = NF // PIECE
AHEAD = 3
CUTS = (0, 4, 6, 7, 8)
COUNTS = (4, 2, 1, 1)
EARLY = len(COUNTS) - 1
TILES = 4
MESH = pl.DeviceIdType.MESH
F32 = jnp.float32
BF16 = jnp.bfloat16


def trig(phase, factor=1.0):
    angle = np.float32(2.0 * math.pi / NT) * phase.astype(np.float32)
    angle = angle.astype(np.float64)
    return np.cos(angle) * factor, -np.sin(angle) * factor


def base_tables():
    samples = np.arange(USED)
    width = (F0 + NF) / NT
    steps = samples[1:] * (USED - samples[1:]) / 2
    diagonal = ((USED - 1) / 2 - samples) ** 2 * math.cos(2 * math.pi * width)
    _, vectors = np.linalg.eigh(np.diag(diagonal) + np.diag(steps, 1) + np.diag(steps, -1))
    basis = vectors[:, ::-1][:, :RANK].T
    half = basis[:, : USED // 2]
    basis = basis * np.sign(np.take_along_axis(half, np.abs(half).argmax(axis=1)[:, None], axis=1))

    def table(place):
        rows = place * COLS + samples
        angle = 2.0 * math.pi / NT * (rows[:, None] * (F0 + np.arange(NF))[None, :] % NT)
        return np.concatenate([np.cos(angle), -np.sin(angle)], axis=1)

    assert np.abs(basis.T @ (basis @ table(0)) - table(0)).max() < 1e-10
    rows = np.concatenate([basis @ table(place) for place in range(MEMBERS)], axis=0)
    basis = np.pad(basis, ((0, 0), (0, EXT - USED)))
    high = basis.astype(ml_dtypes.bfloat16)
    low = (basis - high.astype(np.float64)).astype(ml_dtypes.bfloat16)
    return np.concatenate([high, low], axis=0), rows.astype(ml_dtypes.bfloat16)


def lag_table():
    lags = (np.arange(NLAG) - NLAG // 2) % NT
    phase = (F0 + np.arange(NF))[:, None] * lags[None, :] % NT
    real, imag = trig(phase, 1.0 / math.sqrt(NF))
    return np.concatenate([real, imag], axis=0).astype(ml_dtypes.bfloat16)


def nt_dot(a, b):
    return lax.dot_general(a, b, (((1,), (1,)), ((), ())), preferred_element_type=F32)


def stack_rows(pieces, rows, fill):
    width = sum(piece.shape[1] for piece in pieces)
    extra = jnp.full((1, rows * 128 - width), fill, jnp.int32)
    line = jnp.concatenate([*pieces, extra], axis=1)
    return jnp.concatenate(
        [line[:, index * 128 : (index + 1) * 128] for index in range(rows)], axis=0
    )


def make_band(member, taps):
    tap = lax.broadcasted_iota(jnp.int32, (NTAP, 1024), 0)
    lane = lax.broadcasted_iota(jnp.int32, (NTAP, 1024), 1)
    place = (lane == (1024 - tap) % 1024).astype(F32).astype(BF16)
    taps = jnp.broadcast_to(taps.astype(F32), (8, NTAP)).astype(BF16)
    line = jnp.dot(taps, place, preferred_element_type=F32)
    first_rows = pltpu.roll(line, 0, 1, stride=DECIM, stride_axis=0)
    band = jnp.concatenate(
        [pltpu.roll(first_rows, 8 * DECIM * index, 1) for index in range(EXT // 8)], axis=0
    )
    row = lax.broadcasted_iota(jnp.int32, (EXT, 1024), 0)
    limit = jnp.where(member == MEMBERS - 1, COLS, USED)
    return jnp.where(row < limit, band, 0.0)[:, :960].astype(BF16)


def filtered(band, raw):
    count = raw.shape[0]
    sums = [
        jnp.dot(
            band[low:high, 256 * index : min(256 * (index + 1), count)],
            raw[256 * index : min(256 * (index + 1), count)],
            preferred_element_type=F32,
        )
        for index, (low, high) in enumerate(STRETCHES)
    ]
    pieces = []
    done = 0
    for index, (low, high) in enumerate(STRETCHES):
        end = STRETCHES[index + 1][0] if index + 1 < len(STRETCHES) else high
        pieces.append(sums[index][done - low : end - low])
        if end < high:
            after = STRETCHES[index + 1][0]
            pieces.append(sums[index][end - low :] + sums[index + 1][: high - after])
        done = high
    return jnp.concatenate(pieces, axis=0)


def coordinates(device):
    return device // 8 % 4, device // 2 % 4, device // 32, device % 2


def line_and_place(device, axis):
    z, x, y, c = coordinates(device)
    if axis == 0:
        return y * 8 + x * 2 + c, z
    if axis == 1:
        return y * 8 + z * 2 + c, x
    return z * 8 + x * 2 + c, y


def device_of(line, place, axis):
    first, second, c = line // 8, line // 2 % 4, line % 2
    if axis == 0:
        return first * 32 + place * 8 + second * 2 + c
    if axis == 1:
        return first * 32 + second * 8 + place * 2 + c
    return place * 32 + line


def make_plan(me, src, dst, own, plan_ref):
    rows = src.shape[0]
    mine = own == me
    lane_a = lax.broadcasted_iota(jnp.int32, (128, 128), 0)
    lane = lax.broadcasted_iota(jnp.int32, (rows, 128), 1)
    row = lax.broadcasted_iota(jnp.int32, (rows, 128), 0)
    flags = jnp.where(mine, 1, 0)
    within = flags
    for shift in (1, 2, 4, 8, 16, 32, 64):
        within = within + jnp.where(lane >= shift, pltpu.roll(within, shift, 1), 0)
    totals = jnp.broadcast_to(jnp.sum(flags, axis=1, keepdims=True), (rows, 128))
    before = totals
    for shift in (1, 2, 4, 8, 16, 32):
        before = before + jnp.where(row >= shift, pltpu.roll(before, shift, 0), 0)
    slot = jnp.where(mine, within - flags + before - totals, -1)
    src_dev, dst_dev = src // 16, dst // 16

    first = jnp.zeros((SLOTS, 128), jnp.int32)
    second = jnp.zeros((SLOTS, 128), jnp.int32)
    for index in range(rows):
        hit = slot[index : index + 1, :] == lane_a[:SLOTS]
        first = first + jnp.where(hit, src_dev[index : index + 1, :], 0)
        second = second + jnp.where(hit, dst_dev[index : index + 1, :], 0)
    ends = jnp.sum(jnp.concatenate([first, second], axis=0).T, axis=0, keepdims=True)
    lines = []
    for axis in range(3):
        line, place = line_and_place(ends, axis)
        lines.append(line * 4 + place)
    count = jnp.sum(flags, axis=(0, 1), keepdims=True)
    lines.append(jnp.broadcast_to(count, (1, 128)))
    plan_ref[12:16, :] = jnp.concatenate(lines, axis=0)

    z, x, y, _ = coordinates(me)

    def wanted(entry, _):
        axis, place = entry // 4, entry % 4
        source = jnp.where(
            axis == 0, me + (place - z) * 8, jnp.where(axis == 1, me + (place - x) * 2, me + (place - y) * 32)
        )
        local = jnp.where(src_dev == source, src % 16, 0) + jnp.where(dst_dev == source, dst % 16, 0)
        blocks = jnp.zeros((128, 128), jnp.int32)
        for index in range(rows):
            hit = own[index : index + 1, :] == lane_a
            blocks = blocks + jnp.where(hit, local[index : index + 1, :], 0)
        plan_ref[pl.ds(entry, 1), :] = jnp.sum(blocks.T, axis=0, keepdims=True)
        return 0

    lax.fori_loop(0, 12, wanted, 0)


def cross_spectra(into, plan, cross, slot, tile, axes):
    width = len(axes) * PIECE
    for index, axis in enumerate(axes):
        a = into[index, plan[12 + axis, slot]].astype(F32)
        b = into[index, plan[12 + axis, SLOTS + slot]].astype(F32)
        ar, ai, br, bi = a[:BLK], a[BLK:], b[:BLK], b[BLK:]
        left = index * PIECE
        for pair in range(BLK // 2):
            reals, imags = [], []
            for i in (2 * pair, 2 * pair + 1):
                xr, xi = ar[i : i + 1, :], ai[i : i + 1, :]
                reals.append(xr * br + xi * bi)
                imags.append(xi * br - xr * bi)
            at = tile * 64 + pair * 16
            cross[at : at + 16, left : left + PIECE] = jnp.concatenate(reals, axis=0).astype(BF16)
            cross[at : at + 16, width + left : width + left + PIECE] = jnp.concatenate(
                imags, axis=0
            ).astype(BF16)


def axes_of(part):
    return [piece % 3 for piece in range(CUTS[part], CUTS[part + 1])]


def exchange_kernel(
    strain_ref, taps_hbm, tiles_hbm, owner_hbm, basis_hbm, base_ref, lag0_ref, lag1_ref, lag2_ref,
    late_ref, partial_ref, plan_out_ref,
    raw, taps_ref, tiles_ref, owner_ref, basis, base, lag0, lag1, lag2, band, plan_vector, plan, send, recv, acc,
    gathered0, gathered1, gathered2, gathered3, gathered4, gathered5, gathered6, gathered7,
    out0, out1, out2, out3, in0, in1, in2, cross0, cross1, cross2, first_sums, partial,
    raw_sem, small_sem, base_sem, lag_sem, plan_sem, plan_out_sem, send_sem, recv_sem,
    line_sem, gather_sem, out_sem, in_sem, own_sem, partial_sem, plane_sem,
):
    grp, dev = lax.axis_index("grp"), lax.axis_index("dev")
    me = grp * MEMBERS + dev
    chip, core = dev // 2, dev % 2
    zc, xc = chip // 4, chip % 4

    def turned(offset):
        return jnp.where(core == 0, offset, (4 - offset) % 4)

    def at(z, x, c):
        return z % 4 * 8 + x % 4 * 2 + c

    def chip_at(offset):
        return (zc + turned(offset // 4)) % 4 * 4 + (xc + turned(offset % 4)) % 4

    def raw_copy(offset):
        to_chip = chip_at(offset)
        return pltpu.make_async_copy(
            strain_ref.at[:, pl.ds(pl.multiple_of(to_chip * 256, 256), 256)],
            raw.at[to_chip], raw_sem.at[to_chip],
        )

    def fetch(step, _):
        raw_copy(step * 7 % 16).start()
        return 0

    small = ((taps_hbm, taps_ref), (basis_hbm, basis), (tiles_hbm, tiles_ref))
    small = small + ((owner_hbm, owner_ref),)
    small_copies = [
        pltpu.make_async_copy(source, into, small_sem.at[index])
        for index, (source, into) in enumerate(small)
    ]
    for copy in small_copies:
        copy.start()
    lax.fori_loop(0, 16, fetch, 0)
    def base_copy(plane):
        return pltpu.make_async_copy(base_ref.at[plane], base.at[plane], base_sem.at[plane])

    lag_copies = [
        pltpu.make_async_copy(lag0_ref, lag0, lag_sem.at[0]),
        pltpu.make_async_copy(lag1_ref, lag1, lag_sem.at[1]),
        pltpu.make_async_copy(lag2_ref, lag2, lag_sem.at[2]),
    ]

    barrier = pltpu.get_barrier_semaphore()

    def greet(step, _):
        pl.semaphore_signal(
            barrier, inc=1, device_id=(grp, (dev + step) % MEMBERS), device_id_type=MESH
        )
        return 0

    lax.fori_loop(1, MEMBERS, greet, 0)
    for step in range(1, GROUPS):
        pl.semaphore_signal(
            barrier, inc=1, device_id=((grp + step) % GROUPS, dev), device_id_type=MESH
        )
    small_copies[0].wait()
    small_copies[1].wait()
    band[...] = make_band(dev, taps_ref[...])
    pl.semaphore_wait(barrier, MEMBERS - 1 + GROUPS - 1)

    def samples_to(to):
        return pltpu.make_async_remote_copy(
            src_ref=send.at[to], dst_ref=recv.at[dev], send_sem=send_sem.at[to],
            recv_sem=recv_sem.at[dev], device_id=(grp, to), device_id_type=MESH,
        )

    def decimate(pair, _):
        results = []
        for index in range(2):
            offset = (pair * 2 + index) * 7 % 16
            raw_copy(offset).wait()
            to_chip = chip_at(offset)
            result = filtered(band, raw.at[to_chip]).astype(BF16)
            halves = jnp.dot(basis[...], result, preferred_element_type=F32)
            results.append((to_chip, (halves[:RANK] + halves[RANK:]).astype(BF16)))
        @pl.when(pair % 2 == 1)
        def _():
            base_copy((zc + pair // 2) % 4).start()

        for to_chip, result in results:
            for half in range(2):
                send[to_chip * 2 + half] = result[:, half * CH : (half + 1) * CH]
                to = to_chip * 2 + half

                @pl.when(to != dev)
                def _():
                    samples_to(to).start()

        return 0

    lax.fori_loop(0, 8, decimate, 0)
    for copy in lag_copies:
        copy.start()
    recv[dev] = send[dev]
    for step in range(1, GROUPS):
        pl.semaphore_signal(
            plane_sem, inc=1, device_id=((grp + step) % GROUPS, dev), device_id_type=MESH
        )
    acc[...] = jnp.zeros_like(acc)

    def transform(step, _):
        plane = (zc + step) % 4
        first = plane * 8
        for index in range(8):
            source = first + index

            @pl.when(source != dev)
            def _():
                pltpu.make_async_remote_copy(
                    src_ref=send.at[source], dst_ref=recv.at[source],
                    send_sem=send_sem.at[source], recv_sem=recv_sem.at[source],
                    device_id=(grp, source), device_id_type=MESH,
                ).wait_recv()

        base_copy(plane).wait()
        samples = recv[pl.ds(first, 8)].reshape(8 * RANK, CH)
        acc[...] += lax.dot_general(
            samples, base[plane], (((0,), (0,)), ((), ())), preferred_element_type=F32
        )
        return 0

    lax.fori_loop(0, 4, transform, 0)

    real, imag = acc[:, :NF], acc[:, NF:]
    power = real * real + imag * imag
    level = jnp.mean(power, axis=1, keepdims=True)
    scale = lax.rsqrt(power + level + 1e-06)
    outs, ins = (out0, out1, out2, out3), (in0, in1, in2, late_ref)
    crosses, lags = (cross0, cross1, cross2), (lag0, lag1, lag2)
    gathered = (gathered0, gathered1, gathered2, gathered3)
    gathered = gathered + (gathered4, gathered5, gathered6, gathered7)
    def line_copy(piece, source, blocks, way, sem):
        line, place = line_and_place(me, piece % 3)
        to = device_of(line, lax.rem(place + (1, 3)[way], 4), piece % 3)
        view = gathered[piece].at[source, blocks]
        return pltpu.make_async_remote_copy(
            src_ref=view, dst_ref=view, send_sem=line_sem.at[piece], recv_sem=gather_sem.at[piece, sem],
            device_id=(to // MEMBERS, to % MEMBERS), device_id_type=MESH,
        )

    def near(piece, way):
        _, place = line_and_place(me, piece % 3)
        return line_copy(piece, place, pl.ds(0, 16), way, way)

    def onward(piece, way):
        _, place = line_and_place(me, piece % 3)
        return line_copy(piece, lax.rem(place + (3, 1)[way], 4), pl.ds(8 * way, 8), way, 2 + way)

    def pass_on(piece):
        for way in range(2):
            near(piece, way).wait_recv()
            onward(piece, way).start()

    pl.semaphore_wait(plane_sem, GROUPS - 1)
    for piece in range(PIECES):
        line, place = line_and_place(me, piece % 3)
        bins = slice(piece * PIECE, (piece + 1) * PIECE)
        factor = scale[:, bins]
        parts = (acc[:, bins] * factor, acc[:, NF + piece * PIECE : NF + (piece + 1) * PIECE] * factor)
        gathered[piece][place] = jnp.concatenate(
            [half.reshape(16, BLK, PIECE) for half in parts], axis=1
        ).astype(BF16)
        for way in range(2):
            near(piece, way).start()

    def select(piece, to, out):
        axis = piece % 3
        for place in range(4):
            out[place] = gathered[piece][place, plan[4 * axis + place, to]]

    def shifted(start, offset):
        return lax.rem(start + jnp.where(core == 0, offset, 4 - offset), 4)

    z_at, x_at = ([shifted(start, offset) for offset in range(4)] for start in (zc, xc))
    mate = 1 - core

    def emit(piece, part):
        axis, index = piece % 3, piece - CUTS[part]
        line, _ = line_and_place(me, axis)
        second_at = z_at if axis == 1 else x_at

        def eight(turn, _):
            step = lax.rem(turn + 1, 4)
            first = shifted(zc if axis == 2 else grp, step)
            for offset in (1, 3, 2, 0):
                second = second_at[offset]
                for cross in range(2):
                    to_core = mate if cross else core
                    if axis == 0:
                        to_grp, to_dev = first, zc * 8 + second * 2 + to_core
                    elif axis == 1:
                        to_grp, to_dev = first, second * 8 + xc * 2 + to_core
                    else:
                        to_grp, to_dev = grp, first * 8 + second * 2 + to_core
                    slot = step * 8 + (offset * 2 + cross)

                    def send_one(to_grp=to_grp, to_dev=to_dev, slot=slot):
                        out = outs[part].at[index, slot]
                        select(piece, to_grp * MEMBERS + to_dev, out)
                        pltpu.make_async_remote_copy(
                            src_ref=out, dst_ref=ins[part].at[index, pl.ds(line * 4, 4)],
                            send_sem=out_sem.at[part], recv_sem=in_sem.at[part],
                            device_id=(to_grp, to_dev), device_id_type=MESH,
                        ).start()

                    if offset == 0 and cross == 0:
                        pl.when(step != 0)(send_one)
                    else:
                        send_one()
            return 0

        lax.fori_loop(0, 4, eight, 0)
        select(piece, me, outs[part].at[index, 0])
        return pltpu.make_async_copy(
            outs[part].at[index, 0], ins[part].at[index, pl.ds(line * 4, 4)], own_sem.at[piece]
        )

    for copy in small_copies[2:]:
        copy.wait()
    tile_rows = [stack_rows([tiles_ref[side : side + 1, :]], 40, 0) for side in range(2)]
    owner_rows = stack_rows([owner_ref[...].reshape(1, -1)], 40, -1)
    make_plan(me, *tile_rows, owner_rows, plan_vector)
    plan_copy = pltpu.make_async_copy(plan_vector, plan, plan_sem)
    plan_copy.start()
    plan_out = pltpu.make_async_copy(plan_vector, plan_out_ref, plan_out_sem)
    plan_out.start()
    plan_copy.wait()
    for piece in range(AHEAD):
        pass_on(piece)
    own_copies = []
    for part in range(EARLY + 1):
        for piece in range(CUTS[part], CUTS[part + 1]):
            if piece + AHEAD < PIECES:
                pass_on(piece + AHEAD)
            for way in range(2):
                onward(piece, way).wait_recv()
            own_copies.append(emit(piece, part))
            own_copies[piece].start()

    def drain(step, _):
        samples_to((dev + step) % MEMBERS).wait_send()
        return 0

    lax.fori_loop(1, MEMBERS, drain, 0)
    def await_part(part):
        for piece in range(CUTS[part], CUTS[part + 1]):
            own_copies[piece].wait()
        others = ins[part].at[:, pl.ds(0, DEVICES - 4)]
        pltpu.make_async_copy(others, others, in_sem.at[part]).wait()

    def tiles_of(part):
        def one(group, _):
            for tile in range(TILES):
                cross_spectra(ins[part], plan, crosses[part], group * TILES + tile, tile, axes_of(part))
            lagged = jnp.dot(crosses[part][...], lags[part][...], preferred_element_type=F32)
            lagged = lagged.reshape(TILES, BLK, BLK, NLAG)
            rows = pl.ds(group * TILES, TILES)
            if part > 0:
                lagged = lagged + first_sums[rows]
            if part < EARLY - 1:
                first_sums[rows] = lagged
            else:
                partial[rows] = lagged.astype(BF16)
                pltpu.make_async_copy(partial.at[rows], partial_ref.at[rows], partial_sem).start()
            return 0

        lax.fori_loop(0, SLOTS // TILES, one, 0)

    for copy in lag_copies:
        copy.wait()
    for part in range(EARLY):
        await_part(part)
        tiles_of(part)
    pltpu.make_async_copy(partial, partial_ref, partial_sem).wait()
    plan_out.wait()
    for part in range(EARLY + 1):
        sent = outs[part].at[:, pl.ds(0, MEMBERS - 1)]
        pltpu.make_async_copy(sent, sent, out_sem.at[part]).wait()
    await_part(EARLY)
    for piece in range(PIECES):
        others = gathered[piece].at[pl.ds(0, 3)]
        pltpu.make_async_copy(others, others, line_sem.at[piece]).wait()


def late_kernel(
    plan_ref, late_ref, partial_ref, lag_ref, out_ref,
    late, lag, partial, total, cross, late_sem, lag_sem, in_sem, out_sem,
):
    count = plan_ref[15, 0]
    pieces = 4
    size = DEVICES // pieces
    late_copies = [
        pltpu.make_async_copy(
            late_ref.at[:, pl.ds(size * index, size)], late.at[:, pl.ds(size * index, size)],
            late_sem.at[index],
        )
        for index in range(pieces)
    ]
    lag_copy = pltpu.make_async_copy(lag_ref, lag, lag_sem)

    def rows(group):
        return pl.ds(group * TILES, TILES)

    def load(group):
        return pltpu.make_async_copy(
            partial_ref.at[rows(group)], partial.at[rows(group)], in_sem.at[group]
        )

    for copy in late_copies:
        copy.start()
    lag_copy.start()

    def fetch(group, _):
        load(group).start()
        return 0

    lax.fori_loop(0, SLOTS // TILES, fetch, 0)
    for copy in late_copies:
        copy.wait()
    lag_copy.wait()

    def one(group, _):
        load(group).wait()

        @pl.when(group * TILES < count)
        def _():
            for tile in range(TILES):
                cross_spectra(late, plan_ref, cross, group * TILES + tile, tile, axes_of(EARLY))
            lagged = jnp.dot(cross[...], lag[...], preferred_element_type=F32)
            lagged = lagged + partial[rows(group)].astype(F32).reshape(lagged.shape)
            index = lax.broadcasted_iota(jnp.int32, lagged.shape, 0) // 64 + group * TILES
            total[rows(group)] = jnp.where(index < count, lagged, 0.0).reshape(TILES, BLK, BLK, NLAG)

        @pl.when(group * TILES >= count)
        def _():
            total[rows(group)] = jnp.zeros((TILES, BLK, BLK, NLAG), F32)

        pltpu.make_async_copy(total.at[rows(group)], out_ref.at[rows(group)], out_sem).start()
        return 0

    lax.fori_loop(0, SLOTS // TILES, one, 0)
    pltpu.make_async_copy(total, out_ref, out_sem).wait()


def per_device(strain, taps, tiles, owner):
    hbm = pl.BlockSpec(memory_space=pl.ANY)
    lag = lag_table()
    basis, rows = base_tables()
    lags = [
        lag.reshape(2, PIECES, PIECE, NLAG)[:, CUTS[part] : CUTS[part + 1]].reshape(-1, NLAG)
        for part in range(EARLY + 1)
    ]
    groups = SLOTS // TILES
    late, partial, plan = pl.pallas_call(
        exchange_kernel,
        out_shape=(
            jax.ShapeDtypeStruct((COUNTS[EARLY], DEVICES, 2 * BLK, PIECE), BF16),
            jax.ShapeDtypeStruct((SLOTS, BLK, BLK, NLAG), BF16),
            jax.ShapeDtypeStruct((16, 128), jnp.int32),
        ),
        in_specs=[hbm] * (6 + EARLY),
        out_specs=(hbm, hbm, hbm),
        scratch_shapes=[
            pltpu.VMEM((16, 960, 256), BF16),
            pltpu.VMEM((1, NTAP), BF16),
            pltpu.VMEM((2, 4160), jnp.int32),
            pltpu.VMEM((4160,), jnp.int32),
            pltpu.VMEM((2 * RANK, EXT), BF16),
            pltpu.VMEM((4, 8 * RANK, 2 * NF), BF16),
            *[pltpu.VMEM((2 * count * PIECE, NLAG), BF16) for count in COUNTS[:EARLY]],
            pltpu.VMEM((EXT, 960), BF16),
            pltpu.VMEM((16, 128), jnp.int32),
            pltpu.SMEM((16, 128), jnp.int32),
            pltpu.VMEM((MEMBERS, RANK, CH), BF16),
            pltpu.VMEM((MEMBERS, RANK, CH), BF16),
            pltpu.VMEM((CH, 2 * NF), F32),
            *[pltpu.VMEM((4, 16, 2 * BLK, PIECE), BF16) for _ in range(PIECES)],
            *[pltpu.VMEM((count, MEMBERS, 4, 2 * BLK, PIECE), BF16) for count in COUNTS],
            *[pltpu.VMEM((count, DEVICES, 2 * BLK, PIECE), BF16) for count in COUNTS[:EARLY]],
            *[pltpu.VMEM((TILES * 64, 2 * count * PIECE), BF16) for count in COUNTS[:EARLY]],
            pltpu.VMEM((SLOTS, BLK, BLK, NLAG), F32),
            pltpu.VMEM((SLOTS, BLK, BLK, NLAG), BF16),
            pltpu.SemaphoreType.DMA((16,)),
            pltpu.SemaphoreType.DMA((4,)),
            pltpu.SemaphoreType.DMA((4,)),
            pltpu.SemaphoreType.DMA((EARLY,)),
            pltpu.SemaphoreType.DMA,
            pltpu.SemaphoreType.DMA,
            pltpu.SemaphoreType.DMA((MEMBERS,)),
            pltpu.SemaphoreType.DMA((MEMBERS,)),
            pltpu.SemaphoreType.DMA((PIECES,)),
            pltpu.SemaphoreType.DMA((PIECES, 4)),
            pltpu.SemaphoreType.DMA((EARLY + 1,)),
            pltpu.SemaphoreType.DMA((EARLY + 1,)),
            pltpu.SemaphoreType.DMA((PIECES,)),
            pltpu.SemaphoreType.DMA,
            pltpu.SemaphoreType.REGULAR,
        ],
        compiler_params=pltpu.CompilerParams(
            collective_id=0, has_side_effects=True, vmem_limit_bytes=60 * 2**20
        ),
    )(
        strain.T, taps[None, :], tiles.T, owner, jnp.asarray(basis), jnp.asarray(rows.reshape(4, 8 * RANK, 2 * NF)),
        *[jnp.asarray(part) for part in lags[:EARLY]],
    )

    return pl.pallas_call(
        late_kernel,
        out_shape=jax.ShapeDtypeStruct((SLOTS, BLK, BLK, NLAG), F32),
        in_specs=[pl.BlockSpec(memory_space=pltpu.SMEM), hbm, hbm, hbm],
        out_specs=hbm,
        scratch_shapes=[
            pltpu.VMEM((COUNTS[EARLY], DEVICES, 2 * BLK, PIECE), BF16),
            pltpu.VMEM((2 * COUNTS[EARLY] * PIECE, NLAG), BF16),
            pltpu.VMEM((SLOTS, BLK, BLK, NLAG), BF16),
            pltpu.VMEM((SLOTS, BLK, BLK, NLAG), F32),
            pltpu.VMEM((TILES * 64, 2 * COUNTS[EARLY] * PIECE), BF16),
            pltpu.SemaphoreType.DMA((4,)),
            pltpu.SemaphoreType.DMA,
            pltpu.SemaphoreType.DMA((groups,)),
            pltpu.SemaphoreType.DMA,
        ],
        compiler_params=pltpu.CompilerParams(vmem_limit_bytes=60 * 2**20),
    )(plan, late, partial, jnp.asarray(lags[EARLY]))


def solution(mesh):
    return jax.shard_map(
        per_device,
        mesh=mesh,
        in_specs=(P("grp", "dev"), P(), P(), P()),
        out_specs=P(("grp", "dev"), None, None, None),
        check_vma=False,
    )
```

```python
import functools
import math

import jax
import jax.numpy as jnp
import ml_dtypes
import numpy as np
from jax import lax
from jax.experimental import pallas as pl
from jax.experimental.pallas import tpu as pltpu
from jax.sharding import PartitionSpec as P

NT = 6144
NF = 1024
F0 = 32
NLAG = 384
NTAP = 64
DECIM = 5
BLK = 8
MEMBERS = 32
GROUPS = 4
DEVICES = 128
COLS = NT // MEMBERS
EXT = 208
USED = 205
RANK = 96
STRETCHES = ((0, 64), (48, 120), (96, 168), (144, 208))
PARTS = 8
CH = 128
SLOTS = 64
PIECE = 128
PIECES = NF // PIECE
CUTS = (0, 4, 6, 7, 8)
COUNTS = (4, 2, 1, 1)
EARLY = len(COUNTS) - 1
TILES = 4
MESH = pl.DeviceIdType.MESH
F32 = jnp.float32
BF16 = jnp.bfloat16


def trig(phase, factor=1.0):
    angle = np.float32(2.0 * math.pi / NT) * phase.astype(np.float32)
    angle = angle.astype(np.float64)
    return np.cos(angle) * factor, -np.sin(angle) * factor


def base_tables():
    samples = np.arange(USED)
    width = (F0 + NF) / NT
    steps = samples[1:] * (USED - samples[1:]) / 2
    diagonal = ((USED - 1) / 2 - samples) ** 2 * math.cos(2 * math.pi * width)
    _, vectors = np.linalg.eigh(np.diag(diagonal) + np.diag(steps, 1) + np.diag(steps, -1))
    basis = vectors[:, ::-1][:, :RANK].T
    half = basis[:, : USED // 2]
    basis = basis * np.sign(np.take_along_axis(half, np.abs(half).argmax(axis=1)[:, None], axis=1))

    def table(place):
        rows = place * COLS + samples
        angle = 2.0 * math.pi / NT * (rows[:, None] * (F0 + np.arange(NF))[None, :] % NT)
        return np.concatenate([np.cos(angle), -np.sin(angle)], axis=1)

    assert np.abs(basis.T @ (basis @ table(0)) - table(0)).max() < 1e-10
    rows = np.concatenate([basis @ table(place) for place in range(MEMBERS)], axis=0)
    basis = np.pad(basis, ((0, 0), (0, EXT - USED)))
    high = basis.astype(ml_dtypes.bfloat16)
    low = (basis - high.astype(np.float64)).astype(ml_dtypes.bfloat16)
    return np.concatenate([high, low], axis=0), rows.astype(ml_dtypes.bfloat16)


def lag_table():
    lags = (np.arange(NLAG) - NLAG // 2) % NT
    phase = (F0 + np.arange(NF))[:, None] * lags[None, :] % NT
    real, imag = trig(phase, 1.0 / math.sqrt(NF))
    return np.concatenate([real, imag], axis=0).astype(ml_dtypes.bfloat16)


def nt_dot(a, b):
    return lax.dot_general(a, b, (((1,), (1,)), ((), ())), preferred_element_type=F32)


def stack_rows(pieces, rows, fill):
    width = sum(piece.shape[1] for piece in pieces)
    extra = jnp.full((1, rows * 128 - width), fill, jnp.int32)
    line = jnp.concatenate([*pieces, extra], axis=1)
    return jnp.concatenate(
        [line[:, index * 128 : (index + 1) * 128] for index in range(rows)], axis=0
    )


def make_band(member, taps):
    tap = lax.broadcasted_iota(jnp.int32, (NTAP, 1024), 0)
    lane = lax.broadcasted_iota(jnp.int32, (NTAP, 1024), 1)
    place = (lane == (1024 - tap) % 1024).astype(F32).astype(BF16)
    taps = jnp.broadcast_to(taps.astype(F32), (8, NTAP)).astype(BF16)
    line = jnp.dot(taps, place, preferred_element_type=F32)
    first_rows = pltpu.roll(line, 0, 1, stride=DECIM, stride_axis=0)
    band = jnp.concatenate(
        [pltpu.roll(first_rows, 8 * DECIM * index, 1) for index in range(EXT // 8)], axis=0
    )
    row = lax.broadcasted_iota(jnp.int32, (EXT, 1024), 0)
    limit = jnp.where(member == MEMBERS - 1, COLS, USED)
    return jnp.where(row < limit, band, 0.0)[:, :960].astype(BF16)


def filtered(band, raw):
    count = raw.shape[0]
    sums = [
        jnp.dot(
            band[low:high, 256 * index : min(256 * (index + 1), count)],
            raw[256 * index : min(256 * (index + 1), count)],
            preferred_element_type=F32,
        )
        for index, (low, high) in enumerate(STRETCHES)
    ]
    pieces = []
    done = 0
    for index, (low, high) in enumerate(STRETCHES):
        end = STRETCHES[index + 1][0] if index + 1 < len(STRETCHES) else high
        pieces.append(sums[index][done - low : end - low])
        if end < high:
            after = STRETCHES[index + 1][0]
            pieces.append(sums[index][end - low :] + sums[index + 1][: high - after])
        done = high
    return jnp.concatenate(pieces, axis=0)


def coordinates(device):
    return device // 8 % 4, device // 2 % 4, device // 32, device % 2


def line_and_place(device, axis):
    z, x, y, c = coordinates(device)
    if axis == 0:
        return y * 8 + x * 2 + c, z
    if axis == 1:
        return y * 8 + z * 2 + c, x
    return z * 8 + x * 2 + c, y


def device_of(line, place, axis):
    first, second, c = line // 8, line // 2 % 4, line % 2
    if axis == 0:
        return first * 32 + place * 8 + second * 2 + c
    if axis == 1:
        return first * 32 + second * 8 + place * 2 + c
    return place * 32 + line


def make_plan(me, src, dst, own, plan_ref):
    rows = src.shape[0]
    mine = own == me
    lane_a = lax.broadcasted_iota(jnp.int32, (128, 128), 0)
    lane = lax.broadcasted_iota(jnp.int32, (rows, 128), 1)
    row = lax.broadcasted_iota(jnp.int32, (rows, 128), 0)
    flags = jnp.where(mine, 1, 0)
    within = flags
    for shift in (1, 2, 4, 8, 16, 32, 64):
        within = within + jnp.where(lane >= shift, pltpu.roll(within, shift, 1), 0)
    totals = jnp.broadcast_to(jnp.sum(flags, axis=1, keepdims=True), (rows, 128))
    before = totals
    for shift in (1, 2, 4, 8, 16, 32):
        before = before + jnp.where(row >= shift, pltpu.roll(before, shift, 0), 0)
    slot = jnp.where(mine, within - flags + before - totals, -1)
    src_dev, dst_dev = src // 16, dst // 16

    first = jnp.zeros((SLOTS, 128), jnp.int32)
    second = jnp.zeros((SLOTS, 128), jnp.int32)
    for index in range(rows):
        hit = slot[index : index + 1, :] == lane_a[:SLOTS]
        first = first + jnp.where(hit, src_dev[index : index + 1, :], 0)
        second = second + jnp.where(hit, dst_dev[index : index + 1, :], 0)
    ends = jnp.sum(jnp.concatenate([first, second], axis=0).T, axis=0, keepdims=True)
    lines = []
    for axis in range(3):
        line, place = line_and_place(ends, axis)
        lines.append(line * 4 + place)
    count = jnp.sum(flags, axis=(0, 1), keepdims=True)
    lines.append(jnp.broadcast_to(count, (1, 128)))
    lines.append(jnp.zeros((1, 128), jnp.int32))
    plan_ref[3:8, :] = jnp.concatenate(lines, axis=0)

    z, x, y, _ = coordinates(me)
    tables = []
    for axis in range(3):
        line, place = line_and_place(own, axis)
        _, my_place = line_and_place(me, axis)
        line = jnp.where(place == my_place, line, -1)
        start, stride = ((z, 8), (x, 2), (y, 32))[axis]
        blocks = []
        for other in range(4):
            source = me + (other - start) * stride
            local = jnp.where(src_dev == source, src % 16, 0) + jnp.where(dst_dev == source, dst % 16, 0)
            total = jnp.zeros((32, 128), jnp.int32)
            for index in range(rows):
                hit = line[index : index + 1, :] == lane_a[:32]
                total = total + jnp.where(hit, local[index : index + 1, :], 0)
            blocks.append(total)
        tables.append(jnp.sum(jnp.concatenate(blocks, axis=0).T, axis=0, keepdims=True))
    plan_ref[0:3, :] = jnp.concatenate(tables, axis=0)


def cross_spectra(into, plan, cross, slot, tile, axes):
    width = len(axes) * PIECE
    for index, axis in enumerate(axes):
        a = into[index, plan[3 + axis, slot]].astype(F32)
        b = into[index, plan[3 + axis, SLOTS + slot]].astype(F32)
        ar, ai, br, bi = a[:BLK], a[BLK:], b[:BLK], b[BLK:]
        left = index * PIECE
        for pair in range(BLK // 2):
            reals, imags = [], []
            for i in (2 * pair, 2 * pair + 1):
                xr, xi = ar[i : i + 1, :], ai[i : i + 1, :]
                reals.append(xr * br + xi * bi)
                imags.append(xi * br - xr * bi)
            at = tile * 64 + pair * 16
            cross[at : at + 16, left : left + PIECE] = jnp.concatenate(reals, axis=0).astype(BF16)
            cross[at : at + 16, width + left : width + left + PIECE] = jnp.concatenate(
                imags, axis=0
            ).astype(BF16)


def axes_of(part):
    return [piece % 3 for piece in range(CUTS[part], CUTS[part + 1])]


def exchange_kernel(
    strain_ref, taps_hbm, tiles_hbm, owner_hbm, basis_hbm, base_ref, lag0_ref, lag1_ref, lag2_ref,
    late_ref, partial_ref, plan_out_ref,
    raw, taps_ref, tiles_ref, owner_ref, basis, base, lag0, lag1, lag2, band, plan_vector, plan, send, recv, acc,
    gathered0, gathered1, gathered2, gathered3, gathered4, gathered5, gathered6, gathered7,
    out0, out1, out2, out3, in0, in1, in2, cross0, cross1, cross2, first_sums, partial,
    raw_sem, small_sem, base_sem, lag_sem, plan_sem, plan_out_sem, send_sem, recv_sem,
    line_sem, gather_sem, out_sem, in_sem, own_sem, partial_sem, plane_sem,
):
    grp, dev = lax.axis_index("grp"), lax.axis_index("dev")
    me = grp * MEMBERS + dev
    chip, core = dev // 2, dev % 2
    zc, xc = chip // 4, chip % 4

    def turned(offset):
        return jnp.where(core == 0, offset, (4 - offset) % 4)

    def at(z, x, c):
        return z % 4 * 8 + x % 4 * 2 + c

    def chip_at(offset):
        return (zc + turned(offset // 4)) % 4 * 4 + (xc + turned(offset % 4)) % 4

    def raw_copy(offset):
        to_chip = chip_at(offset)
        return pltpu.make_async_copy(
            strain_ref.at[:, pl.ds(pl.multiple_of(to_chip * 256, 256), 256)],
            raw.at[to_chip], raw_sem.at[to_chip],
        )

    def fetch(step, _):
        raw_copy(step * 7 % 16).start()
        return 0

    small = ((taps_hbm, taps_ref), (basis_hbm, basis), (tiles_hbm, tiles_ref))
    small = small + ((owner_hbm, owner_ref),)
    small_copies = [
        pltpu.make_async_copy(source, into, small_sem.at[index])
        for index, (source, into) in enumerate(small)
    ]
    for copy in small_copies:
        copy.start()
    lax.fori_loop(0, 16, fetch, 0)
    def base_copy(plane):
        return pltpu.make_async_copy(base_ref.at[plane], base.at[plane], base_sem.at[plane])

    lag_copies = [
        pltpu.make_async_copy(lag0_ref, lag0, lag_sem.at[0]),
        pltpu.make_async_copy(lag1_ref, lag1, lag_sem.at[1]),
        pltpu.make_async_copy(lag2_ref, lag2, lag_sem.at[2]),
    ]

    barrier = pltpu.get_barrier_semaphore()

    def greet(step, _):
        pl.semaphore_signal(
            barrier, inc=1, device_id=(grp, (dev + step) % MEMBERS), device_id_type=MESH
        )
        return 0

    lax.fori_loop(1, MEMBERS, greet, 0)
    for step in range(1, GROUPS):
        pl.semaphore_signal(
            barrier, inc=1, device_id=((grp + step) % GROUPS, dev), device_id_type=MESH
        )
    small_copies[0].wait()
    small_copies[1].wait()
    band[...] = make_band(dev, taps_ref[...])
    pl.semaphore_wait(barrier, MEMBERS - 1 + GROUPS - 1)

    def samples_to(to):
        return pltpu.make_async_remote_copy(
            src_ref=send.at[to], dst_ref=recv.at[dev], send_sem=send_sem.at[to],
            recv_sem=recv_sem.at[dev], device_id=(grp, to), device_id_type=MESH,
        )

    def decimate(pair, _):
        results = []
        for index in range(2):
            offset = (pair * 2 + index) * 7 % 16
            raw_copy(offset).wait()
            to_chip = chip_at(offset)
            result = filtered(band, raw.at[to_chip]).astype(BF16)
            halves = jnp.dot(basis[...], result, preferred_element_type=F32)
            results.append((to_chip, (halves[:RANK] + halves[RANK:]).astype(BF16)))
        @pl.when(pair % 2 == 1)
        def _():
            base_copy((zc + pair // 2) % 4).start()

        for to_chip, result in results:
            for half in range(2):
                send[to_chip * 2 + half] = result[:, half * CH : (half + 1) * CH]
                to = to_chip * 2 + half

                @pl.when(to != dev)
                def _():
                    samples_to(to).start()

        return 0

    lax.fori_loop(0, 8, decimate, 0)
    for copy in lag_copies:
        copy.start()
    recv[dev] = send[dev]
    for step in range(1, GROUPS):
        pl.semaphore_signal(
            plane_sem, inc=1, device_id=((grp + step) % GROUPS, dev), device_id_type=MESH
        )
    acc[...] = jnp.zeros_like(acc)

    def transform(step, _):
        plane = (zc + step) % 4
        first = plane * 8
        for index in range(8):
            source = first + index

            @pl.when(source != dev)
            def _():
                pltpu.make_async_remote_copy(
                    src_ref=send.at[source], dst_ref=recv.at[source],
                    send_sem=send_sem.at[source], recv_sem=recv_sem.at[source],
                    device_id=(grp, source), device_id_type=MESH,
                ).wait_recv()

        base_copy(plane).wait()
        samples = recv[pl.ds(first, 8)].reshape(8 * RANK, CH)
        acc[...] += lax.dot_general(
            samples, base[plane], (((0,), (0,)), ((), ())), preferred_element_type=F32
        )
        return 0

    lax.fori_loop(0, 4, transform, 0)

    real, imag = acc[:, :NF], acc[:, NF:]
    power = real * real + imag * imag
    level = jnp.mean(power, axis=1, keepdims=True)
    scale = lax.rsqrt(power + level + 1e-06)
    outs, ins = (out0, out1, out2, out3), (in0, in1, in2, late_ref)
    crosses, lags = (cross0, cross1, cross2), (lag0, lag1, lag2)
    gathered = (gathered0, gathered1, gathered2, gathered3)
    gathered = gathered + (gathered4, gathered5, gathered6, gathered7)
    pl.semaphore_wait(plane_sem, GROUPS - 1)
    for piece in range(PIECES):
        line, place = line_and_place(me, piece % 3)
        bins = slice(piece * PIECE, (piece + 1) * PIECE)
        factor = scale[:, bins]
        parts = (acc[:, bins] * factor, acc[:, NF + piece * PIECE : NF + (piece + 1) * PIECE] * factor)
        gathered[piece][place] = jnp.concatenate(
            [half.reshape(16, BLK, PIECE) for half in parts], axis=1
        ).astype(BF16)
        for step in (1, 3, 2):
            to = device_of(line, (place + step) % 4, piece % 3)
            pltpu.make_async_remote_copy(
                src_ref=gathered[piece].at[place], dst_ref=gathered[piece].at[place],
                send_sem=line_sem.at[piece], recv_sem=gather_sem.at[piece],
                device_id=(to // MEMBERS, to % MEMBERS), device_id_type=MESH,
            ).start()

    def select(piece, to_line, out):
        axis = piece % 3
        for place in range(4):
            out[place] = gathered[piece][place, plan[axis, 32 * place + to_line]]

    def shifted(start, offset):
        return lax.rem(start + jnp.where(core == 0, offset, 4 - offset), 4)

    z_at, x_at = ([shifted(start, offset) for offset in range(4)] for start in (zc, xc))
    mate = 1 - core

    def emit(piece, part):
        axis, index = piece % 3, piece - CUTS[part]
        line, _ = line_and_place(me, axis)
        second_at = z_at if axis == 1 else x_at

        def eight(turn, _):
            step = lax.rem(turn + 1, 4)
            first = shifted(zc if axis == 2 else grp, step)
            for offset in (1, 3, 2, 0):
                second = second_at[offset]
                for cross in range(2):
                    to_core = mate if cross else core
                    if axis == 0:
                        to_grp, to_dev = first, zc * 8 + second * 2 + to_core
                    elif axis == 1:
                        to_grp, to_dev = first, second * 8 + xc * 2 + to_core
                    else:
                        to_grp, to_dev = grp, first * 8 + second * 2 + to_core
                    to_line = first * 8 + second * 2 + to_core
                    slot = step * 8 + (offset * 2 + cross)

                    def send_one(to_grp=to_grp, to_dev=to_dev, to_line=to_line, slot=slot):
                        out = outs[part].at[index, slot]
                        select(piece, to_line, out)
                        pltpu.make_async_remote_copy(
                            src_ref=out, dst_ref=ins[part].at[index, pl.ds(line * 4, 4)],
                            send_sem=out_sem.at[part], recv_sem=in_sem.at[part],
                            device_id=(to_grp, to_dev), device_id_type=MESH,
                        ).start()

                    if offset == 0 and cross == 0:
                        pl.when(step != 0)(send_one)
                    else:
                        send_one()
            return 0

        lax.fori_loop(0, 4, eight, 0)
        select(piece, line, outs[part].at[index, 0])
        return pltpu.make_async_copy(
            outs[part].at[index, 0], ins[part].at[index, pl.ds(line * 4, 4)], own_sem.at[piece]
        )

    for copy in small_copies[2:]:
        copy.wait()
    tile_rows = [stack_rows([tiles_ref[side : side + 1, :]], 40, 0) for side in range(2)]
    owner_rows = stack_rows([owner_ref[...].reshape(1, -1)], 40, -1)
    make_plan(me, *tile_rows, owner_rows, plan_vector)
    plan_copy = pltpu.make_async_copy(plan_vector, plan, plan_sem)
    plan_copy.start()
    plan_out = pltpu.make_async_copy(plan_vector, plan_out_ref, plan_out_sem)
    plan_out.start()
    plan_copy.wait()
    own_copies = []
    for part in range(EARLY + 1):
        for piece in range(CUTS[part], CUTS[part + 1]):
            others = gathered[piece].at[pl.ds(0, 3)]
            pltpu.make_async_copy(others, others, gather_sem.at[piece]).wait()
            own_copies.append(emit(piece, part))
            own_copies[piece].start()

    def drain(step, _):
        samples_to((dev + step) % MEMBERS).wait_send()
        return 0

    lax.fori_loop(1, MEMBERS, drain, 0)
    def await_part(part):
        for piece in range(CUTS[part], CUTS[part + 1]):
            own_copies[piece].wait()
        others = ins[part].at[:, pl.ds(0, DEVICES - 4)]
        pltpu.make_async_copy(others, others, in_sem.at[part]).wait()

    def tiles_of(part):
        def one(group, _):
            for tile in range(TILES):
                cross_spectra(ins[part], plan, crosses[part], group * TILES + tile, tile, axes_of(part))
            lagged = jnp.dot(crosses[part][...], lags[part][...], preferred_element_type=F32)
            lagged = lagged.reshape(TILES, BLK, BLK, NLAG)
            rows = pl.ds(group * TILES, TILES)
            if part > 0:
                lagged = lagged + first_sums[rows]
            if part < EARLY - 1:
                first_sums[rows] = lagged
            else:
                partial[rows] = lagged.astype(BF16)
                pltpu.make_async_copy(partial.at[rows], partial_ref.at[rows], partial_sem).start()
            return 0

        lax.fori_loop(0, SLOTS // TILES, one, 0)

    for copy in lag_copies:
        copy.wait()
    for part in range(EARLY):
        await_part(part)
        tiles_of(part)
    pltpu.make_async_copy(partial, partial_ref, partial_sem).wait()
    plan_out.wait()
    for part in range(EARLY + 1):
        sent = outs[part].at[:, pl.ds(0, MEMBERS - 1)]
        pltpu.make_async_copy(sent, sent, out_sem.at[part]).wait()
    await_part(EARLY)
    for piece in range(PIECES):
        others = gathered[piece].at[pl.ds(0, 3)]
        pltpu.make_async_copy(others, others, line_sem.at[piece]).wait()


def late_kernel(
    plan_ref, late_ref, partial_ref, lag_ref, out_ref,
    late, lag, partial, total, cross, late_sem, lag_sem, in_sem, out_sem,
):
    count = plan_ref[6, 0]
    pieces = 4
    size = DEVICES // pieces
    late_copies = [
        pltpu.make_async_copy(
            late_ref.at[:, pl.ds(size * index, size)], late.at[:, pl.ds(size * index, size)],
            late_sem.at[index],
        )
        for index in range(pieces)
    ]
    lag_copy = pltpu.make_async_copy(lag_ref, lag, lag_sem)

    def rows(group):
        return pl.ds(group * TILES, TILES)

    def load(group):
        return pltpu.make_async_copy(
            partial_ref.at[rows(group)], partial.at[rows(group)], in_sem.at[group]
        )

    for copy in late_copies:
        copy.start()
    lag_copy.start()

    def fetch(group, _):
        load(group).start()
        return 0

    lax.fori_loop(0, SLOTS // TILES, fetch, 0)
    for copy in late_copies:
        copy.wait()
    lag_copy.wait()

    def one(group, _):
        load(group).wait()

        @pl.when(group * TILES < count)
        def _():
            for tile in range(TILES):
                cross_spectra(late, plan_ref, cross, group * TILES + tile, tile, axes_of(EARLY))
            lagged = jnp.dot(cross[...], lag[...], preferred_element_type=F32)
            lagged = lagged + partial[rows(group)].astype(F32).reshape(lagged.shape)
            index = lax.broadcasted_iota(jnp.int32, lagged.shape, 0) // 64 + group * TILES
            total[rows(group)] = jnp.where(index < count, lagged, 0.0).reshape(TILES, BLK, BLK, NLAG)

        @pl.when(group * TILES >= count)
        def _():
            total[rows(group)] = jnp.zeros((TILES, BLK, BLK, NLAG), F32)

        pltpu.make_async_copy(total.at[rows(group)], out_ref.at[rows(group)], out_sem).start()
        return 0

    lax.fori_loop(0, SLOTS // TILES, one, 0)
    pltpu.make_async_copy(total, out_ref, out_sem).wait()


def per_device(strain, taps, tiles, owner):
    hbm = pl.BlockSpec(memory_space=pl.ANY)
    lag = lag_table()
    basis, rows = base_tables()
    lags = [
        lag.reshape(2, PIECES, PIECE, NLAG)[:, CUTS[part] : CUTS[part + 1]].reshape(-1, NLAG)
        for part in range(EARLY + 1)
    ]
    groups = SLOTS // TILES
    late, partial, plan = pl.pallas_call(
        exchange_kernel,
        out_shape=(
            jax.ShapeDtypeStruct((COUNTS[EARLY], DEVICES, 2 * BLK, PIECE), BF16),
            jax.ShapeDtypeStruct((SLOTS, BLK, BLK, NLAG), BF16),
            jax.ShapeDtypeStruct((8, 128), jnp.int32),
        ),
        in_specs=[hbm] * (6 + EARLY),
        out_specs=(hbm, hbm, hbm),
        scratch_shapes=[
            pltpu.VMEM((16, 960, 256), BF16),
            pltpu.VMEM((1, NTAP), BF16),
            pltpu.VMEM((2, 4160), jnp.int32),
            pltpu.VMEM((4160,), jnp.int32),
            pltpu.VMEM((2 * RANK, EXT), BF16),
            pltpu.VMEM((4, 8 * RANK, 2 * NF), BF16),
            *[pltpu.VMEM((2 * count * PIECE, NLAG), BF16) for count in COUNTS[:EARLY]],
            pltpu.VMEM((EXT, 960), BF16),
            pltpu.VMEM((8, 128), jnp.int32),
            pltpu.SMEM((8, 128), jnp.int32),
            pltpu.VMEM((MEMBERS, RANK, CH), BF16),
            pltpu.VMEM((MEMBERS, RANK, CH), BF16),
            pltpu.VMEM((CH, 2 * NF), F32),
            *[pltpu.VMEM((4, 16, 2 * BLK, PIECE), BF16) for _ in range(PIECES)],
            *[pltpu.VMEM((count, MEMBERS, 4, 2 * BLK, PIECE), BF16) for count in COUNTS],
            *[pltpu.VMEM((count, DEVICES, 2 * BLK, PIECE), BF16) for count in COUNTS[:EARLY]],
            *[pltpu.VMEM((TILES * 64, 2 * count * PIECE), BF16) for count in COUNTS[:EARLY]],
            pltpu.VMEM((SLOTS, BLK, BLK, NLAG), F32),
            pltpu.VMEM((SLOTS, BLK, BLK, NLAG), BF16),
            pltpu.SemaphoreType.DMA((16,)),
            pltpu.SemaphoreType.DMA((4,)),
            pltpu.SemaphoreType.DMA((4,)),
            pltpu.SemaphoreType.DMA((EARLY,)),
            pltpu.SemaphoreType.DMA,
            pltpu.SemaphoreType.DMA,
            pltpu.SemaphoreType.DMA((MEMBERS,)),
            pltpu.SemaphoreType.DMA((MEMBERS,)),
            pltpu.SemaphoreType.DMA((PIECES,)),
            pltpu.SemaphoreType.DMA((PIECES,)),
            pltpu.SemaphoreType.DMA((EARLY + 1,)),
            pltpu.SemaphoreType.DMA((EARLY + 1,)),
            pltpu.SemaphoreType.DMA((PIECES,)),
            pltpu.SemaphoreType.DMA,
            pltpu.SemaphoreType.REGULAR,
        ],
        compiler_params=pltpu.CompilerParams(
            collective_id=0, has_side_effects=True, vmem_limit_bytes=60 * 2**20
        ),
    )(
        strain.T, taps[None, :], tiles.T, owner, jnp.asarray(basis), jnp.asarray(rows.reshape(4, 8 * RANK, 2 * NF)),
        *[jnp.asarray(part) for part in lags[:EARLY]],
    )

    return pl.pallas_call(
        late_kernel,
        out_shape=jax.ShapeDtypeStruct((SLOTS, BLK, BLK, NLAG), F32),
        in_specs=[pl.BlockSpec(memory_space=pltpu.SMEM), hbm, hbm, hbm],
        out_specs=hbm,
        scratch_shapes=[
            pltpu.VMEM((COUNTS[EARLY], DEVICES, 2 * BLK, PIECE), BF16),
            pltpu.VMEM((2 * COUNTS[EARLY] * PIECE, NLAG), BF16),
            pltpu.VMEM((SLOTS, BLK, BLK, NLAG), BF16),
            pltpu.VMEM((SLOTS, BLK, BLK, NLAG), F32),
            pltpu.VMEM((TILES * 64, 2 * COUNTS[EARLY] * PIECE), BF16),
            pltpu.SemaphoreType.DMA((4,)),
            pltpu.SemaphoreType.DMA,
            pltpu.SemaphoreType.DMA((groups,)),
            pltpu.SemaphoreType.DMA,
        ],
        compiler_params=pltpu.CompilerParams(vmem_limit_bytes=60 * 2**20),
    )(plan, late, partial, jnp.asarray(lags[EARLY]))


def solution(mesh):
    return jax.shard_map(
        per_device,
        mesh=mesh,
        in_specs=(P("grp", "dev"), P(), P(), P()),
        out_specs=P(("grp", "dev"), None, None, None),
        check_vma=False,
    )
```

```python
import functools
import math

import jax
import jax.numpy as jnp
import ml_dtypes
import numpy as np
from jax import lax
from jax.experimental import pallas as pl
from jax.experimental.pallas import tpu as pltpu
from jax.sharding import PartitionSpec as P

NT = 6144
NF = 1024
F0 = 32
NLAG = 384
NTAP = 64
DECIM = 5
BLK = 8
MEMBERS = 32
GROUPS = 4
DEVICES = 128
COLS = NT // MEMBERS
EXT = 208
USED = 205
RANK = 96
STRETCHES = ((0, 64), (48, 120), (96, 168), (144, 208))
PARTS = 8
CH = 128
SLOTS = 64
PIECE = 128
PIECES = NF // PIECE
CUTS = (0, 4, 6, 7, 8)
COUNTS = (4, 2, 1, 1)
EARLY = len(COUNTS) - 1
TILES = 4
LATE_TILES = 8
MESH = pl.DeviceIdType.MESH
F32 = jnp.float32
BF16 = jnp.bfloat16


def trig(phase, factor=1.0):
    angle = np.float32(2.0 * math.pi / NT) * phase.astype(np.float32)
    angle = angle.astype(np.float64)
    return np.cos(angle) * factor, -np.sin(angle) * factor


def base_tables():
    samples = np.arange(USED)
    width = (F0 + NF) / NT
    steps = samples[1:] * (USED - samples[1:]) / 2
    diagonal = ((USED - 1) / 2 - samples) ** 2 * math.cos(2 * math.pi * width)
    _, vectors = np.linalg.eigh(np.diag(diagonal) + np.diag(steps, 1) + np.diag(steps, -1))
    basis = vectors[:, ::-1][:, :RANK].T
    half = basis[:, : USED // 2]
    basis = basis * np.sign(np.take_along_axis(half, np.abs(half).argmax(axis=1)[:, None], axis=1))

    def table(place):
        rows = place * COLS + samples
        angle = 2.0 * math.pi / NT * (rows[:, None] * (F0 + np.arange(NF))[None, :] % NT)
        return np.concatenate([np.cos(angle), -np.sin(angle)], axis=1)

    assert np.abs(basis.T @ (basis @ table(0)) - table(0)).max() < 1e-10
    rows = np.concatenate([basis @ table(place) for place in range(MEMBERS)], axis=0)
    basis = np.pad(basis, ((0, 0), (0, EXT - USED)))
    high = basis.astype(ml_dtypes.bfloat16)
    low = (basis - high.astype(np.float64)).astype(ml_dtypes.bfloat16)
    return np.concatenate([high, low], axis=0), rows.astype(ml_dtypes.bfloat16)


def lag_table():
    lags = (np.arange(NLAG) - NLAG // 2) % NT
    phase = (F0 + np.arange(NF))[:, None] * lags[None, :] % NT
    real, imag = trig(phase, 1.0 / math.sqrt(NF))
    return np.concatenate([real, imag], axis=0).astype(ml_dtypes.bfloat16)


def nt_dot(a, b):
    return lax.dot_general(a, b, (((1,), (1,)), ((), ())), preferred_element_type=F32)


def stack_rows(pieces, rows, fill):
    width = sum(piece.shape[1] for piece in pieces)
    extra = jnp.full((1, rows * 128 - width), fill, jnp.int32)
    line = jnp.concatenate([*pieces, extra], axis=1)
    return jnp.concatenate(
        [line[:, index * 128 : (index + 1) * 128] for index in range(rows)], axis=0
    )


def make_band(member, taps):
    tap = lax.broadcasted_iota(jnp.int32, (NTAP, 1024), 0)
    lane = lax.broadcasted_iota(jnp.int32, (NTAP, 1024), 1)
    place = (lane == (1024 - tap) % 1024).astype(F32).astype(BF16)
    taps = jnp.broadcast_to(taps.astype(F32), (8, NTAP)).astype(BF16)
    line = jnp.dot(taps, place, preferred_element_type=F32)
    first_rows = pltpu.roll(line, 0, 1, stride=DECIM, stride_axis=0)
    band = jnp.concatenate(
        [pltpu.roll(first_rows, 8 * DECIM * index, 1) for index in range(EXT // 8)], axis=0
    )
    row = lax.broadcasted_iota(jnp.int32, (EXT, 1024), 0)
    limit = jnp.where(member == MEMBERS - 1, COLS, USED)
    return jnp.where(row < limit, band, 0.0)[:, :960].astype(BF16)


def filtered(band, raw):
    count = raw.shape[0]
    sums = [
        jnp.dot(
            band[low:high, 256 * index : min(256 * (index + 1), count)],
            raw[256 * index : min(256 * (index + 1), count)],
            preferred_element_type=F32,
        )
        for index, (low, high) in enumerate(STRETCHES)
    ]
    pieces = []
    done = 0
    for index, (low, high) in enumerate(STRETCHES):
        end = STRETCHES[index + 1][0] if index + 1 < len(STRETCHES) else high
        pieces.append(sums[index][done - low : end - low])
        if end < high:
            after = STRETCHES[index + 1][0]
            pieces.append(sums[index][end - low :] + sums[index + 1][: high - after])
        done = high
    return jnp.concatenate(pieces, axis=0)


def coordinates(device):
    return device // 8 % 4, device // 2 % 4, device // 32, device % 2


def line_and_place(device, axis):
    z, x, y, c = coordinates(device)
    if axis == 0:
        return y * 8 + x * 2 + c, z
    if axis == 1:
        return y * 8 + z * 2 + c, x
    return z * 8 + x * 2 + c, y


def device_of(line, place, axis):
    first, second, c = line // 8, line // 2 % 4, line % 2
    if axis == 0:
        return first * 32 + place * 8 + second * 2 + c
    if axis == 1:
        return first * 32 + second * 8 + place * 2 + c
    return place * 32 + line


def make_plan(me, src, dst, own, plan_ref):
    rows = src.shape[0]
    mine = own == me
    lane_a = lax.broadcasted_iota(jnp.int32, (128, 128), 0)
    lane = lax.broadcasted_iota(jnp.int32, (rows, 128), 1)
    row = lax.broadcasted_iota(jnp.int32, (rows, 128), 0)
    flags = jnp.where(mine, 1, 0)
    within = flags
    for shift in (1, 2, 4, 8, 16, 32, 64):
        within = within + jnp.where(lane >= shift, pltpu.roll(within, shift, 1), 0)
    totals = jnp.broadcast_to(jnp.sum(flags, axis=1, keepdims=True), (rows, 128))
    before = totals
    for shift in (1, 2, 4, 8, 16, 32):
        before = before + jnp.where(row >= shift, pltpu.roll(before, shift, 0), 0)
    slot = jnp.where(mine, within - flags + before - totals, -1)
    src_dev, dst_dev = src // 16, dst // 16

    first = jnp.zeros((SLOTS, 128), jnp.int32)
    second = jnp.zeros((SLOTS, 128), jnp.int32)
    for index in range(rows):
        hit = slot[index : index + 1, :] == lane_a[:SLOTS]
        first = first + jnp.where(hit, src_dev[index : index + 1, :], 0)
        second = second + jnp.where(hit, dst_dev[index : index + 1, :], 0)
    ends = jnp.sum(jnp.concatenate([first, second], axis=0).T, axis=0, keepdims=True)
    lines = []
    for axis in range(3):
        line, place = line_and_place(ends, axis)
        lines.append(line * 4 + place)
    count = jnp.sum(flags, axis=(0, 1), keepdims=True)
    lines.append(jnp.broadcast_to(count, (1, 128)))
    plan_ref[12:16, :] = jnp.concatenate(lines, axis=0)

    z, x, y, _ = coordinates(me)

    def wanted(entry, _):
        axis, place = entry // 4, entry % 4
        source = jnp.where(
            axis == 0, me + (place - z) * 8, jnp.where(axis == 1, me + (place - x) * 2, me + (place - y) * 32)
        )
        local = jnp.where(src_dev == source, src % 16, 0) + jnp.where(dst_dev == source, dst % 16, 0)
        blocks = jnp.zeros((128, 128), jnp.int32)
        for index in range(rows):
            hit = own[index : index + 1, :] == lane_a
            blocks = blocks + jnp.where(hit, local[index : index + 1, :], 0)
        plan_ref[pl.ds(entry, 1), :] = jnp.sum(blocks.T, axis=0, keepdims=True)
        return 0

    lax.fori_loop(0, 12, wanted, 0)


def cross_spectra(into, plan, cross, slot, tile, axes):
    width = len(axes) * PIECE
    for index, axis in enumerate(axes):
        a = into[index, plan[12 + axis, slot]].astype(F32)
        b = into[index, plan[12 + axis, SLOTS + slot]].astype(F32)
        ar, ai, br, bi = a[:BLK], a[BLK:], b[:BLK], b[BLK:]
        left = index * PIECE
        for pair in range(BLK // 2):
            reals, imags = [], []
            for i in (2 * pair, 2 * pair + 1):
                xr, xi = ar[i : i + 1, :], ai[i : i + 1, :]
                reals.append(xr * br + xi * bi)
                imags.append(xi * br - xr * bi)
            at = tile * 64 + pair * 16
            cross[at : at + 16, left : left + PIECE] = jnp.concatenate(reals, axis=0).astype(BF16)
            cross[at : at + 16, width + left : width + left + PIECE] = jnp.concatenate(
                imags, axis=0
            ).astype(BF16)


def axes_of(part):
    return [piece % 3 for piece in range(CUTS[part], CUTS[part + 1])]


def exchange_kernel(
    strain_ref, taps_hbm, tiles_hbm, owner_hbm, basis_hbm, base_ref, lag0_ref, lag1_ref, lag2_ref,
    late_ref, partial_ref, plan_out_ref,
    raw, taps_ref, tiles_ref, owner_ref, basis, base, lag0, lag1, lag2, band, plan_vector, plan, send, recv, acc,
    gathered0, gathered1, gathered2, gathered3, gathered4, gathered5, gathered6, gathered7,
    out0, out1, out2, out3, in0, in1, in2, cross0, cross1, cross2, first_sums, partial,
    raw_sem, small_sem, base_sem, lag_sem, plan_sem, plan_out_sem, send_sem, recv_sem,
    line_sem, gather_sem, out_sem, in_sem, own_sem, partial_sem, plane_sem,
):
    grp, dev = lax.axis_index("grp"), lax.axis_index("dev")
    me = grp * MEMBERS + dev
    chip, core = dev // 2, dev % 2
    zc, xc = chip // 4, chip % 4

    def turned(offset):
        return jnp.where(core == 0, offset, (4 - offset) % 4)

    def at(z, x, c):
        return z % 4 * 8 + x % 4 * 2 + c

    def chip_at(offset):
        return (zc + turned(offset // 4)) % 4 * 4 + (xc + turned(offset % 4)) % 4

    def raw_copy(offset):
        to_chip = chip_at(offset)
        return pltpu.make_async_copy(
            strain_ref.at[:, pl.ds(pl.multiple_of(to_chip * 256, 256), 256)],
            raw.at[to_chip], raw_sem.at[to_chip],
        )

    def fetch(step, _):
        raw_copy(step * 7 % 16).start()
        return 0

    small = ((taps_hbm, taps_ref), (basis_hbm, basis), (tiles_hbm, tiles_ref))
    small = small + ((owner_hbm, owner_ref),)
    small_copies = [
        pltpu.make_async_copy(source, into, small_sem.at[index])
        for index, (source, into) in enumerate(small)
    ]
    for copy in small_copies:
        copy.start()
    lax.fori_loop(0, 16, fetch, 0)
    def base_copy(plane):
        return pltpu.make_async_copy(base_ref.at[plane], base.at[plane], base_sem.at[plane])

    lag_copies = [
        pltpu.make_async_copy(lag0_ref, lag0, lag_sem.at[0]),
        pltpu.make_async_copy(lag1_ref, lag1, lag_sem.at[1]),
        pltpu.make_async_copy(lag2_ref, lag2, lag_sem.at[2]),
    ]

    barrier = pltpu.get_barrier_semaphore()

    def greet(step, _):
        pl.semaphore_signal(
            barrier, inc=1, device_id=(grp, (dev + step) % MEMBERS), device_id_type=MESH
        )
        return 0

    lax.fori_loop(1, MEMBERS, greet, 0)
    for step in range(1, GROUPS):
        pl.semaphore_signal(
            barrier, inc=1, device_id=((grp + step) % GROUPS, dev), device_id_type=MESH
        )
    small_copies[0].wait()
    small_copies[1].wait()
    band[...] = make_band(dev, taps_ref[...])
    pl.semaphore_wait(barrier, MEMBERS - 1 + GROUPS - 1)

    def samples_to(to):
        return pltpu.make_async_remote_copy(
            src_ref=send.at[to], dst_ref=recv.at[dev], send_sem=send_sem.at[to],
            recv_sem=recv_sem.at[dev], device_id=(grp, to), device_id_type=MESH,
        )

    def decimate(pair, _):
        results = []
        for index in range(2):
            offset = (pair * 2 + index) * 7 % 16
            raw_copy(offset).wait()
            to_chip = chip_at(offset)
            result = filtered(band, raw.at[to_chip]).astype(BF16)
            halves = jnp.dot(basis[...], result, preferred_element_type=F32)
            results.append((to_chip, (halves[:RANK] + halves[RANK:]).astype(BF16)))
        @pl.when(pair % 2 == 1)
        def _():
            base_copy((zc + pair // 2) % 4).start()

        for to_chip, result in results:
            for half in range(2):
                send[to_chip * 2 + half] = result[:, half * CH : (half + 1) * CH]
                to = to_chip * 2 + half

                @pl.when(to != dev)
                def _():
                    samples_to(to).start()

        return 0

    lax.fori_loop(0, 8, decimate, 0)
    for copy in lag_copies:
        copy.start()
    recv[dev] = send[dev]
    for step in range(1, GROUPS):
        pl.semaphore_signal(
            plane_sem, inc=1, device_id=((grp + step) % GROUPS, dev), device_id_type=MESH
        )
    acc[...] = jnp.zeros_like(acc)

    def transform(step, _):
        plane = (zc + step) % 4
        first = plane * 8
        for index in range(8):
            source = first + index

            @pl.when(source != dev)
            def _():
                pltpu.make_async_remote_copy(
                    src_ref=send.at[source], dst_ref=recv.at[source],
                    send_sem=send_sem.at[source], recv_sem=recv_sem.at[source],
                    device_id=(grp, source), device_id_type=MESH,
                ).wait_recv()

        base_copy(plane).wait()
        samples = recv[pl.ds(first, 8)].reshape(8 * RANK, CH)
        acc[...] += lax.dot_general(
            samples, base[plane], (((0,), (0,)), ((), ())), preferred_element_type=F32
        )
        return 0

    lax.fori_loop(0, 4, transform, 0)

    real, imag = acc[:, :NF], acc[:, NF:]
    power = real * real + imag * imag
    level = jnp.mean(power, axis=1, keepdims=True)
    scale = lax.rsqrt(power + level + 1e-06)
    outs, ins = (out0, out1, out2, out3), (in0, in1, in2, late_ref)
    crosses, lags = (cross0, cross1, cross2), (lag0, lag1, lag2)
    gathered = (gathered0, gathered1, gathered2, gathered3)
    gathered = gathered + (gathered4, gathered5, gathered6, gathered7)
    pl.semaphore_wait(plane_sem, GROUPS - 1)
    for piece in range(PIECES):
        line, place = line_and_place(me, piece % 3)
        bins = slice(piece * PIECE, (piece + 1) * PIECE)
        factor = scale[:, bins]
        parts = (acc[:, bins] * factor, acc[:, NF + piece * PIECE : NF + (piece + 1) * PIECE] * factor)
        gathered[piece][place] = jnp.concatenate(
            [half.reshape(16, BLK, PIECE) for half in parts], axis=1
        ).astype(BF16)
        for step in (1, 3, 2):
            to = device_of(line, (place + step) % 4, piece % 3)
            pltpu.make_async_remote_copy(
                src_ref=gathered[piece].at[place], dst_ref=gathered[piece].at[place],
                send_sem=line_sem.at[piece], recv_sem=gather_sem.at[piece],
                device_id=(to // MEMBERS, to % MEMBERS), device_id_type=MESH,
            ).start()

    def select(piece, to, out):
        axis = piece % 3
        for place in range(4):
            out[place] = gathered[piece][place, plan[4 * axis + place, to]]

    def shifted(start, offset):
        return lax.rem(start + jnp.where(core == 0, offset, 4 - offset), 4)

    z_at, x_at = ([shifted(start, offset) for offset in range(4)] for start in (zc, xc))
    mate = 1 - core

    def emit(piece, part):
        axis, index = piece % 3, piece - CUTS[part]
        line, _ = line_and_place(me, axis)
        second_at = z_at if axis == 1 else x_at

        def eight(turn, _):
            step = lax.rem(turn + 1, 4)
            first = shifted(zc if axis == 2 else grp, step)
            for offset in (1, 3, 2, 0):
                second = second_at[offset]
                for cross in range(2):
                    to_core = mate if cross else core
                    if axis == 0:
                        to_grp, to_dev = first, zc * 8 + second * 2 + to_core
                    elif axis == 1:
                        to_grp, to_dev = first, second * 8 + xc * 2 + to_core
                    else:
                        to_grp, to_dev = grp, first * 8 + second * 2 + to_core
                    slot = step * 8 + (offset * 2 + cross)

                    def send_one(to_grp=to_grp, to_dev=to_dev, slot=slot):
                        out = outs[part].at[index, slot]
                        select(piece, to_grp * MEMBERS + to_dev, out)
                        pltpu.make_async_remote_copy(
                            src_ref=out, dst_ref=ins[part].at[index, pl.ds(line * 4, 4)],
                            send_sem=out_sem.at[part], recv_sem=in_sem.at[part],
                            device_id=(to_grp, to_dev), device_id_type=MESH,
                        ).start()

                    if offset == 0 and cross == 0:
                        pl.when(step != 0)(send_one)
                    else:
                        send_one()
            return 0

        lax.fori_loop(0, 4, eight, 0)
        select(piece, me, outs[part].at[index, 0])
        return pltpu.make_async_copy(
            outs[part].at[index, 0], ins[part].at[index, pl.ds(line * 4, 4)], own_sem.at[piece]
        )

    for copy in small_copies[2:]:
        copy.wait()
    tile_rows = [stack_rows([tiles_ref[side : side + 1, :]], 40, 0) for side in range(2)]
    owner_rows = stack_rows([owner_ref[...].reshape(1, -1)], 40, -1)
    make_plan(me, *tile_rows, owner_rows, plan_vector)
    plan_copy = pltpu.make_async_copy(plan_vector, plan, plan_sem)
    plan_copy.start()
    plan_out = pltpu.make_async_copy(plan_vector, plan_out_ref, plan_out_sem)
    plan_out.start()
    plan_copy.wait()
    own_copies = []
    for part in range(EARLY + 1):
        for piece in range(CUTS[part], CUTS[part + 1]):
            others = gathered[piece].at[pl.ds(0, 3)]
            pltpu.make_async_copy(others, others, gather_sem.at[piece]).wait()
            own_copies.append(emit(piece, part))
            own_copies[piece].start()

    def drain(step, _):
        samples_to((dev + step) % MEMBERS).wait_send()
        return 0

    lax.fori_loop(1, MEMBERS, drain, 0)
    def await_part(part):
        for piece in range(CUTS[part], CUTS[part + 1]):
            own_copies[piece].wait()
        others = ins[part].at[:, pl.ds(0, DEVICES - 4)]
        pltpu.make_async_copy(others, others, in_sem.at[part]).wait()

    def tiles_of(part):
        def one(group, _):
            for tile in range(TILES):
                cross_spectra(ins[part], plan, crosses[part], group * TILES + tile, tile, axes_of(part))
            lagged = jnp.dot(crosses[part][...], lags[part][...], preferred_element_type=F32)
            lagged = lagged.reshape(TILES, BLK, BLK, NLAG)
            rows = pl.ds(group * TILES, TILES)
            if part > 0:
                lagged = lagged + first_sums[rows]
            if part < EARLY - 1:
                first_sums[rows] = lagged
            else:
                partial[rows] = lagged.astype(BF16)
                pltpu.make_async_copy(partial.at[rows], partial_ref.at[rows], partial_sem).start()
            return 0

        lax.fori_loop(0, SLOTS // TILES, one, 0)

    for copy in lag_copies:
        copy.wait()
    for part in range(EARLY):
        await_part(part)
        tiles_of(part)
    pltpu.make_async_copy(partial, partial_ref, partial_sem).wait()
    plan_out.wait()
    for part in range(EARLY + 1):
        sent = outs[part].at[:, pl.ds(0, MEMBERS - 1)]
        pltpu.make_async_copy(sent, sent, out_sem.at[part]).wait()
    await_part(EARLY)
    for piece in range(PIECES):
        others = gathered[piece].at[pl.ds(0, 3)]
        pltpu.make_async_copy(others, others, line_sem.at[piece]).wait()


def late_kernel(
    plan_ref, late_ref, partial_ref, lag_ref, out_ref,
    late, lag, partial, total, cross, late_sem, lag_sem, in_sem, out_sem,
):
    count = plan_ref[15, 0]
    pieces = 4
    size = DEVICES // pieces
    late_copies = [
        pltpu.make_async_copy(
            late_ref.at[:, pl.ds(size * index, size)], late.at[:, pl.ds(size * index, size)],
            late_sem.at[index],
        )
        for index in range(pieces)
    ]
    lag_copy = pltpu.make_async_copy(lag_ref, lag, lag_sem)

    def rows(group):
        return pl.ds(group * LATE_TILES, LATE_TILES)

    def load(group):
        return pltpu.make_async_copy(
            partial_ref.at[rows(group)], partial.at[rows(group)], in_sem.at[group]
        )

    for copy in late_copies:
        copy.start()
    lag_copy.start()

    def fetch(group, _):
        load(group).start()
        return 0

    lax.fori_loop(0, SLOTS // LATE_TILES, fetch, 0)
    for copy in late_copies:
        copy.wait()
    lag_copy.wait()

    def one(group, _):
        load(group).wait()

        @pl.when(group * LATE_TILES < count)
        def _():
            for tile in range(LATE_TILES):
                cross_spectra(late, plan_ref, cross, group * LATE_TILES + tile, tile, axes_of(EARLY))
            lagged = jnp.dot(cross[...], lag[...], preferred_element_type=F32)
            lagged = lagged + partial[rows(group)].astype(F32).reshape(lagged.shape)
            index = lax.broadcasted_iota(jnp.int32, lagged.shape, 0) // 64 + group * LATE_TILES
            total[rows(group)] = jnp.where(index < count, lagged, 0.0).reshape(LATE_TILES, BLK, BLK, NLAG)

        @pl.when(group * LATE_TILES >= count)
        def _():
            total[rows(group)] = jnp.zeros((LATE_TILES, BLK, BLK, NLAG), F32)

        pltpu.make_async_copy(total.at[rows(group)], out_ref.at[rows(group)], out_sem).start()
        return 0

    lax.fori_loop(0, SLOTS // LATE_TILES, one, 0)
    pltpu.make_async_copy(total, out_ref, out_sem).wait()


def per_device(strain, taps, tiles, owner):
    hbm = pl.BlockSpec(memory_space=pl.ANY)
    lag = lag_table()
    basis, rows = base_tables()
    lags = [
        lag.reshape(2, PIECES, PIECE, NLAG)[:, CUTS[part] : CUTS[part + 1]].reshape(-1, NLAG)
        for part in range(EARLY + 1)
    ]
    late, partial, plan = pl.pallas_call(
        exchange_kernel,
        out_shape=(
            jax.ShapeDtypeStruct((COUNTS[EARLY], DEVICES, 2 * BLK, PIECE), BF16),
            jax.ShapeDtypeStruct((SLOTS, BLK, BLK, NLAG), BF16),
            jax.ShapeDtypeStruct((16, 128), jnp.int32),
        ),
        in_specs=[hbm] * (6 + EARLY),
        out_specs=(hbm, hbm, hbm),
        scratch_shapes=[
            pltpu.VMEM((16, 960, 256), BF16),
            pltpu.VMEM((1, NTAP), BF16),
            pltpu.VMEM((2, 4160), jnp.int32),
            pltpu.VMEM((4160,), jnp.int32),
            pltpu.VMEM((2 * RANK, EXT), BF16),
            pltpu.VMEM((4, 8 * RANK, 2 * NF), BF16),
            *[pltpu.VMEM((2 * count * PIECE, NLAG), BF16) for count in COUNTS[:EARLY]],
            pltpu.VMEM((EXT, 960), BF16),
            pltpu.VMEM((16, 128), jnp.int32),
            pltpu.SMEM((16, 128), jnp.int32),
            pltpu.VMEM((MEMBERS, RANK, CH), BF16),
            pltpu.VMEM((MEMBERS, RANK, CH), BF16),
            pltpu.VMEM((CH, 2 * NF), F32),
            *[pltpu.VMEM((4, 16, 2 * BLK, PIECE), BF16) for _ in range(PIECES)],
            *[pltpu.VMEM((count, MEMBERS, 4, 2 * BLK, PIECE), BF16) for count in COUNTS],
            *[pltpu.VMEM((count, DEVICES, 2 * BLK, PIECE), BF16) for count in COUNTS[:EARLY]],
            *[pltpu.VMEM((TILES * 64, 2 * count * PIECE), BF16) for count in COUNTS[:EARLY]],
            pltpu.VMEM((SLOTS, BLK, BLK, NLAG), F32),
            pltpu.VMEM((SLOTS, BLK, BLK, NLAG), BF16),
            pltpu.SemaphoreType.DMA((16,)),
            pltpu.SemaphoreType.DMA((4,)),
            pltpu.SemaphoreType.DMA((4,)),
            pltpu.SemaphoreType.DMA((EARLY,)),
            pltpu.SemaphoreType.DMA,
            pltpu.SemaphoreType.DMA,
            pltpu.SemaphoreType.DMA((MEMBERS,)),
            pltpu.SemaphoreType.DMA((MEMBERS,)),
            pltpu.SemaphoreType.DMA((PIECES,)),
            pltpu.SemaphoreType.DMA((PIECES,)),
            pltpu.SemaphoreType.DMA((EARLY + 1,)),
            pltpu.SemaphoreType.DMA((EARLY + 1,)),
            pltpu.SemaphoreType.DMA((PIECES,)),
            pltpu.SemaphoreType.DMA,
            pltpu.SemaphoreType.REGULAR,
        ],
        compiler_params=pltpu.CompilerParams(
            collective_id=0, has_side_effects=True, vmem_limit_bytes=60 * 2**20
        ),
    )(
        strain.T, taps[None, :], tiles.T, owner, jnp.asarray(basis), jnp.asarray(rows.reshape(4, 8 * RANK, 2 * NF)),
        *[jnp.asarray(part) for part in lags[:EARLY]],
    )

    return pl.pallas_call(
        late_kernel,
        out_shape=jax.ShapeDtypeStruct((SLOTS, BLK, BLK, NLAG), F32),
        in_specs=[pl.BlockSpec(memory_space=pltpu.SMEM), hbm, hbm, hbm],
        out_specs=hbm,
        scratch_shapes=[
            pltpu.VMEM((COUNTS[EARLY], DEVICES, 2 * BLK, PIECE), BF16),
            pltpu.VMEM((2 * COUNTS[EARLY] * PIECE, NLAG), BF16),
            pltpu.VMEM((SLOTS, BLK, BLK, NLAG), BF16),
            pltpu.VMEM((SLOTS, BLK, BLK, NLAG), F32),
            pltpu.VMEM((LATE_TILES * 64, 2 * COUNTS[EARLY] * PIECE), BF16),
            pltpu.SemaphoreType.DMA((4,)),
            pltpu.SemaphoreType.DMA,
            pltpu.SemaphoreType.DMA((SLOTS // LATE_TILES,)),
            pltpu.SemaphoreType.DMA,
        ],
        compiler_params=pltpu.CompilerParams(vmem_limit_bytes=60 * 2**20),
    )(plan, late, partial, jnp.asarray(lags[EARLY]))


def solution(mesh):
    return jax.shard_map(
        per_device,
        mesh=mesh,
        in_specs=(P("grp", "dev"), P(), P(), P()),
        out_specs=P(("grp", "dev"), None, None, None),
        check_vma=False,
    )
```

```python
import functools
import math

import jax
import jax.numpy as jnp
import ml_dtypes
import numpy as np
from jax import lax
from jax.experimental import pallas as pl
from jax.experimental.pallas import tpu as pltpu
from jax.sharding import PartitionSpec as P

NT = 6144
NF = 1024
F0 = 32
NLAG = 384
NTAP = 64
DECIM = 5
BLK = 8
MEMBERS = 32
GROUPS = 4
DEVICES = 128
COLS = NT // MEMBERS
EXT = 208
USED = 205
RANK = 96
STRETCHES = ((0, 64), (48, 120), (96, 168), (144, 208))
PARTS = 8
CH = 128
SLOTS = 64
PIECE = 128
PIECES = NF // PIECE
CUTS = (0, 4, 6, 7, 8)
COUNTS = (4, 2, 1, 1)
EARLY = len(COUNTS) - 1
TILES = 4
LATE_TILES = 8
MESH = pl.DeviceIdType.MESH
F32 = jnp.float32
BF16 = jnp.bfloat16


def trig(phase, factor=1.0):
    angle = np.float32(2.0 * math.pi / NT) * phase.astype(np.float32)
    angle = angle.astype(np.float64)
    return np.cos(angle) * factor, -np.sin(angle) * factor


def base_tables():
    samples = np.arange(USED)
    width = (F0 + NF) / NT
    steps = samples[1:] * (USED - samples[1:]) / 2
    diagonal = ((USED - 1) / 2 - samples) ** 2 * math.cos(2 * math.pi * width)
    _, vectors = np.linalg.eigh(np.diag(diagonal) + np.diag(steps, 1) + np.diag(steps, -1))
    basis = vectors[:, ::-1][:, :RANK].T
    half = basis[:, : USED // 2]
    basis = basis * np.sign(np.take_along_axis(half, np.abs(half).argmax(axis=1)[:, None], axis=1))

    def table(place):
        rows = place * COLS + samples
        angle = 2.0 * math.pi / NT * (rows[:, None] * (F0 + np.arange(NF))[None, :] % NT)
        return np.concatenate([np.cos(angle), -np.sin(angle)], axis=1)

    assert np.abs(basis.T @ (basis @ table(0)) - table(0)).max() < 1e-10
    rows = np.concatenate([basis @ table(place) for place in range(MEMBERS)], axis=0)
    basis = np.pad(basis, ((0, 0), (0, EXT - USED)))
    high = basis.astype(ml_dtypes.bfloat16)
    low = (basis - high.astype(np.float64)).astype(ml_dtypes.bfloat16)
    return np.concatenate([high, low], axis=0), rows.astype(ml_dtypes.bfloat16)


def lag_table():
    lags = (np.arange(NLAG) - NLAG // 2) % NT
    phase = (F0 + np.arange(NF))[:, None] * lags[None, :] % NT
    real, imag = trig(phase, 1.0 / math.sqrt(NF))
    return np.concatenate([real, imag], axis=0).astype(ml_dtypes.bfloat16)


def nt_dot(a, b):
    return lax.dot_general(a, b, (((1,), (1,)), ((), ())), preferred_element_type=F32)


def stack_rows(pieces, rows, fill):
    width = sum(piece.shape[1] for piece in pieces)
    extra = jnp.full((1, rows * 128 - width), fill, jnp.int32)
    line = jnp.concatenate([*pieces, extra], axis=1)
    return jnp.concatenate(
        [line[:, index * 128 : (index + 1) * 128] for index in range(rows)], axis=0
    )


def make_band(member, taps):
    tap = lax.broadcasted_iota(jnp.int32, (NTAP, 1024), 0)
    lane = lax.broadcasted_iota(jnp.int32, (NTAP, 1024), 1)
    place = (lane == (1024 - tap) % 1024).astype(F32).astype(BF16)
    taps = jnp.broadcast_to(taps.astype(F32), (8, NTAP)).astype(BF16)
    line = jnp.dot(taps, place, preferred_element_type=F32)
    first_rows = pltpu.roll(line, 0, 1, stride=DECIM, stride_axis=0)
    band = jnp.concatenate(
        [pltpu.roll(first_rows, 8 * DECIM * index, 1) for index in range(EXT // 8)], axis=0
    )
    row = lax.broadcasted_iota(jnp.int32, (EXT, 1024), 0)
    limit = jnp.where(member == MEMBERS - 1, COLS, USED)
    return jnp.where(row < limit, band, 0.0)[:, :960].astype(BF16)


def filtered(band, raw):
    count = raw.shape[0]
    sums = [
        jnp.dot(
            band[low:high, 256 * index : min(256 * (index + 1), count)],
            raw[256 * index : min(256 * (index + 1), count)],
            preferred_element_type=F32,
        )
        for index, (low, high) in enumerate(STRETCHES)
    ]
    pieces = []
    done = 0
    for index, (low, high) in enumerate(STRETCHES):
        end = STRETCHES[index + 1][0] if index + 1 < len(STRETCHES) else high
        pieces.append(sums[index][done - low : end - low])
        if end < high:
            after = STRETCHES[index + 1][0]
            pieces.append(sums[index][end - low :] + sums[index + 1][: high - after])
        done = high
    return jnp.concatenate(pieces, axis=0)


def coordinates(device):
    return device // 8 % 4, device // 2 % 4, device // 32, device % 2


def axis_of(turn, core):
    return (turn + 2 * core) % 3


def line_and_place(device, axis):
    z, x, y, c = coordinates(device)
    first, second = jnp.where(axis == 2, z, y), jnp.where(axis == 1, z, x)
    return first * 8 + second * 2 + c, jnp.where(axis == 0, z, jnp.where(axis == 1, x, y))


def device_of(line, place, axis):
    first, second, c = line // 8, line // 2 % 4, line % 2
    z = jnp.where(axis == 0, place, jnp.where(axis == 1, second, first))
    x, y = jnp.where(axis == 1, place, second), jnp.where(axis == 2, place, first)
    return y * 32 + z * 8 + x * 2 + c


def make_plan(me, src, dst, own, plan_ref):
    rows = src.shape[0]
    mine = own == me
    lane_a = lax.broadcasted_iota(jnp.int32, (128, 128), 0)
    lane = lax.broadcasted_iota(jnp.int32, (rows, 128), 1)
    row = lax.broadcasted_iota(jnp.int32, (rows, 128), 0)
    flags = jnp.where(mine, 1, 0)
    within = flags
    for shift in (1, 2, 4, 8, 16, 32, 64):
        within = within + jnp.where(lane >= shift, pltpu.roll(within, shift, 1), 0)
    totals = jnp.broadcast_to(jnp.sum(flags, axis=1, keepdims=True), (rows, 128))
    before = totals
    for shift in (1, 2, 4, 8, 16, 32):
        before = before + jnp.where(row >= shift, pltpu.roll(before, shift, 0), 0)
    slot = jnp.where(mine, within - flags + before - totals, -1)
    src_dev, dst_dev = src // 16, dst // 16

    first = jnp.zeros((SLOTS, 128), jnp.int32)
    second = jnp.zeros((SLOTS, 128), jnp.int32)
    for index in range(rows):
        hit = slot[index : index + 1, :] == lane_a[:SLOTS]
        first = first + jnp.where(hit, src_dev[index : index + 1, :], 0)
        second = second + jnp.where(hit, dst_dev[index : index + 1, :], 0)
    ends = jnp.sum(jnp.concatenate([first, second], axis=0).T, axis=0, keepdims=True)
    lines = []
    for turn in range(3):
        line, place = line_and_place(ends, axis_of(turn, ends % 2))
        lines.append(line * 4 + place)
    count = jnp.sum(flags, axis=(0, 1), keepdims=True)
    lines.append(jnp.broadcast_to(count, (1, 128)))
    plan_ref[12:16, :] = jnp.concatenate(lines, axis=0)

    z, x, y, _ = coordinates(me)

    def wanted(entry, _):
        axis, place = entry // 4, entry % 4
        source = jnp.where(
            axis == 0, me + (place - z) * 8, jnp.where(axis == 1, me + (place - x) * 2, me + (place - y) * 32)
        )
        local = jnp.where(src_dev == source, src % 16, 0) + jnp.where(dst_dev == source, dst % 16, 0)
        blocks = jnp.zeros((128, 128), jnp.int32)
        for index in range(rows):
            hit = own[index : index + 1, :] == lane_a
            blocks = blocks + jnp.where(hit, local[index : index + 1, :], 0)
        plan_ref[pl.ds(entry, 1), :] = jnp.sum(blocks.T, axis=0, keepdims=True)
        return 0

    lax.fori_loop(0, 12, wanted, 0)


def cross_spectra(into, plan, cross, slot, tile, axes):
    width = len(axes) * PIECE
    for index, axis in enumerate(axes):
        a = into[index, plan[12 + axis, slot]].astype(F32)
        b = into[index, plan[12 + axis, SLOTS + slot]].astype(F32)
        ar, ai, br, bi = a[:BLK], a[BLK:], b[:BLK], b[BLK:]
        left = index * PIECE
        for pair in range(BLK // 2):
            reals, imags = [], []
            for i in (2 * pair, 2 * pair + 1):
                xr, xi = ar[i : i + 1, :], ai[i : i + 1, :]
                reals.append(xr * br + xi * bi)
                imags.append(xi * br - xr * bi)
            at = tile * 64 + pair * 16
            cross[at : at + 16, left : left + PIECE] = jnp.concatenate(reals, axis=0).astype(BF16)
            cross[at : at + 16, width + left : width + left + PIECE] = jnp.concatenate(
                imags, axis=0
            ).astype(BF16)


def axes_of(part):
    return [piece % 3 for piece in range(CUTS[part], CUTS[part + 1])]


def exchange_kernel(
    strain_ref, taps_hbm, tiles_hbm, owner_hbm, basis_hbm, base_ref, lag0_ref, lag1_ref, lag2_ref,
    late_ref, partial_ref, plan_out_ref,
    raw, taps_ref, tiles_ref, owner_ref, basis, base, lag0, lag1, lag2, band, plan_vector, plan, send, recv, acc,
    gathered0, gathered1, gathered2, gathered3, gathered4, gathered5, gathered6, gathered7,
    out0, out1, out2, out3, in0, in1, in2, cross0, cross1, cross2, first_sums, partial,
    raw_sem, small_sem, base_sem, lag_sem, plan_sem, plan_out_sem, send_sem, recv_sem,
    line_sem, gather_sem, out_sem, in_sem, own_sem, partial_sem, plane_sem,
):
    grp, dev = lax.axis_index("grp"), lax.axis_index("dev")
    me = grp * MEMBERS + dev
    chip, core = dev // 2, dev % 2
    zc, xc = chip // 4, chip % 4

    def turned(offset):
        return jnp.where(core == 0, offset, (4 - offset) % 4)

    def at(z, x, c):
        return z % 4 * 8 + x % 4 * 2 + c

    def chip_at(offset):
        return (zc + turned(offset // 4)) % 4 * 4 + (xc + turned(offset % 4)) % 4

    def raw_copy(offset):
        to_chip = chip_at(offset)
        return pltpu.make_async_copy(
            strain_ref.at[:, pl.ds(pl.multiple_of(to_chip * 256, 256), 256)],
            raw.at[to_chip], raw_sem.at[to_chip],
        )

    def fetch(step, _):
        raw_copy(step * 7 % 16).start()
        return 0

    small = ((taps_hbm, taps_ref), (basis_hbm, basis), (tiles_hbm, tiles_ref))
    small = small + ((owner_hbm, owner_ref),)
    small_copies = [
        pltpu.make_async_copy(source, into, small_sem.at[index])
        for index, (source, into) in enumerate(small)
    ]
    for copy in small_copies:
        copy.start()
    lax.fori_loop(0, 16, fetch, 0)
    def base_copy(plane):
        return pltpu.make_async_copy(base_ref.at[plane], base.at[plane], base_sem.at[plane])

    lag_copies = [
        pltpu.make_async_copy(lag0_ref, lag0, lag_sem.at[0]),
        pltpu.make_async_copy(lag1_ref, lag1, lag_sem.at[1]),
        pltpu.make_async_copy(lag2_ref, lag2, lag_sem.at[2]),
    ]

    barrier = pltpu.get_barrier_semaphore()

    def greet(step, _):
        pl.semaphore_signal(
            barrier, inc=1, device_id=(grp, (dev + step) % MEMBERS), device_id_type=MESH
        )
        return 0

    lax.fori_loop(1, MEMBERS, greet, 0)
    for step in range(1, GROUPS):
        pl.semaphore_signal(
            barrier, inc=1, device_id=((grp + step) % GROUPS, dev), device_id_type=MESH
        )
    small_copies[0].wait()
    small_copies[1].wait()
    band[...] = make_band(dev, taps_ref[...])
    pl.semaphore_wait(barrier, MEMBERS - 1 + GROUPS - 1)

    def samples_to(to):
        return pltpu.make_async_remote_copy(
            src_ref=send.at[to], dst_ref=recv.at[dev], send_sem=send_sem.at[to],
            recv_sem=recv_sem.at[dev], device_id=(grp, to), device_id_type=MESH,
        )

    def decimate(pair, _):
        results = []
        for index in range(2):
            offset = (pair * 2 + index) * 7 % 16
            raw_copy(offset).wait()
            to_chip = chip_at(offset)
            result = filtered(band, raw.at[to_chip]).astype(BF16)
            halves = jnp.dot(basis[...], result, preferred_element_type=F32)
            results.append((to_chip, (halves[:RANK] + halves[RANK:]).astype(BF16)))
        @pl.when(pair % 2 == 1)
        def _():
            base_copy((zc + pair // 2) % 4).start()

        for to_chip, result in results:
            for half in range(2):
                send[to_chip * 2 + half] = result[:, half * CH : (half + 1) * CH]
                to = to_chip * 2 + half

                @pl.when(to != dev)
                def _():
                    samples_to(to).start()

        return 0

    lax.fori_loop(0, 8, decimate, 0)
    for copy in lag_copies:
        copy.start()
    recv[dev] = send[dev]
    for step in range(1, GROUPS):
        pl.semaphore_signal(
            plane_sem, inc=1, device_id=((grp + step) % GROUPS, dev), device_id_type=MESH
        )
    acc[...] = jnp.zeros_like(acc)

    def transform(step, _):
        plane = (zc + step) % 4
        first = plane * 8
        for index in range(8):
            source = first + index

            @pl.when(source != dev)
            def _():
                pltpu.make_async_remote_copy(
                    src_ref=send.at[source], dst_ref=recv.at[source],
                    send_sem=send_sem.at[source], recv_sem=recv_sem.at[source],
                    device_id=(grp, source), device_id_type=MESH,
                ).wait_recv()

        base_copy(plane).wait()
        samples = recv[pl.ds(first, 8)].reshape(8 * RANK, CH)
        acc[...] += lax.dot_general(
            samples, base[plane], (((0,), (0,)), ((), ())), preferred_element_type=F32
        )
        return 0

    lax.fori_loop(0, 4, transform, 0)

    real, imag = acc[:, :NF], acc[:, NF:]
    power = real * real + imag * imag
    level = jnp.mean(power, axis=1, keepdims=True)
    scale = lax.rsqrt(power + level + 1e-06)
    outs, ins = (out0, out1, out2, out3), (in0, in1, in2, late_ref)
    crosses, lags = (cross0, cross1, cross2), (lag0, lag1, lag2)
    gathered = (gathered0, gathered1, gathered2, gathered3)
    gathered = gathered + (gathered4, gathered5, gathered6, gathered7)
    pl.semaphore_wait(plane_sem, GROUPS - 1)
    for piece in range(PIECES):
        axis = axis_of(piece % 3, core)
        line, place = line_and_place(me, axis)
        bins = slice(piece * PIECE, (piece + 1) * PIECE)
        factor = scale[:, bins]
        parts = (acc[:, bins] * factor, acc[:, NF + piece * PIECE : NF + (piece + 1) * PIECE] * factor)
        gathered[piece][place] = jnp.concatenate(
            [half.reshape(16, BLK, PIECE) for half in parts], axis=1
        ).astype(BF16)
        for step in (1, 3, 2):
            to = device_of(line, (place + step) % 4, axis)
            pltpu.make_async_remote_copy(
                src_ref=gathered[piece].at[place], dst_ref=gathered[piece].at[place],
                send_sem=line_sem.at[piece], recv_sem=gather_sem.at[piece],
                device_id=(to // MEMBERS, to % MEMBERS), device_id_type=MESH,
            ).start()

    def select(piece, to, out):
        axis = axis_of(piece % 3, core)
        for place in range(4):
            out[place] = gathered[piece][place, plan[4 * axis + place, to]]

    def shifted(start, offset):
        return lax.rem(start + jnp.where(core == 0, offset, 4 - offset), 4)

    z_at, x_at = ([shifted(start, offset) for offset in range(4)] for start in (zc, xc))
    mate = 1 - core

    def emit(piece, part):
        axis, index = axis_of(piece % 3, core), piece - CUTS[part]
        line, _ = line_and_place(me, axis)
        second_at = [jnp.where(axis == 1, z, x) for z, x in zip(z_at, x_at)]

        def eight(turn, _):
            step = lax.rem(turn + 1, 4)
            first = shifted(jnp.where(axis == 2, zc, grp), step)
            to_grp = jnp.where(axis == 2, grp, first)
            for offset in (1, 3, 2, 0):
                second = second_at[offset]
                near = jnp.where(axis == 0, zc, jnp.where(axis == 1, second, first)) * 8
                near = near + jnp.where(axis == 1, xc, second) * 2
                for cross in range(2):
                    to_dev = near + (mate if cross else core)
                    slot = step * 8 + (offset * 2 + cross)

                    def send_one(to_dev=to_dev, slot=slot):
                        out = outs[part].at[index, slot]
                        select(piece, to_grp * MEMBERS + to_dev, out)
                        pltpu.make_async_remote_copy(
                            src_ref=out, dst_ref=ins[part].at[index, pl.ds(line * 4, 4)],
                            send_sem=out_sem.at[part], recv_sem=in_sem.at[part],
                            device_id=(to_grp, to_dev), device_id_type=MESH,
                        ).start()

                    if offset == 0 and cross == 0:
                        pl.when(step != 0)(send_one)
                    else:
                        send_one()
            return 0

        lax.fori_loop(0, 4, eight, 0)
        select(piece, me, outs[part].at[index, 0])
        return pltpu.make_async_copy(
            outs[part].at[index, 0], ins[part].at[index, pl.ds(line * 4, 4)], own_sem.at[piece]
        )

    for copy in small_copies[2:]:
        copy.wait()
    tile_rows = [stack_rows([tiles_ref[side : side + 1, :]], 40, 0) for side in range(2)]
    owner_rows = stack_rows([owner_ref[...].reshape(1, -1)], 40, -1)
    make_plan(me, *tile_rows, owner_rows, plan_vector)
    plan_copy = pltpu.make_async_copy(plan_vector, plan, plan_sem)
    plan_copy.start()
    plan_out = pltpu.make_async_copy(plan_vector, plan_out_ref, plan_out_sem)
    plan_out.start()
    plan_copy.wait()
    own_copies = []
    for part in range(EARLY + 1):
        for piece in range(CUTS[part], CUTS[part + 1]):
            others = gathered[piece].at[pl.ds(0, 3)]
            pltpu.make_async_copy(others, others, gather_sem.at[piece]).wait()
            own_copies.append(emit(piece, part))
            own_copies[piece].start()

    def drain(step, _):
        samples_to((dev + step) % MEMBERS).wait_send()
        return 0

    lax.fori_loop(1, MEMBERS, drain, 0)
    def await_part(part):
        for piece in range(CUTS[part], CUTS[part + 1]):
            own_copies[piece].wait()
        others = ins[part].at[:, pl.ds(0, DEVICES - 4)]
        pltpu.make_async_copy(others, others, in_sem.at[part]).wait()

    def tiles_of(part):
        def one(group, _):
            for tile in range(TILES):
                cross_spectra(ins[part], plan, crosses[part], group * TILES + tile, tile, axes_of(part))
            lagged = jnp.dot(crosses[part][...], lags[part][...], preferred_element_type=F32)
            lagged = lagged.reshape(TILES, BLK, BLK, NLAG)
            rows = pl.ds(group * TILES, TILES)
            if part > 0:
                lagged = lagged + first_sums[rows]
            if part < EARLY - 1:
                first_sums[rows] = lagged
            else:
                partial[rows] = lagged.astype(BF16)
                pltpu.make_async_copy(partial.at[rows], partial_ref.at[rows], partial_sem).start()
            return 0

        lax.fori_loop(0, SLOTS // TILES, one, 0)

    for copy in lag_copies:
        copy.wait()
    for part in range(EARLY):
        await_part(part)
        tiles_of(part)
    pltpu.make_async_copy(partial, partial_ref, partial_sem).wait()
    plan_out.wait()
    for part in range(EARLY + 1):
        sent = outs[part].at[:, pl.ds(0, MEMBERS - 1)]
        pltpu.make_async_copy(sent, sent, out_sem.at[part]).wait()
    await_part(EARLY)
    for piece in range(PIECES):
        others = gathered[piece].at[pl.ds(0, 3)]
        pltpu.make_async_copy(others, others, line_sem.at[piece]).wait()


def late_kernel(
    plan_ref, late_ref, partial_ref, lag_ref, out_ref,
    late, lag, partial, total, cross, late_sem, lag_sem, in_sem, out_sem,
):
    count = plan_ref[15, 0]
    pieces = 4
    size = DEVICES // pieces
    late_copies = [
        pltpu.make_async_copy(
            late_ref.at[:, pl.ds(size * index, size)], late.at[:, pl.ds(size * index, size)],
            late_sem.at[index],
        )
        for index in range(pieces)
    ]
    lag_copy = pltpu.make_async_copy(lag_ref, lag, lag_sem)

    def rows(group):
        return pl.ds(group * LATE_TILES, LATE_TILES)

    def load(group):
        return pltpu.make_async_copy(
            partial_ref.at[rows(group)], partial.at[rows(group)], in_sem.at[group]
        )

    for copy in late_copies:
        copy.start()
    lag_copy.start()

    def fetch(group, _):
        load(group).start()
        return 0

    lax.fori_loop(0, SLOTS // LATE_TILES, fetch, 0)
    for copy in late_copies:
        copy.wait()
    lag_copy.wait()

    def one(group, _):
        load(group).wait()

        @pl.when(group * LATE_TILES < count)
        def _():
            for tile in range(LATE_TILES):
                cross_spectra(late, plan_ref, cross, group * LATE_TILES + tile, tile, axes_of(EARLY))
            lagged = jnp.dot(cross[...], lag[...], preferred_element_type=F32)
            lagged = lagged + partial[rows(group)].astype(F32).reshape(lagged.shape)
            index = lax.broadcasted_iota(jnp.int32, lagged.shape, 0) // 64 + group * LATE_TILES
            total[rows(group)] = jnp.where(index < count, lagged, 0.0).reshape(LATE_TILES, BLK, BLK, NLAG)

        @pl.when(group * LATE_TILES >= count)
        def _():
            total[rows(group)] = jnp.zeros((LATE_TILES, BLK, BLK, NLAG), F32)

        pltpu.make_async_copy(total.at[rows(group)], out_ref.at[rows(group)], out_sem).start()
        return 0

    lax.fori_loop(0, SLOTS // LATE_TILES, one, 0)
    pltpu.make_async_copy(total, out_ref, out_sem).wait()


def per_device(strain, taps, tiles, owner):
    hbm = pl.BlockSpec(memory_space=pl.ANY)
    lag = lag_table()
    basis, rows = base_tables()
    lags = [
        lag.reshape(2, PIECES, PIECE, NLAG)[:, CUTS[part] : CUTS[part + 1]].reshape(-1, NLAG)
        for part in range(EARLY + 1)
    ]
    late, partial, plan = pl.pallas_call(
        exchange_kernel,
        out_shape=(
            jax.ShapeDtypeStruct((COUNTS[EARLY], DEVICES, 2 * BLK, PIECE), BF16),
            jax.ShapeDtypeStruct((SLOTS, BLK, BLK, NLAG), BF16),
            jax.ShapeDtypeStruct((16, 128), jnp.int32),
        ),
        in_specs=[hbm] * (6 + EARLY),
        out_specs=(hbm, hbm, hbm),
        scratch_shapes=[
            pltpu.VMEM((16, 960, 256), BF16),
            pltpu.VMEM((1, NTAP), BF16),
            pltpu.VMEM((2, 4160), jnp.int32),
            pltpu.VMEM((4160,), jnp.int32),
            pltpu.VMEM((2 * RANK, EXT), BF16),
            pltpu.VMEM((4, 8 * RANK, 2 * NF), BF16),
            *[pltpu.VMEM((2 * count * PIECE, NLAG), BF16) for count in COUNTS[:EARLY]],
            pltpu.VMEM((EXT, 960), BF16),
            pltpu.VMEM((16, 128), jnp.int32),
            pltpu.SMEM((16, 128), jnp.int32),
            pltpu.VMEM((MEMBERS, RANK, CH), BF16),
            pltpu.VMEM((MEMBERS, RANK, CH), BF16),
            pltpu.VMEM((CH, 2 * NF), F32),
            *[pltpu.VMEM((4, 16, 2 * BLK, PIECE), BF16) for _ in range(PIECES)],
            *[pltpu.VMEM((count, MEMBERS, 4, 2 * BLK, PIECE), BF16) for count in COUNTS],
            *[pltpu.VMEM((count, DEVICES, 2 * BLK, PIECE), BF16) for count in COUNTS[:EARLY]],
            *[pltpu.VMEM((TILES * 64, 2 * count * PIECE), BF16) for count in COUNTS[:EARLY]],
            pltpu.VMEM((SLOTS, BLK, BLK, NLAG), F32),
            pltpu.VMEM((SLOTS, BLK, BLK, NLAG), BF16),
            pltpu.SemaphoreType.DMA((16,)),
            pltpu.SemaphoreType.DMA((4,)),
            pltpu.SemaphoreType.DMA((4,)),
            pltpu.SemaphoreType.DMA((EARLY,)),
            pltpu.SemaphoreType.DMA,
            pltpu.SemaphoreType.DMA,
            pltpu.SemaphoreType.DMA((MEMBERS,)),
            pltpu.SemaphoreType.DMA((MEMBERS,)),
            pltpu.SemaphoreType.DMA((PIECES,)),
            pltpu.SemaphoreType.DMA((PIECES,)),
            pltpu.SemaphoreType.DMA((EARLY + 1,)),
            pltpu.SemaphoreType.DMA((EARLY + 1,)),
            pltpu.SemaphoreType.DMA((PIECES,)),
            pltpu.SemaphoreType.DMA,
            pltpu.SemaphoreType.REGULAR,
        ],
        compiler_params=pltpu.CompilerParams(
            collective_id=0, has_side_effects=True, vmem_limit_bytes=60 * 2**20
        ),
    )(
        strain.T, taps[None, :], tiles.T, owner, jnp.asarray(basis), jnp.asarray(rows.reshape(4, 8 * RANK, 2 * NF)),
        *[jnp.asarray(part) for part in lags[:EARLY]],
    )

    return pl.pallas_call(
        late_kernel,
        out_shape=jax.ShapeDtypeStruct((SLOTS, BLK, BLK, NLAG), F32),
        in_specs=[pl.BlockSpec(memory_space=pltpu.SMEM), hbm, hbm, hbm],
        out_specs=hbm,
        scratch_shapes=[
            pltpu.VMEM((COUNTS[EARLY], DEVICES, 2 * BLK, PIECE), BF16),
            pltpu.VMEM((2 * COUNTS[EARLY] * PIECE, NLAG), BF16),
            pltpu.VMEM((SLOTS, BLK, BLK, NLAG), BF16),
            pltpu.VMEM((SLOTS, BLK, BLK, NLAG), F32),
            pltpu.VMEM((LATE_TILES * 64, 2 * COUNTS[EARLY] * PIECE), BF16),
            pltpu.SemaphoreType.DMA((4,)),
            pltpu.SemaphoreType.DMA,
            pltpu.SemaphoreType.DMA((SLOTS // LATE_TILES,)),
            pltpu.SemaphoreType.DMA,
        ],
        compiler_params=pltpu.CompilerParams(vmem_limit_bytes=60 * 2**20),
    )(plan, late, partial, jnp.asarray(lags[EARLY]))


def solution(mesh):
    return jax.shard_map(
        per_device,
        mesh=mesh,
        in_specs=(P("grp", "dev"), P(), P(), P()),
        out_specs=P(("grp", "dev"), None, None, None),
        check_vma=False,
    )
```
